32 devices in a mesh: groups: 2 (over x), gx: 16 (over z, y, core).
Axes of the slice: x: 2, y: 2, z: 4, core: 2. Of those that a mesh axis runs over, the one named last changes fastest.
Arguments:
- permeability: float32 [512, 1024], P(('groups', 'gx')), parts along dimension 0, may hold values from 0.05 to 20
- storage: float32 [512, 1024], P(('groups', 'gx')), parts along dimension 0, may hold values from 0.02 to 0.5
- support_mask: int32 [32, 2, 2, 32, 32], P(('groups', 'gx')), parts along dimension 0, may hold values from 0 to 262143
- prev_basis: float32 [32, 2, 2, 32, 1024], P(('groups', 'gx')), parts along dimension 0, may hold values from 0 to 1
Outputs:
- basis: float32 [32, 2, 2, 32, 1024], P(('groups', 'gx')), parts along dimension 0
- coarse_matrix: float32 [32, 2, 2, 27], P(('groups', 'gx')), parts along dimension 0
The draws below stay inside these ranges and needn't reach their ends.
There are 2 independent parts, one for each index of `groups`. The reference program is written for one: setup_inputs(seed, part) draws one part's arguments, and reference() takes and returns one part's arrays. A program takes and returns all parts, laid end to end along the dimension named above; each array names one. Nothing has to cross between parts.
All inputs are finite; a program needn't handle non-finite values.
Results may differ from the reference program's by a relative error of at most 0.0003.
Values sent between devices are 32-bit elements; how exact they have to be, the bound alone decides.
No kernel may reach another device: no remote copies, remote signals or barrier semaphores. Data moves between devices by JAX's collectives and lax.ppermute only.
A program may use at most 128 MiB of HBM per device.

```python
import math
import jax
import jax.numpy as jnp
from jax import lax

BY = 2
BZ = 2
ITERS = 2
NBX = 16
NX = 256
NY = 32
NZ = 32


def set_ends(array, rng, low, top_value):
    dims = array.shape
    spot = [jax.random.randint(jax.random.fold_in(rng, axis), (), 0, dims[axis]) for axis in range(len(dims))]
    array = array.at[tuple(spot)].set(low)
    longest = dims.index(max(dims))
    spot[longest] = (spot[longest] + 1) % dims[longest]
    return array.at[tuple(spot)].set(top_value)


def block_levels(key, dims, cuts, low, largest):
    gain = 1.0
    for dim, parts in cuts:
        steps = jax.random.uniform(jax.random.fold_in(jax.random.fold_in(key, 6), dim), (parts,), jnp.float32, low / len(cuts), largest / len(cuts))
        gain = gain * jnp.repeat(jnp.exp(steps), dims[dim] // parts).reshape((-1,) + (1,) * (len(dims) - 1 - dim))
    return gain


def setup_inputs(seed: int = 0, part: int = 0) -> dict:
    key_of = jax.random.split(jax.random.key(seed), 5)
    part_splits = jax.random.split(jax.random.fold_in(key_of[4], part), 5)
    return {
        "permeability": jnp.clip(jnp.exp(math.log(20.0) - 5.9914645 * jax.random.uniform(part_splits[0], (NX, NY * NZ), jnp.float32) ** block_levels(part_splits[0], (NX, NY * NZ), ((0, 16),), -0.2, 0.2)), 0.05, 20.0),
        "storage": jnp.clip(jnp.exp(math.log(0.5) - 3.218876 * jax.random.uniform(part_splits[1], (NX, NY * NZ), jnp.float32) ** block_levels(part_splits[1], (NX, NY * NZ), ((0, 16),), -0.2, 0.2)), 0.02, 0.5),
        "support_mask": set_ends(jax.random.randint(part_splits[2], (NBX, BY, BZ, 32, 32), 0, 262144), jax.random.fold_in(part_splits[2], 1), 0, 262143).astype(jnp.int32),
        "prev_basis": jnp.clip(1.0 * jax.random.uniform(part_splits[3], (NBX, BY, BZ, 32, 32 * NZ), jnp.float32) ** block_levels(part_splits[3], (NBX, BY, BZ, 32, 32 * NZ), ((0, 16),), -0.2, 0.2), 0.0, 1.0),
    }


relaxation = 2.0 / 3.0
sum_floor = 0.5


def harmonic(first_perm, second_perm):
    summed = first_perm + second_perm
    guarded = jnp.where(summed > 0.0, summed, 1.0)
    return jnp.where(summed > 0.0, 2.0 * first_perm * second_perm / guarded, 0.0)


def face_fields(perm_field):
    east_face = jnp.concatenate([harmonic(perm_field[:-1], perm_field[1:]), jnp.zeros_like(perm_field[:1])], axis=0)
    north_face = jnp.concatenate([harmonic(perm_field[:, :-1], perm_field[:, 1:]), jnp.zeros_like(perm_field[:, :1])], axis=1)
    upper_face = jnp.concatenate([harmonic(perm_field[:, :, :-1], perm_field[:, :, 1:]), jnp.zeros_like(perm_field[:, :, :1])], axis=2)
    return east_face, north_face, upper_face


def windows(values, position, blocks):
    extent = values.shape
    blocked = values.reshape(extent[:position] + (blocks + 2, 16) + extent[position + 1:])
    pieces = [lax.slice_in_dim(blocked, block_shift, block_shift + blocks, axis=position) for block_shift in range(3)]
    joined = jnp.concatenate(pieces, axis=position + 1)
    return lax.slice_in_dim(joined, 0, 36, axis=position + 1)


def to_boxes(values, blocks_x, blocks_y):
    framed = windows(values, 0, blocks_x)
    framed = windows(framed, 2, blocks_y)
    return framed.transpose(0, 2, 1, 3, 4)


def add_axis(boxes, position, blocks):
    margins = [(0, 0)] * boxes.ndim
    margins[position + 1] = (2, 14)
    padded = jnp.pad(boxes, margins)
    extent = padded.shape
    blocked = padded.reshape(extent[:position + 1] + (3, 16) + extent[position + 2:])
    summed = None
    for block_shift in range(3):
        portion = lax.index_in_dim(blocked, block_shift, axis=position + 1, keepdims=False)
        spread = [(0, 0)] * portion.ndim
        spread[position] = (block_shift, 2 - block_shift)
        placed = jnp.pad(portion, spread)
        summed = placed if summed is None else summed + placed
    return summed.reshape(extent[:position] + (16 * (blocks + 2),) + extent[position + 2:])


def to_fine(boxes, blocks_x, blocks_y):
    merged = jnp.sum(boxes, axis=2).transpose(0, 2, 1, 3, 4)
    along_x = add_axis(merged, 0, blocks_x)
    return add_axis(along_x, 1, blocks_y)


def coefficient_boxes(perm_field, storage_field, blocks_x, blocks_y):
    east_face, north_face, upper_face = face_fields(perm_field)
    return tuple(to_boxes(values, blocks_x, blocks_y)[:, :, None] for values in (east_face, north_face, upper_face, storage_field))


def apply_operator(values, coefficients, low, high):
    east_face, north_face, upper_face, storage_box = coefficients
    center = slice(low, high)
    plus_side = slice(low + 1, high + 1)
    minus_side = slice(low - 1, high - 1)
    central = values[..., center, center, :]
    east_here = east_face[..., center, center, :]
    west_here = east_face[..., minus_side, center, :]
    north_here = north_face[..., center, center, :]
    south_here = north_face[..., center, minus_side, :]
    upper_here = upper_face[..., center, center, :]
    lower_here = jnp.concatenate([jnp.zeros_like(upper_here[..., :1]), upper_here[..., :-1]], axis=-1)
    upper_value = jnp.concatenate([central[..., 1:], jnp.zeros_like(central[..., :1])], axis=-1)
    lower_value = jnp.concatenate([jnp.zeros_like(central[..., :1]), central[..., :-1]], axis=-1)
    storage_here = storage_box[..., center, center, :]
    applied = storage_here * central
    applied = applied + east_here * (central - values[..., plus_side, center, :])
    applied = applied + west_here * (central - values[..., minus_side, center, :])
    applied = applied + north_here * (central - values[..., center, plus_side, :])
    applied = applied + south_here * (central - values[..., center, minus_side, :])
    applied = applied + upper_here * (central - upper_value) + lower_here * (central - lower_value)
    diagonal = storage_here + east_here + west_here + north_here + south_here + upper_here + lower_here
    return applied, diagonal


def decode_support(support_mask, first_block, total_x, total_y):
    blocks_x, blocks_y, layers = support_mask.shape[0], support_mask.shape[1], support_mask.shape[2]
    vertical = 16 * layers
    heights = jnp.arange(vertical, dtype=jnp.int32)[None, :]
    layer_ids = jnp.arange(layers, dtype=jnp.int32)[:, None]
    relative = heights - 8 * layer_ids
    within = (relative >= 0) & (relative < 18)
    shifted = jnp.right_shift(support_mask[..., None], jnp.clip(relative, 0, 17)[None, None, :, None, None, :])
    marked = (jnp.bitwise_and(shifted, 1) == 1) & within[None, None, :, None, None, :]
    offsets = jnp.arange(32, dtype=jnp.int32)
    core_line = (offsets >= 8) & (offsets < 24)
    core_layer = (heights >= 16 * layer_ids) & (heights < 16 * layer_ids + 16)
    core_full = core_line[:, None, None] & core_line[None, :, None]
    core_full = core_full[None, None, None] & core_layer[None, None, :, None, None, :]
    global_x = 16 * (first_block + jnp.arange(blocks_x, dtype=jnp.int32))[:, None] - 8 + offsets[None, :]
    global_y = 16 * jnp.arange(blocks_y, dtype=jnp.int32)[:, None] - 8 + offsets[None, :]
    inside_x = (global_x >= 0) & (global_x < total_x)
    inside_y = (global_y >= 0) & (global_y < total_y)
    inside = inside_x[:, None, None, :, None, None] & inside_y[None, :, None, None, :, None]
    return ((marked | core_full) & inside).astype(jnp.float32)


def relax_step(basis, support, coefficients):
    padded = jnp.pad(basis, ((0, 0), (0, 0), (0, 0), (2, 2), (2, 2), (0, 0)))
    applied, diagonal = apply_operator(padded, coefficients, 2, 34)
    return support * jnp.maximum(basis - relaxation * applied / diagonal, 0.0)


def normalize(kept, totals, blocks_x, blocks_y):
    totals_box = to_boxes(totals, blocks_x, blocks_y)[:, :, None, 2:34, 2:34, :]
    return kept / jnp.maximum(totals_box, sum_floor)


def galerkin_entries(basis, applied, left_column, right_column):
    blocks_x, blocks_y, layers = basis.shape[0], basis.shape[1], basis.shape[2]
    neighbours = jnp.concatenate([left_column[None], applied, right_column[None]], axis=0)
    neighbours = jnp.pad(neighbours, ((0, 0), (1, 1), (1, 1), (0, 0), (0, 0), (0, 0)))
    window_pairs = {-1: (slice(0, 17), slice(17, 34)), 0: (slice(0, 32), slice(1, 33)), 1: (slice(15, 32), slice(0, 17))}
    entries = []
    for offset_x in (-1, 0, 1):
        near_x, far_x = window_pairs[offset_x]
        for offset_y in (-1, 0, 1):
            near_y, far_y = window_pairs[offset_y]
            for offset_z in (-1, 0, 1):
                near_part = basis[:, :, :, near_x, near_y, :]
                far_part = neighbours[1 + offset_x:1 + offset_x + blocks_x, 1 + offset_y:1 + offset_y + blocks_y, 1 + offset_z:1 + offset_z + layers, far_x, far_y, :]
                entries.append(jnp.sum(near_part * far_part, axis=(3, 4, 5)))
    return jnp.stack(entries, axis=-1)


def reference(permeability, storage, support_mask, prev_basis):
    perm_field = jnp.pad(permeability.reshape(NX, NY, NZ), ((10, 22), (10, 22), (0, 0)))
    storage_field = jnp.pad(storage.reshape(NX, NY, NZ), ((10, 22), (10, 22), (0, 0)))
    coefficients = coefficient_boxes(perm_field, storage_field, NBX, BY)
    support = decode_support(support_mask, 0, NX, NY)
    basis = support * prev_basis.reshape(support.shape)
    for sweep in range(ITERS):
        kept = relax_step(basis, support, coefficients)
        totals = to_fine(kept, NBX, BY)
        basis = normalize(kept, totals, NBX, BY)
    padded = jnp.pad(basis, ((0, 0), (0, 0), (0, 0), (2, 2), (2, 2), (0, 0)))
    applied, unused = apply_operator(padded, coefficients, 1, 35)
    empty_column = jnp.zeros_like(applied[0])
    coarse = galerkin_entries(basis, applied, empty_column, empty_column)
    return basis.reshape(prev_basis.shape), coarse
```

```python
import functools

import jax
import jax.numpy as jnp
from jax import lax
from jax.experimental import pallas as pl
from jax.experimental.pallas import tpu as pltpu
from jax.sharding import PartitionSpec as P

ITERS = 2
SUM_FLOOR = 0.5
TINY = 1e-30
F32 = jnp.float32


BLOCKS = 4
LANE_TILES = 8
USED = 6

PERM_AT = 2 * BLOCKS * USED
STOR_AT = PERM_AT + LANE_TILES
MASK_AT = STOR_AT + LANE_TILES
REST_AT = MASK_AT + 2
REST = BLOCKS * USED + 2 * LANE_TILES + 1
REST_SLOTS = (REST + 1) // 2
MESSAGE = REST_AT + REST_SLOTS
THIN = BLOCKS * USED + 1
THIN_SLOTS = (THIN + 1) // 2


def box_tile(by, u):
    return u + 2 * (1 - by)


def lanes_of(tile):
    return pl.ds(128 * tile, 128)


def half_rows(upper):
    rows = lax.broadcasted_iota(jnp.int32, (8, 128), 0)
    return rows // 4 == upper


def joined_mask(mask_ref):
    parts = [mask_ref[0, by, bz] for by in range(2) for bz in range(2)]
    return jnp.concatenate(parts, axis=1)


def pack_kernel(perm_ref, stor_ref, mask_ref, prev_ref, near_ref, far_ref, far2_ref, near2_ref, mask_buf):
    odd = lax.rem(lax.axis_index("gx"), 2)
    mask_buf[...] = joined_mask(mask_ref).astype(F32)

    def rows_of(ref, tile, *rest):
        return ref[(*rest[:-1], pl.ds(pl.multiple_of(8 * tile, 8), 8), rest[-1])]

    def put_pairs(out_ref, at, slots, pieces, upper):
        keep = half_rows(upper)
        for s in range(slots):
            tile = pieces[s]()
            if s + slots < len(pieces):
                tile = jnp.where(keep, tile, pltpu.roll(pieces[s + slots](), 4, 0))
            out_ref[at + s] = tile

    def message(out_ref, leftward):
        first = 2 - 2 * leftward
        for xt in range(2):
            for blk in range(BLOCKS):
                by, bz = divmod(blk, 2)
                for u in range(USED):
                    out_ref[(xt * BLOCKS + blk) * USED + u] = rows_of(
                        prev_ref, first + xt, 0, by, bz, lanes_of(box_tile(by, u))
                    )
            out_ref[MASK_AT + xt] = rows_of(mask_buf, first + xt, lanes_of(0))
        for t in range(LANE_TILES):
            out_ref[PERM_AT + t] = rows_of(perm_ref, 1 - leftward, lanes_of(t))
            out_ref[STOR_AT + t] = rows_of(stor_ref, 1 - leftward, lanes_of(t))
        rest = 1 + leftward
        pieces = [
            functools.partial(rows_of, prev_ref, rest, 0, blk // 2, blk % 2, lanes_of(box_tile(blk // 2, u)))
            for blk in range(BLOCKS)
            for u in range(USED)
        ]
        pieces += [functools.partial(rows_of, perm_ref, leftward, lanes_of(t)) for t in range(LANE_TILES)]
        pieces += [functools.partial(rows_of, stor_ref, leftward, lanes_of(t)) for t in range(LANE_TILES)]
        pieces += [functools.partial(rows_of, mask_buf, rest, lanes_of(0))]
        put_pairs(out_ref, REST_AT, REST_SLOTS, pieces, 1 - leftward)

    def thin(out_ref, leftward):
        edge = 3 - 3 * leftward
        pieces = [
            functools.partial(rows_of, prev_ref, edge, 0, blk // 2, blk % 2, lanes_of(box_tile(blk // 2, u)))
            for blk in range(BLOCKS)
            for u in range(USED)
        ]
        pieces += [functools.partial(rows_of, mask_buf, edge, lanes_of(0))]
        put_pairs(out_ref, 0, THIN_SLOTS, pieces, 1 - leftward)

    message(far_ref, 1 - odd)
    message(near_ref, odd)
    thin(far2_ref, odd)
    thin(near2_ref, 1 - odd)


def main_kernel(
    perm_ref, stor_ref, mask_ref, prev_ref, near_ref, far_ref, far2_ref, near2_ref,
    basis_ref, coarse_ref,
    kbuf, cbuf, wbuf, gbuf, mown, mring, mtwo, sup, pbuf, qbuf, own_mask, sums,
):
    here = lax.axis_index("gx")
    last = lax.axis_size("gx") - 1
    odd = lax.rem(here, 2) == 1
    rows = lax.broadcasted_iota(jnp.int32, (8, 128), 0)
    lanes = lax.broadcasted_iota(jnp.int32, (8, 128), 1)
    heights = lax.rem(lanes, 32)
    low_rows = rows < 4
    zero = jnp.zeros((8, 128), F32)

    def left_big(i):
        return jnp.where(odd, near_ref[i], far_ref[i])

    def right_big(i):
        return jnp.where(odd, far_ref[i], near_ref[i])

    def left_thin(i):
        return jnp.where(odd, near2_ref[i], far2_ref[i])

    def right_thin(i):
        return jnp.where(odd, far2_ref[i], near2_ref[i])

    def paired(left, right, at, slots, index):
        slot = index % slots
        tile = jnp.where(low_rows, right(at + slot), left(at + slot))
        if index >= slots:
            other = jnp.where(low_rows, left(at + slot), right(at + slot))
            tile = pltpu.roll(other, 4, 0)
        return tile

    def rest_tile(index):
        return paired(left_big, right_big, REST_AT, REST_SLOTS, index)

    def thin_tile(index):
        return paired(left_thin, right_thin, 0, THIN_SLOTS, index)

    for t in range(LANE_TILES):
        for buf, ref, bulk, rest in (
            (kbuf, perm_ref, PERM_AT, BLOCKS * USED),
            (cbuf, stor_ref, STOR_AT, BLOCKS * USED + LANE_TILES),
        ):
            buf[t, 0:8] = left_big(bulk + t)
            buf[t, 8:16] = ref[0:8, 128 * t : 128 * t + 128]
            buf[t, 16:24] = ref[8:16, 128 * t : 128 * t + 128]
            buf[t, 24:32] = right_big(bulk + t)
            buf[t, 32:40] = rest_tile(rest + t)
    kbuf[LANE_TILES] = jnp.zeros((40, 128), F32)

    own_mask[...] = joined_mask(mask_ref)
    block = lanes // 32
    inner = (heights >= 8) & (heights < 24)
    core_bits = jnp.where(inner, jnp.where(lax.rem(block, 2) == 0, 0xFFFF, 0xFFFF00), 0)
    for k in range(4):
        tile = own_mask[8 * k : 8 * k + 8]
        if k in (1, 2):
            tile = tile | core_bits
        if k == 0:
            tile = jnp.where(here == 0, 0, tile)
        if k == 3:
            tile = jnp.where(here == last, 0, tile)
        mown[k] = tile
    mring[0] = left_big(MASK_AT).astype(jnp.int32) | core_bits
    mring[1] = left_big(MASK_AT + 1).astype(jnp.int32)
    mring[2] = right_big(MASK_AT).astype(jnp.int32)
    mring[3] = right_big(MASK_AT + 1).astype(jnp.int32) | core_bits
    mring[4] = rest_tile(REST - 1).astype(jnp.int32) | core_bits
    mtwo[...] = thin_tile(THIN - 1).astype(jnp.int32)

    lane_bits = []
    for bz in range(2):
        offset = heights - 8 * bz
        valid = (offset >= 0) & (offset < (18, 24)[bz])
        lane_bits.append(jnp.where(valid, jnp.left_shift(1, jnp.clip(offset, 0, 23)), 0))

    def support_of(tile, by, bz, u):
        index = 32 * (2 * by + bz) + 4 * u + 8 * (1 - by) + lanes // 32
        spread = jnp.take_along_axis(tile, index, axis=1, mode="promise_in_bounds")
        return jnp.where((spread & lane_bits[bz]) != 0, 1.0, 0.0)

    blank = jnp.zeros((40, 128), F32)
    for e in range(2):
        for by in range(2):
            for bz in range(2):
                for slot in range(LANE_TILES + 2):
                    if not 1 + 2 * by <= slot <= USED + 2 * by:
                        pbuf[e, by, bz, slot] = blank
                        qbuf[e, by, bz, slot] = blank
                for u in range(USED):
                    t = u + 2 * by
                    blk = 2 * by + bz
                    cell = blk * USED + u

                    def put(e, k, tile, bits):
                        s = support_of(bits, by, bz, u)
                        sup[e, by, bz, u, 8 * k : 8 * k + 8] = s
                        pbuf[e, by, bz, t + 1, 8 * k : 8 * k + 8] = s * tile

                    if e == 0:
                        for k in range(4):
                            at = 128 * box_tile(by, u)
                            put(0, k, prev_ref[0, by, bz, 8 * k : 8 * k + 8, at : at + 128], mown[k])
                        put(0, 4, thin_tile(cell), mtwo[...])
                    else:
                        put(1, 0, left_big(cell), mring[0])
                        put(1, 1, left_big(BLOCKS * USED + cell), mring[1])
                        put(1, 2, right_big(cell), mring[2])
                        put(1, 3, right_big(BLOCKS * USED + cell), mring[3])
                        put(1, 4, rest_tile(cell), mring[4])

    def up_x(tiles, ends):
        turned = [pltpu.roll(v, 7, 0) for v in tiles]
        return [jnp.where(rows < 7, turned[i], ends[i] if not isinstance(ends[i], int) else turned[ends[i]]) for i in range(len(tiles))]

    def down_x(tiles, ends):
        turned = [pltpu.roll(v, 1, 0) for v in tiles]
        return [jnp.where(rows > 0, turned[i], ends[i] if not isinstance(ends[i], int) else turned[ends[i]]) for i in range(len(tiles))]

    def up_y(here_, next_):
        return pltpu.roll(jnp.where(lanes >= 32, here_, next_), 96, 1)

    def down_y(here_, before):
        return pltpu.roll(jnp.where(lanes < 96, here_, before), 32, 1)

    def up_z(v):
        return pltpu.roll(v, 127, 1)

    def down_z(v):
        return pltpu.roll(v, 1, 1)

    def harmonic(a, b):
        return 2.0 * a * b / jnp.maximum(a + b, TINY)

    def faces(t, carry):
        k = [kbuf[t, 8 * i : 8 * i + 8] for i in range(5)]
        kn = [kbuf[t + 1, 8 * i : 8 * i + 8] for i in range(5)]
        east = [harmonic(a, b) for a, b in zip(k, up_x(k, [1, 2, 3, 4, 0]))]
        west = down_x(east, [4, 0, 1, 2, 3])
        for i in range(5):
            north = harmonic(k[i], up_y(k[i], kn[i]))
            upper = jnp.where(heights < 31, harmonic(k[i], up_z(k[i])), 0.0)
            lower = down_z(upper)
            south = down_y(north, carry[i])
            diag = cbuf[t, 8 * i : 8 * i + 8] + east[i] + west[i] + north + south + upper + lower
            scale = (2.0 / 3.0) / jnp.maximum(diag, TINY)
            for d, face in enumerate((east[i], west[i], north, south, upper, lower)):
                wbuf[d, t, 8 * i : 8 * i + 8] = face * scale
            gbuf[t, 8 * i : 8 * i + 8] = 1.5 * diag
            carry = carry[:i] + (north,) + carry[i + 1 :]
        return carry

    lax.fori_loop(0, LANE_TILES, faces, (zero,) * 5)

    def stencil(e, by, bz, t, tiles, ups, downs, which, weights):
        out = []
        for n, i in enumerate(which):
            v = tiles[n]
            above = pbuf[e, by, bz, t + 2, 8 * i : 8 * i + 8]
            below = pbuf[e, by, bz, t, 8 * i : 8 * i + 8]
            w = weights[i]
            total = w[0] * ups[n] + w[1] * downs[n]
            total += w[2] * up_y(v, above) + w[3] * down_y(v, below)
            total += w[4] * up_z(v) + w[5] * down_z(v)
            out.append(total)
        return out

    def load_weights(t):
        return [[wbuf[d, t, 8 * i : 8 * i + 8] for d in range(6)] for i in range(5)]

    def groups(e):
        if e == 0:
            return (((0, 1, 2, 3), [1, 2, 3, zero], [zero, 0, 1, 2]), ((4,), [zero], [zero]))
        return (((0, 1, 2, 3, 4), [1, zero, 3, 4, 0], [4, 0, zero, 2, 3]),)

    def relax(step, carry):
        by = step // USED
        u = step - by * USED
        t = u + 2 * by
        weights = load_weights(t)
        for bz in range(2):
            for e in range(2):
                for which, ups, downs in groups(e):
                    tiles = [pbuf[e, by, bz, t + 1, 8 * i : 8 * i + 8] for i in which]
                    near = stencil(e, by, bz, t, tiles, up_x(tiles, ups), down_x(tiles, downs), which, weights)
                    for n, i in enumerate(which):
                        s = sup[e, by, bz, u, 8 * i : 8 * i + 8]
                        kept = s * jnp.maximum(tiles[n] * (1.0 / 3.0) + near[n], 0.0)
                        qbuf[e, by, bz, t + 1, 8 * i : 8 * i + 8] = kept
        return carry

    def normalise(t, carry):
        for i in range(5):
            at = pl.ds(8 * i, 8)
            kept = [qbuf[e, by, bz, t + 1, at] for e in range(2) for by in range(2) for bz in range(2)]
            total = functools.reduce(lambda a, b: a + b, kept)
            scale = 1.0 / jnp.maximum(total, SUM_FLOOR)
            for n, v in enumerate(kept):
                pbuf[n // 4, (n // 2) % 2, n % 2, t + 1, at] = v * scale
        return carry

    def sweep(_, carry):
        lax.fori_loop(0, 2 * USED, relax, 0)
        lax.fori_loop(0, LANE_TILES, normalise, 0)
        return carry

    lax.fori_loop(0, ITERS, sweep, 0)

    for by in range(2):
        for bz in range(2):
            for u in range(USED):
                at = 128 * box_tile(by, u)
                basis_ref[0, by, bz, :, at : at + 128] = pbuf[0, by, bz, u + 2 * by + 1, 0:32]
            at = 0 if by == 0 else 768
            basis_ref[0, by, bz, :, at : at + 256] = jnp.zeros((32, 256), F32)

    for by in range(2):

        def couple(step, acc):
            t = step + by
            weights = load_weights(t)
            scale = [gbuf[t, 8 * i : 8 * i + 8] for i in range(5)]
            acc = list(acc)
            images = []
            for bz in range(2):
                tiles = [pbuf[0, by, bz, t + 1, 8 * i : 8 * i + 8] for i in range(4)]
                ups, downs = up_x(tiles, [1, 2, 3, zero]), down_x(tiles, [zero, 0, 1, 2])
                near = stencil(0, by, bz, t, tiles, ups, downs, (0, 1, 2, 3), weights)
                image = [scale[i] * (tiles[i] * (2.0 / 3.0) - near[i]) for i in range(4)]
                beyond = jnp.where(rows == 0, pltpu.roll(tiles[3], 1, 0), 0.0) * weights[4][1]
                before = jnp.where(rows == 7, pltpu.roll(tiles[0], 7, 0), 0.0) * weights[4][0]
                images.append((image, -scale[4] * before, -scale[4] * beyond))
            for partner in range(BLOCKS):
                by2, bz2 = divmod(partner, 2)
                own = [pbuf[0, by2, bz2, t + 1, 8 * i : 8 * i + 8] for i in range(4)]
                side = [pbuf[1, by2, bz2, t + 1, 8 * i : 8 * i + 8] for i in range(5)]
                for bz in range(2):
                    image, before, beyond = images[bz]
                    at = bz * 12 + partner
                    acc[at] += image[0] * side[0] + image[1] * side[1] + before * side[4]
                    acc[at + 4] += image[0] * own[0] + image[1] * own[1] + image[2] * own[2] + image[3] * own[3]
                    acc[at + 8] += image[2] * side[2] + image[3] * side[3] + beyond * side[4]
            return tuple(acc)

        acc = lax.fori_loop(0, USED + 1, couple, (zero,) * 24)
        for bz in range(2):
            for n in range(12):
                sums[2 * by + bz, n] = jnp.sum(acc[bz * 12 + n], axis=0)

    entry = lax.broadcasted_iota(jnp.int32, (16, 128), 0)
    column = lax.broadcasted_iota(jnp.int32, (16, 128), 1)
    for by in range(2):
        for bz in range(2):
            values = jnp.sum(sums[2 * by + bz], axis=1, keepdims=True)
            target = 9 * (entry // 4) + 3 * (lax.rem(entry // 2, 2) - by + 1) + (lax.rem(entry, 2) - bz + 1)
            placed = jnp.where((column == target) & (entry < 12), values, 0.0)
            coarse_ref[0, by, bz, :] = jnp.sum(placed, axis=0)[:27]


def shards(permeability, storage, support_mask, prev_basis):
    vmem = pl.BlockSpec(memory_space=pltpu.VMEM)
    near, far, far2, near2 = pl.pallas_call(
        pack_kernel,
        in_specs=[vmem] * 4,
        out_specs=[vmem] * 4,
        out_shape=[jax.ShapeDtypeStruct((n, 8, 128), F32) for n in (MESSAGE, MESSAGE, THIN_SLOTS, THIN_SLOTS)],
        scratch_shapes=[pltpu.VMEM((32, 128), F32)],
        name="pack",
    )(permeability, storage, support_mask, prev_basis)

    size = lax.axis_size("gx")

    def move(x, step_even, step_odd):
        pairs = [(i, i + (step_odd if i % 2 else step_even)) for i in range(size)]
        return lax.ppermute(x, "gx", [(i, j) for i, j in pairs if 0 <= j < size])

    far = move(far, -1, 1)
    far2 = move(far2, 2, -2)
    near2 = move(near2, -2, 2)
    near = move(near, 1, -1)

    ring = (2, 2, 2, LANE_TILES + 2, 40, 128)
    return pl.pallas_call(
        main_kernel,
        in_specs=[vmem] * 8,
        out_specs=[vmem] * 2,
        out_shape=[
            jax.ShapeDtypeStruct(prev_basis.shape, F32),
            jax.ShapeDtypeStruct((*prev_basis.shape[:3], 27), F32),
        ],
        scratch_shapes=[
            pltpu.VMEM((LANE_TILES + 1, 40, 128), F32),
            pltpu.VMEM((LANE_TILES, 40, 128), F32),
            pltpu.VMEM((6, LANE_TILES, 40, 128), F32),
            pltpu.VMEM((LANE_TILES, 40, 128), F32),
            pltpu.VMEM((4, 8, 128), jnp.int32),
            pltpu.VMEM((5, 8, 128), jnp.int32),
            pltpu.VMEM((8, 128), jnp.int32),
            pltpu.VMEM((2, 2, 2, USED, 40, 128), F32),
            pltpu.VMEM(ring, F32),
            pltpu.VMEM(ring, F32),
            pltpu.VMEM((32, 128), jnp.int32),
            pltpu.VMEM((4, 16, 128), F32),
        ],
        compiler_params=pltpu.CompilerParams(vmem_limit_bytes=32 * 1024 * 1024),
        name="smooth",
    )(permeability, storage, support_mask, prev_basis, near, far, far2, near2)


def solution(mesh):
    placed = (
        P(("groups", "gx"), None),
        P(("groups", "gx"), None),
        P(("groups", "gx"), None, None, None, None),
        P(("groups", "gx"), None, None, None, None),
    )
    return jax.shard_map(
        shards,
        mesh=mesh,
        in_specs=placed,
        out_specs=(
            P(("groups", "gx"), None, None, None, None),
            P(("groups", "gx"), None, None, None),
        ),
        check_vma=False,
    )
```

```python
import functools

import jax
import jax.numpy as jnp
from jax import lax
from jax.experimental import pallas as pl
from jax.experimental.pallas import tpu as pltpu
from jax.sharding import PartitionSpec as P

ITERS = 2
SUM_FLOOR = 0.5
TINY = 1e-30
F32 = jnp.float32


BLOCKS = 4
LANE_TILES = 8
USED = 6

PERM_AT = 2 * BLOCKS * USED
STOR_AT = PERM_AT + LANE_TILES
MASK_AT = STOR_AT + LANE_TILES
REST_AT = MASK_AT + 2
REST = BLOCKS * USED + 2 * LANE_TILES + 1
REST_SLOTS = (REST + 1) // 2
MESSAGE = REST_AT + REST_SLOTS
THIN = BLOCKS * USED + 1
THIN_SLOTS = (THIN + 1) // 2


OWN, TWO, SIDE, STRIP = 8, 48, 64, 112
PADS = (0, 40, 56, 104)
TILES = tuple((OWN + 8 * k, k) for k in range(4)) + ((TWO, 4),) + tuple((SIDE + 8 * n, (n + 2) % 5) for n in range(5))


def box_tile(by, u):
    return u + 2 * (1 - by)


def lanes_of(tile):
    return pl.ds(128 * tile, 128)


def half_rows(upper):
    rows = lax.broadcasted_iota(jnp.int32, (8, 128), 0)
    return rows // 4 == upper


def joined_mask(mask_ref):
    parts = [mask_ref[0, by, bz] for by in range(2) for bz in range(2)]
    return jnp.concatenate(parts, axis=1)


def pack_kernel(perm_ref, stor_ref, mask_ref, prev_ref, near_ref, far_ref, far2_ref, near2_ref, mask_buf):
    odd = lax.rem(lax.axis_index("gx"), 2)
    mask_buf[...] = joined_mask(mask_ref).astype(F32)

    def rows_of(ref, tile, *rest):
        return ref[(*rest[:-1], pl.ds(pl.multiple_of(8 * tile, 8), 8), rest[-1])]

    def put_pairs(out_ref, at, slots, pieces, upper):
        keep = half_rows(upper)
        for s in range(slots):
            tile = pieces[s]()
            if s + slots < len(pieces):
                tile = jnp.where(keep, tile, pltpu.roll(pieces[s + slots](), 4, 0))
            out_ref[at + s] = tile

    def message(out_ref, leftward):
        first = 2 - 2 * leftward
        for xt in range(2):
            for blk in range(BLOCKS):
                by, bz = divmod(blk, 2)
                for u in range(USED):
                    out_ref[(xt * BLOCKS + blk) * USED + u] = rows_of(
                        prev_ref, first + xt, 0, by, bz, lanes_of(box_tile(by, u))
                    )
            out_ref[MASK_AT + xt] = rows_of(mask_buf, first + xt, lanes_of(0))
        for t in range(LANE_TILES):
            out_ref[PERM_AT + t] = rows_of(perm_ref, 1 - leftward, lanes_of(t))
            out_ref[STOR_AT + t] = rows_of(stor_ref, 1 - leftward, lanes_of(t))
        rest = 1 + leftward
        pieces = [
            functools.partial(rows_of, prev_ref, rest, 0, blk // 2, blk % 2, lanes_of(box_tile(blk // 2, u)))
            for blk in range(BLOCKS)
            for u in range(USED)
        ]
        pieces += [functools.partial(rows_of, perm_ref, leftward, lanes_of(t)) for t in range(LANE_TILES)]
        pieces += [functools.partial(rows_of, stor_ref, leftward, lanes_of(t)) for t in range(LANE_TILES)]
        pieces += [functools.partial(rows_of, mask_buf, rest, lanes_of(0))]
        put_pairs(out_ref, REST_AT, REST_SLOTS, pieces, 1 - leftward)

    def thin(out_ref, leftward):
        edge = 3 - 3 * leftward
        pieces = [
            functools.partial(rows_of, prev_ref, edge, 0, blk // 2, blk % 2, lanes_of(box_tile(blk // 2, u)))
            for blk in range(BLOCKS)
            for u in range(USED)
        ]
        pieces += [functools.partial(rows_of, mask_buf, edge, lanes_of(0))]
        put_pairs(out_ref, 0, THIN_SLOTS, pieces, 1 - leftward)

    message(far_ref, 1 - odd)
    message(near_ref, odd)
    thin(far2_ref, odd)
    thin(near2_ref, 1 - odd)


def main_kernel(
    perm_ref, stor_ref, mask_ref, prev_ref, near_ref, far_ref, far2_ref, near2_ref,
    basis_ref, coarse_ref,
    kbuf, cbuf, wbuf, gbuf, sup, pbuf, qbuf, own_mask, sums,
):
    here = lax.axis_index("gx")
    last = lax.axis_size("gx") - 1
    odd = lax.rem(here, 2) == 1
    rows = lax.broadcasted_iota(jnp.int32, (8, 128), 0)
    lanes = lax.broadcasted_iota(jnp.int32, (8, 128), 1)
    heights = lax.rem(lanes, 32)
    low_rows = rows < 4
    zero = jnp.zeros((8, 128), F32)

    def left_big(i):
        return jnp.where(odd, near_ref[i], far_ref[i])

    def right_big(i):
        return jnp.where(odd, far_ref[i], near_ref[i])

    def left_thin(i):
        return jnp.where(odd, near2_ref[i], far2_ref[i])

    def right_thin(i):
        return jnp.where(odd, far2_ref[i], near2_ref[i])

    def paired(left, right, at, slots, index):
        slot = index % slots
        tile = jnp.where(low_rows, right(at + slot), left(at + slot))
        if index >= slots:
            other = jnp.where(low_rows, left(at + slot), right(at + slot))
            tile = pltpu.roll(other, 4, 0)
        return tile

    def rest_tile(index):
        return paired(left_big, right_big, REST_AT, REST_SLOTS, index)

    def thin_tile(index):
        return paired(left_thin, right_thin, 0, THIN_SLOTS, index)

    for t in range(LANE_TILES):
        for buf, ref, bulk, rest in (
            (kbuf, perm_ref, PERM_AT, BLOCKS * USED),
            (cbuf, stor_ref, STOR_AT, BLOCKS * USED + LANE_TILES),
        ):
            buf[t, 0:8] = left_big(bulk + t)
            buf[t, 8:16] = ref[0:8, 128 * t : 128 * t + 128]
            buf[t, 16:24] = ref[8:16, 128 * t : 128 * t + 128]
            buf[t, 24:32] = right_big(bulk + t)
            buf[t, 32:40] = rest_tile(rest + t)

    own_mask[...] = joined_mask(mask_ref)
    block = lanes // 32
    inner = (heights >= 8) & (heights < 24)
    core_bits = jnp.where(inner, jnp.where(lax.rem(block, 2) == 0, 0xFFFF, 0xFFFF00), 0)
    own_bits = [own_mask[8 * k : 8 * k + 8] for k in range(4)]
    own_bits[0] = jnp.where(here == 0, 0, own_bits[0])
    own_bits[1] |= core_bits
    own_bits[2] |= core_bits
    own_bits[3] = jnp.where(here == last, 0, own_bits[3])
    two_bits = thin_tile(THIN - 1).astype(jnp.int32)
    side_bits = [
        right_big(MASK_AT).astype(jnp.int32),
        right_big(MASK_AT + 1).astype(jnp.int32) | core_bits,
        rest_tile(REST - 1).astype(jnp.int32) | core_bits,
        left_big(MASK_AT).astype(jnp.int32) | core_bits,
        left_big(MASK_AT + 1).astype(jnp.int32),
    ]

    lane_bits = []
    for bz in range(2):
        offset = heights - 8 * bz
        valid = (offset >= 0) & (offset < (18, 24)[bz])
        lane_bits.append(jnp.where(valid, jnp.left_shift(1, jnp.clip(offset, 0, 23)), 0))

    def support_of(tile, by, bz, u):
        index = 32 * (2 * by + bz) + 4 * u + 8 * (1 - by) + lanes // 32
        spread = jnp.take_along_axis(tile, index, axis=1, mode="promise_in_bounds")
        return jnp.where((spread & lane_bits[bz]) != 0, 1.0, 0.0)

    for by in range(2):
        for bz in range(2):
            for u in range(USED):
                cell = (2 * by + bz) * USED + u
                for row in PADS:
                    pbuf[by, bz, u, row : row + 8] = zero

                def put(row, tile, bits):
                    s = support_of(bits, by, bz, u)
                    sup[by, bz, u, row : row + 8] = s
                    pbuf[by, bz, u, row : row + 8] = s * tile

                for k in range(4):
                    at = 128 * box_tile(by, u)
                    put(OWN + 8 * k, prev_ref[0, by, bz, 8 * k : 8 * k + 8, at : at + 128], own_bits[k])
                put(TWO, thin_tile(cell), two_bits)
                put(SIDE, right_big(cell), side_bits[0])
                put(SIDE + 8, right_big(BLOCKS * USED + cell), side_bits[1])
                put(SIDE + 16, rest_tile(cell), side_bits[2])
                put(SIDE + 24, left_big(cell), side_bits[3])
                put(SIDE + 32, left_big(BLOCKS * USED + cell), side_bits[4])

    def up_y(here_, next_):
        return pltpu.roll(jnp.where(lanes >= 32, here_, next_), 96, 1)

    def down_y(here_, before):
        return pltpu.roll(jnp.where(lanes < 96, here_, before), 32, 1)

    def up_z(v):
        return pltpu.roll(v, 127, 1)

    def down_z(v):
        return pltpu.roll(v, 1, 1)

    def inverse(v):
        first = pl.reciprocal(v, approx=True)
        return first * (2.0 - v * first)

    def harmonic(a, b):
        return 2.0 * (a * b) * inverse(jnp.maximum(a + b, TINY))

    south = [zero] * 5
    for t in range(LANE_TILES):
        k = [kbuf[t, 8 * i : 8 * i + 8] for i in range(5)]
        turned = [pltpu.roll(v, 7, 0) for v in k]
        east = [harmonic(k[i], jnp.where(rows < 7, turned[i], turned[(i + 1) % 5])) for i in range(5)]
        turned = [pltpu.roll(v, 1, 0) for v in east]
        west = [jnp.where(rows > 0, turned[i], turned[i - 1]) for i in range(5)]
        for i in range(5):
            above = kbuf[t + 1, 8 * i : 8 * i + 8] if t + 1 < LANE_TILES else zero
            north = harmonic(k[i], up_y(k[i], above))
            upper = jnp.where(heights < 31, harmonic(k[i], up_z(k[i])), 0.0)
            lower = down_z(upper)
            below = down_y(north, south[i])
            south[i] = north
            diag = cbuf[t, 8 * i : 8 * i + 8] + east[i] + west[i] + north + below + upper + lower
            scale = (2.0 / 3.0) * inverse(jnp.maximum(diag, TINY))
            for d, face in enumerate((east[i], west[i], north, below, upper, lower)):
                wbuf[t, d, 8 * i : 8 * i + 8] = face * scale
            gbuf[t, 8 * i : 8 * i + 8] = 1.5 * diag

    def weights_of(t):
        return [[wbuf[t, d, 8 * i : 8 * i + 8] for d in range(6)] for i in range(5)]

    def tile_of(by, bz, u, row):
        if 0 <= u < USED:
            return pbuf[by, bz, u, row : row + 8]
        return zero

    def stencil(by, bz, u, row, v, w):
        near = w[0] * pbuf[by, bz, u, row + 1 : row + 9] + w[1] * pbuf[by, bz, u, row - 1 : row + 7]
        near += w[2] * up_y(v, tile_of(by, bz, u + 1, row)) + w[3] * down_y(v, tile_of(by, bz, u - 1, row))
        return near + (w[4] * up_z(v) + w[5] * down_z(v))

    def relax(by, carry):
        for u in range(USED):
            weights = weights_of(u + 2 * by)
            for bz in range(2):
                for row, i in TILES:
                    v = tile_of(by, bz, u, row)
                    near = stencil(by, bz, u, row, v, weights[i])
                    s = sup[by, bz, u, row : row + 8]
                    qbuf[by, bz, u, row : row + 8] = s * jnp.maximum(v * (1.0 / 3.0) + near, 0.0)
        return carry

    def normalise(final):
        for t in range(LANE_TILES):
            blocks = [(by, bz, t - 2 * by) for by in range(2) for bz in range(2) if 0 <= t - 2 * by < USED]
            for i in range(5):
                at = [(b, row) for b in blocks for row, ring in TILES if ring == i]
                kept = [qbuf[by, bz, u, row : row + 8] for (by, bz, u), row in at]
                total = functools.reduce(lambda a, b: a + b, kept)
                scale = inverse(jnp.maximum(total, SUM_FLOOR))
                for ((by, bz, u), row), v in zip(at, kept):
                    v = v * scale
                    pbuf[by, bz, u, row : row + 8] = v
                    if final and row < TWO:
                        lane = 128 * box_tile(by, u)
                        basis_ref[0, by, bz, row - OWN : row - OWN + 8, lane : lane + 128] = v

    for sweep in range(ITERS):
        lax.fori_loop(0, 2, relax, 0)
        normalise(sweep == ITERS - 1)

    for by in range(2):
        for bz in range(2):
            at = 0 if by == 0 else 768
            basis_ref[0, by, bz, :, at : at + 256] = jnp.zeros((32, 256), F32)

    for by in range(2):
        acc = [[] for _ in range(24)]
        for t in range(by, by + USED + 1):
            u = t - 2 * by
            weights = weights_of(t)
            scale = [gbuf[t, 8 * i : 8 * i + 8] for i in range(5)]
            images = []
            for bz in range(2):
                image = []
                for k in range(4):
                    row = OWN + 8 * k
                    if 0 <= u < USED:
                        v = tile_of(by, bz, u, row)
                        image.append(scale[k] * (v * (2.0 / 3.0) - stencil(by, bz, u, row, v, weights[k])))
                    elif u < 0:
                        image.append(-scale[k] * (weights[k][2] * up_y(zero, tile_of(by, bz, u + 1, row))))
                    else:
                        image.append(-scale[k] * (weights[k][3] * down_y(zero, tile_of(by, bz, u - 1, row))))
                before = beyond = None
                if 0 <= u < USED:
                    edge = pbuf[by, bz, u, OWN + 31 : OWN + 39]
                    beyond = -scale[4] * (weights[4][1] * edge)
                    edge = pbuf[by, bz, u, OWN - 7 : OWN + 1]
                    before = -scale[4] * (weights[4][0] * edge)
                images.append((image, before, beyond))
            for partner in range(BLOCKS):
                by2, bz2 = divmod(partner, 2)
                u2 = t - 2 * by2
                if not 0 <= u2 < USED:
                    continue
                own = [tile_of(by2, bz2, u2, OWN + 8 * k) for k in range(4)]
                side = [tile_of(by2, bz2, u2, SIDE + 8 * k) for k in range(5)]
                for bz in range(2):
                    image, before, beyond = images[bz]
                    at = bz * 12 + partner
                    acc[at] += [image[0] * side[3], image[1] * side[4]]
                    acc[at + 4] += [image[k] * own[k] for k in range(4)]
                    acc[at + 8] += [image[2] * side[0], image[3] * side[1]]
                    if before is not None:
                        acc[at] += [before * side[2]]
                        acc[at + 8] += [beyond * side[2]]
            acc = [[functools.reduce(lambda a, b: a + b, terms)] if terms else [] for terms in acc]
        for bz in range(2):
            for n in range(12):
                sums[2 * by + bz, n] = jnp.sum(acc[bz * 12 + n][0], axis=0)

    entry = lax.broadcasted_iota(jnp.int32, (16, 128), 0)
    column = lax.broadcasted_iota(jnp.int32, (16, 128), 1)
    for by in range(2):
        for bz in range(2):
            values = jnp.sum(sums[2 * by + bz], axis=1, keepdims=True)
            target = 9 * (entry // 4) + 3 * (lax.rem(entry // 2, 2) - by + 1) + (lax.rem(entry, 2) - bz + 1)
            placed = jnp.where((column == target) & (entry < 12), values, 0.0)
            coarse_ref[0, by, bz, :] = jnp.sum(placed, axis=0)[:27]


def shards(permeability, storage, support_mask, prev_basis):
    vmem = pl.BlockSpec(memory_space=pltpu.VMEM)
    near, far, far2, near2 = pl.pallas_call(
        pack_kernel,
        in_specs=[vmem] * 4,
        out_specs=[vmem] * 4,
        out_shape=[jax.ShapeDtypeStruct((n, 8, 128), F32) for n in (MESSAGE, MESSAGE, THIN_SLOTS, THIN_SLOTS)],
        scratch_shapes=[pltpu.VMEM((32, 128), F32)],
        name="pack",
    )(permeability, storage, support_mask, prev_basis)

    size = lax.axis_size("gx")

    def move(x, step_even, step_odd):
        pairs = [(i, i + (step_odd if i % 2 else step_even)) for i in range(size)]
        return lax.ppermute(x, "gx", [(i, j) for i, j in pairs if 0 <= j < size])

    far = move(far, -1, 1)
    far2 = move(far2, 2, -2)
    near2 = move(near2, -2, 2)
    near = move(near, 1, -1)

    strips = (2, 2, USED, STRIP, 128)
    return pl.pallas_call(
        main_kernel,
        in_specs=[vmem] * 8,
        out_specs=[vmem] * 2,
        out_shape=[
            jax.ShapeDtypeStruct(prev_basis.shape, F32),
            jax.ShapeDtypeStruct((*prev_basis.shape[:3], 27), F32),
        ],
        scratch_shapes=[
            pltpu.VMEM((LANE_TILES, 40, 128), F32),
            pltpu.VMEM((LANE_TILES, 40, 128), F32),
            pltpu.VMEM((LANE_TILES, 6, 40, 128), F32),
            pltpu.VMEM((LANE_TILES, 40, 128), F32),
            pltpu.VMEM(strips, F32),
            pltpu.VMEM(strips, F32),
            pltpu.VMEM(strips, F32),
            pltpu.VMEM((32, 128), jnp.int32),
            pltpu.VMEM((4, 16, 128), F32),
        ],
        compiler_params=pltpu.CompilerParams(vmem_limit_bytes=32 * 1024 * 1024),
        name="smooth",
    )(permeability, storage, support_mask, prev_basis, near, far, far2, near2)


def solution(mesh):
    placed = (
        P(("groups", "gx"), None),
        P(("groups", "gx"), None),
        P(("groups", "gx"), None, None, None, None),
        P(("groups", "gx"), None, None, None, None),
    )
    return jax.shard_map(
        shards,
        mesh=mesh,
        in_specs=placed,
        out_specs=(
            P(("groups", "gx"), None, None, None, None),
            P(("groups", "gx"), None, None, None),
        ),
        check_vma=False,
    )
```

```python
import functools

import jax
import jax.numpy as jnp
from jax import lax
from jax.experimental import pallas as pl
from jax.experimental.pallas import tpu as pltpu
from jax.sharding import PartitionSpec as P

ITERS = 2
SUM_FLOOR = 0.5
TINY = 1e-30
F32 = jnp.float32


BLOCKS = 4
LANE_TILES = 8
USED = 6

LEVELS = 16
BULK = 2 * USED * 3
PERM_AT = BULK
STOR_AT = PERM_AT + LANE_TILES
MASK_AT = STOR_AT + LANE_TILES
REST_AT = 8 * (MASK_AT + 2)
HALF = USED // 2
CELLS = 2 * (HALF + USED)
REST = CELLS + 2 * LANE_TILES + 1
THIN = CELLS + 1
EDGE = 3


def whole_tiles(rows):
    return 8 * ((rows + 7) // 8)


MESSAGE = whole_tiles(REST_AT + EDGE * REST + 8 - EDGE)
THIN_MESSAGE = whole_tiles(EDGE * THIN + 8 - EDGE)

OWN, TWO, SIDE, STRIP = 8, 48, 64, 112
PADS = (0, 40, 56, 104)
TILES = tuple((OWN + 8 * k, k) for k in range(4)) + ((TWO, 4),) + tuple((SIDE + 8 * n, (n + 2) % 5) for n in range(5))


def box_tile(by, u):
    return u + 2 * (1 - by)


def lanes_of(tile):
    return pl.ds(128 * tile, 128)


def joined_mask(mask_ref):
    parts = [mask_ref[0, by, bz] for by in range(2) for bz in range(2)]
    return jnp.concatenate(parts, axis=1)


def height_of_lane():
    return lax.rem(lax.broadcasted_iota(jnp.int32, (8, 128), 1), 32)


def share(first, second):
    heights = height_of_lane()
    first_up, second_up = pltpu.roll(first, LEVELS, 1), pltpu.roll(second, LEVELS, 1)
    return jnp.where(heights < LEVELS, first, second_up), first_up, second_up


def unshare(common, first_rest, second_rest):
    heights = height_of_lane()
    first = jnp.where(heights < LEVELS, common, pltpu.roll(first_rest, 128 - LEVELS, 1))
    second = pltpu.roll(jnp.where(heights >= LEVELS, common, second_rest), 128 - LEVELS, 1)
    return first, second


def put_edges(out_ref, at, pieces, rightward):
    for n, tile in enumerate(pieces):
        tile = jnp.where(rightward == 1, pltpu.roll(tile, EDGE, 0), tile)
        out_ref[at + EDGE * n : at + EDGE * (n + 1)] = tile[:EDGE]


def cells(tile):
    low = height_of_lane() < 2
    pieces = []
    for by in range(2):
        common, rests = [], [None] * USED
        for u in range(HALF):
            both, rests[u], rests[u + HALF] = share(tile(by, 0, u), tile(by, 0, u + HALF))
            common.append(both)
        pieces += common + [jnp.where(low, rests[u], tile(by, 1, u)) for u in range(USED)]
    return pieces


def put_message(out_ref, leftward, prev_tile, perm_tile, stor_tile, mask_tile):
    low = height_of_lane() < 2
    def put_tile(n, tile):
        out_ref[8 * n : 8 * n + 8] = tile

    for by in range(2):
        for u in range(USED):
            common, first_up, second_up = share(prev_tile(0, by, 0, u), prev_tile(1, by, 0, u))
            at = 24 * (by * USED + u)
            out_ref[at : at + 8] = common
            out_ref[at + 8 : at + 16] = jnp.where(low, first_up, prev_tile(0, by, 1, u))
            out_ref[at + 16 : at + 24] = jnp.where(low, second_up, prev_tile(1, by, 1, u))
    for n in range(2):
        put_tile(MASK_AT + n, mask_tile(n))
    for t in range(LANE_TILES):
        put_tile(PERM_AT + t, perm_tile(1 - leftward, t))
        put_tile(STOR_AT + t, stor_tile(1 - leftward, t))
    pieces = cells(functools.partial(prev_tile, 2))
    pieces += [perm_tile(leftward, t) for t in range(LANE_TILES)]
    pieces += [stor_tile(leftward, t) for t in range(LANE_TILES)]
    pieces += [mask_tile(2)]
    put_edges(out_ref, REST_AT, pieces, 1 - leftward)
    tail = REST_AT + EDGE * REST
    out_ref[tail:MESSAGE] = jnp.zeros((MESSAGE - tail, 128), F32)


def eight(tile):
    return pl.ds(pl.multiple_of(8 * tile, 8), 8)


def put_thin(out_ref, leftward, prev_tile, mask_tile):
    edge = 3 - 3 * leftward
    pieces = cells(functools.partial(prev_tile, edge)) + [mask_tile(edge)]
    put_edges(out_ref, 0, pieces, 1 - leftward)
    tail = EDGE * THIN
    out_ref[tail:THIN_MESSAGE] = jnp.zeros((THIN_MESSAGE - tail, 128), F32)


def pack_kernel(
    perm_ref, stor_ref, mask_ref, prev_ref, far_ref, far2_ref, near2_ref, near_ref, perm, stor, mask, prev, mask_buf, sems
):
    odd = lax.rem(lax.axis_index("gx"), 2)
    copies = []
    for by in range(2):
        for bz in range(2):
            blk = 2 * by + bz
            lanes = pl.ds(128 * box_tile(by, 0), 128 * USED)
            copies.append((prev_ref.at[0, by, bz, :, lanes], prev.at[blk]))
            copies.append((mask_ref.at[0, by, bz], mask.at[blk]))
    copies += [(perm_ref, perm), (stor_ref, stor)]
    copies = [pltpu.make_async_copy(src, dst, sems.at[n]) for n, (src, dst) in enumerate(copies)]
    for copy in copies:
        copy.start()
    for copy in copies:
        copy.wait()
    mask_buf[...] = jnp.concatenate([mask[blk] for blk in range(BLOCKS)], axis=1).astype(F32)

    def prev_tile(tile, by, bz, u):
        return prev[2 * by + bz, eight(tile), lanes_of(u)]

    def mask_tile(tile):
        return mask_buf[eight(tile), lanes_of(0)]

    def message(out_ref, leftward):
        def tile_at(n):
            return jnp.where(leftward == 1, n, (2, 3, 1)[n])

        put_message(
            out_ref,
            leftward,
            lambda n, by, bz, u: prev_tile(tile_at(n), by, bz, u),
            lambda n, t: perm[eight(n), lanes_of(t)],
            lambda n, t: stor[eight(n), lanes_of(t)],
            lambda n: mask_tile(tile_at(n)),
        )

    message(far_ref, 1 - odd)
    put_thin(far2_ref, odd, prev_tile, mask_tile)
    put_thin(near2_ref, 1 - odd, prev_tile, mask_tile)
    message(near_ref, odd)


def main_kernel(
    perm_ref, stor_ref, mask_ref, prev_ref, near_ref, far_ref, far2_ref, near2_ref,
    basis_ref, coarse_ref,
    kbuf, cbuf, wbuf, gbuf, sup, pbuf, qbuf, own_mask, sums,
):
    here = lax.axis_index("gx")
    last = lax.axis_size("gx") - 1
    odd = lax.rem(here, 2) == 1
    rows = lax.broadcasted_iota(jnp.int32, (8, 128), 0)
    lanes = lax.broadcasted_iota(jnp.int32, (8, 128), 1)
    heights = lax.rem(lanes, 32)
    low_rows = rows < 4
    zero = jnp.zeros((8, 128), F32)

    def left_big(i):
        at = pl.ds(8 * i, 8)
        return jnp.where(odd, near_ref[at], far_ref[at])

    def right_big(i):
        at = pl.ds(8 * i, 8)
        return jnp.where(odd, far_ref[at], near_ref[at])

    def edges(ref, at, left):
        start = at - (8 - EDGE) if left else at
        tile = ref[max(start, 0) : max(start, 0) + 8]
        return pltpu.roll(tile, -start, 0) if start < 0 else tile

    def rest_tile(index):
        at = REST_AT + EDGE * index
        right = jnp.where(odd, edges(far_ref, at, False), edges(near_ref, at, False))
        left = jnp.where(odd, edges(near_ref, at, True), edges(far_ref, at, True))
        return jnp.where(low_rows, right, left)

    def thin_tile(index):
        at = EDGE * index
        right = jnp.where(odd, edges(far2_ref, at, False), edges(near2_ref, at, False))
        left = jnp.where(odd, edges(near2_ref, at, True), edges(far2_ref, at, True))
        return jnp.where(low_rows, right, left)

    for t in range(LANE_TILES):
        for buf, ref, bulk, rest in (
            (kbuf, perm_ref, PERM_AT, CELLS),
            (cbuf, stor_ref, STOR_AT, CELLS + LANE_TILES),
        ):
            buf[t, 0:8] = left_big(bulk + t)
            buf[t, 8:16] = ref[0:8, 128 * t : 128 * t + 128]
            buf[t, 16:24] = ref[8:16, 128 * t : 128 * t + 128]
            buf[t, 24:32] = right_big(bulk + t)
            buf[t, 32:40] = rest_tile(rest + t)

    own_mask[...] = joined_mask(mask_ref)
    block = lanes // 32
    inner = (heights >= 8) & (heights < 24)
    core_bits = jnp.where(inner, jnp.where(lax.rem(block, 2) == 0, 0xFFFF, 0xFFFF00), 0)
    own_bits = [own_mask[8 * k : 8 * k + 8] for k in range(4)]
    own_bits[0] = jnp.where(here == 0, 0, own_bits[0])
    own_bits[1] |= core_bits
    own_bits[2] |= core_bits
    own_bits[3] = jnp.where(here == last, 0, own_bits[3])
    two_bits = thin_tile(THIN - 1).astype(jnp.int32)
    side_bits = [
        right_big(MASK_AT).astype(jnp.int32),
        right_big(MASK_AT + 1).astype(jnp.int32) | core_bits,
        rest_tile(REST - 1).astype(jnp.int32) | core_bits,
        left_big(MASK_AT).astype(jnp.int32) | core_bits,
        left_big(MASK_AT + 1).astype(jnp.int32),
    ]

    lane_bits = []
    for bz in range(2):
        offset = heights - 8 * bz
        valid = (offset >= 0) & (offset < (18, 24)[bz])
        lane_bits.append(jnp.where(valid, jnp.left_shift(1, jnp.clip(offset, 0, 23)), 0))

    def support_of(tile, by, bz, u):
        index = 32 * (2 * by + bz) + 4 * u + 8 * (1 - by) + lanes // 32
        spread = jnp.take_along_axis(tile, index, axis=1, mode="promise_in_bounds")
        return jnp.where((spread & lane_bits[bz]) != 0, 1.0, 0.0)

    side = [{} for _ in range(5)]
    two = {}
    for by in range(2):
        for u in range(USED):
            at = 3 * (by * USED + u)
            for side_tile, first in ((right_big, 0), (left_big, 3)):
                common, first_top, second_top = [side_tile(at + n) for n in range(3)]
                low, high = unshare(common, first_top, second_top)
                side[first][by, 0, u], side[first + 1][by, 0, u] = low, high
                side[first][by, 1, u], side[first + 1][by, 1, u] = first_top, second_top
        base = by * (HALF + USED)
        for fetch, cells_of in ((rest_tile, side[2]), (thin_tile, two)):
            for u in range(HALF):
                tops = [fetch(base + HALF + u), fetch(base + HALF + u + HALF)]
                low, high = unshare(fetch(base + u), *tops)
                cells_of[by, 0, u], cells_of[by, 0, u + HALF] = low, high
                cells_of[by, 1, u], cells_of[by, 1, u + HALF] = tops

    for by in range(2):
        for bz in range(2):
            for u in range(USED):
                for row in PADS:
                    pbuf[by, bz, u, row : row + 8] = zero

                def put(row, tile, bits):
                    s = support_of(bits, by, bz, u)
                    sup[by, bz, u, row : row + 8] = s
                    pbuf[by, bz, u, row : row + 8] = s * tile

                for k in range(4):
                    at = 128 * box_tile(by, u)
                    put(OWN + 8 * k, prev_ref[0, by, bz, 8 * k : 8 * k + 8, at : at + 128], own_bits[k])
                put(TWO, two[by, bz, u], two_bits)
                for n in range(5):
                    put(SIDE + 8 * n, side[n][by, bz, u], side_bits[n])

    def up_y(here_, next_):
        return pltpu.roll(jnp.where(lanes >= 32, here_, next_), 96, 1)

    def down_y(here_, before):
        return pltpu.roll(jnp.where(lanes < 96, here_, before), 32, 1)

    def up_z(v):
        return pltpu.roll(v, 127, 1)

    def down_z(v):
        return pltpu.roll(v, 1, 1)

    def inverse(v):
        first = pl.reciprocal(v, approx=True)
        return first * (2.0 - v * first)

    def harmonic(a, b):
        return 2.0 * (a * b) * inverse(jnp.maximum(a + b, TINY))

    south = [zero] * 5
    for t in range(LANE_TILES):
        k = [kbuf[t, 8 * i : 8 * i + 8] for i in range(5)]
        turned = [pltpu.roll(v, 7, 0) for v in k]
        east = [harmonic(k[i], jnp.where(rows < 7, turned[i], turned[(i + 1) % 5])) for i in range(5)]
        turned = [pltpu.roll(v, 1, 0) for v in east]
        west = [jnp.where(rows > 0, turned[i], turned[i - 1]) for i in range(5)]
        for i in range(5):
            above = kbuf[t + 1, 8 * i : 8 * i + 8] if t + 1 < LANE_TILES else zero
            north = harmonic(k[i], up_y(k[i], above))
            upper = jnp.where(heights < 31, harmonic(k[i], up_z(k[i])), 0.0)
            lower = down_z(upper)
            below = down_y(north, south[i])
            south[i] = north
            diag = cbuf[t, 8 * i : 8 * i + 8] + east[i] + west[i] + north + below + upper + lower
            scale = (2.0 / 3.0) * inverse(jnp.maximum(diag, TINY))
            for d, face in enumerate((east[i], west[i], north, below, upper, lower)):
                wbuf[t, d, 8 * i : 8 * i + 8] = face * scale
            gbuf[t, 8 * i : 8 * i + 8] = 1.5 * diag

    def weights_of(t):
        return [[wbuf[t, d, 8 * i : 8 * i + 8] for d in range(6)] for i in range(5)]

    def tile_of(by, bz, u, row):
        if 0 <= u < USED:
            return pbuf[by, bz, u, row : row + 8]
        return zero

    def stencil(by, bz, u, row, v, w):
        near = w[0] * pbuf[by, bz, u, row + 1 : row + 9] + w[1] * pbuf[by, bz, u, row - 1 : row + 7]
        near += w[2] * up_y(v, tile_of(by, bz, u + 1, row)) + w[3] * down_y(v, tile_of(by, bz, u - 1, row))
        return near + (w[4] * up_z(v) + w[5] * down_z(v))

    def relax(by, carry):
        for u in range(USED):
            weights = weights_of(u + 2 * by)
            for bz in range(2):
                for row, i in TILES:
                    v = tile_of(by, bz, u, row)
                    near = stencil(by, bz, u, row, v, weights[i])
                    s = sup[by, bz, u, row : row + 8]
                    qbuf[by, bz, u, row : row + 8] = s * jnp.maximum(v * (1.0 / 3.0) + near, 0.0)
        return carry

    def normalise(final):
        for t in range(LANE_TILES):
            blocks = [(by, bz, t - 2 * by) for by in range(2) for bz in range(2) if 0 <= t - 2 * by < USED]
            for i in range(5):
                at = [(b, row) for b in blocks for row, ring in TILES if ring == i]
                kept = [qbuf[by, bz, u, row : row + 8] for (by, bz, u), row in at]
                total = functools.reduce(lambda a, b: a + b, kept)
                scale = inverse(jnp.maximum(total, SUM_FLOOR))
                for ((by, bz, u), row), v in zip(at, kept):
                    v = v * scale
                    pbuf[by, bz, u, row : row + 8] = v
                    if final and row < TWO:
                        lane = 128 * box_tile(by, u)
                        basis_ref[0, by, bz, row - OWN : row - OWN + 8, lane : lane + 128] = v

    for sweep in range(ITERS):
        lax.fori_loop(0, 2, relax, 0)
        normalise(sweep == ITERS - 1)

    for by in range(2):
        for bz in range(2):
            at = 0 if by == 0 else 768
            basis_ref[0, by, bz, :, at : at + 256] = jnp.zeros((32, 256), F32)

    for by in range(2):
        acc = [[] for _ in range(24)]
        for t in range(by, by + USED + 1):
            u = t - 2 * by
            weights = weights_of(t)
            scale = [gbuf[t, 8 * i : 8 * i + 8] for i in range(5)]
            images = []
            for bz in range(2):
                image = []
                for k in range(4):
                    row = OWN + 8 * k
                    if 0 <= u < USED:
                        v = tile_of(by, bz, u, row)
                        image.append(scale[k] * (v * (2.0 / 3.0) - stencil(by, bz, u, row, v, weights[k])))
                    elif u < 0:
                        image.append(-scale[k] * (weights[k][2] * up_y(zero, tile_of(by, bz, u + 1, row))))
                    else:
                        image.append(-scale[k] * (weights[k][3] * down_y(zero, tile_of(by, bz, u - 1, row))))
                before = beyond = None
                if 0 <= u < USED:
                    edge = pbuf[by, bz, u, OWN + 31 : OWN + 39]
                    beyond = -scale[4] * (weights[4][1] * edge)
                    edge = pbuf[by, bz, u, OWN - 7 : OWN + 1]
                    before = -scale[4] * (weights[4][0] * edge)
                images.append((image, before, beyond))
            for partner in range(BLOCKS):
                by2, bz2 = divmod(partner, 2)
                u2 = t - 2 * by2
                if not 0 <= u2 < USED:
                    continue
                own = [tile_of(by2, bz2, u2, OWN + 8 * k) for k in range(4)]
                side = [tile_of(by2, bz2, u2, SIDE + 8 * k) for k in range(5)]
                for bz in range(2):
                    image, before, beyond = images[bz]
                    at = bz * 12 + partner
                    acc[at] += [image[0] * side[3], image[1] * side[4]]
                    acc[at + 4] += [image[k] * own[k] for k in range(4)]
                    acc[at + 8] += [image[2] * side[0], image[3] * side[1]]
                    if before is not None:
                        acc[at] += [before * side[2]]
                        acc[at + 8] += [beyond * side[2]]
            acc = [[functools.reduce(lambda a, b: a + b, terms)] if terms else [] for terms in acc]
        for bz in range(2):
            for n in range(12):
                sums[2 * by + bz, n] = jnp.sum(acc[bz * 12 + n][0], axis=0)

    entry = lax.broadcasted_iota(jnp.int32, (16, 128), 0)
    column = lax.broadcasted_iota(jnp.int32, (16, 128), 1)
    for by in range(2):
        for bz in range(2):
            values = jnp.sum(sums[2 * by + bz], axis=1, keepdims=True)
            target = 9 * (entry // 4) + 3 * (lax.rem(entry // 2, 2) - by + 1) + (lax.rem(entry, 2) - bz + 1)
            placed = jnp.where((column == target) & (entry < 12), values, 0.0)
            coarse_ref[0, by, bz, :] = jnp.sum(placed, axis=0)[:27]


def shards(permeability, storage, support_mask, prev_basis):
    vmem = pl.BlockSpec(memory_space=pltpu.VMEM)
    arguments = (permeability, storage, support_mask, prev_basis)
    far, far2, near2, near = pl.pallas_call(
        pack_kernel,
        in_specs=[pl.BlockSpec(memory_space=pl.ANY)] * 4,
        out_specs=[vmem] * 4,
        out_shape=[pltpu.VMEM((n, 128), F32) for n in (MESSAGE, THIN_MESSAGE, THIN_MESSAGE, MESSAGE)],
        scratch_shapes=[
            pltpu.VMEM(permeability.shape, F32),
            pltpu.VMEM(storage.shape, F32),
            pltpu.VMEM((BLOCKS, 32, 32), jnp.int32),
            pltpu.VMEM((BLOCKS, 32, 128 * USED), F32),
            pltpu.VMEM((32, 128), F32),
            pltpu.SemaphoreType.DMA((2 * BLOCKS + 2,)),
        ],
        name="pack",
    )(*arguments)
    size = lax.axis_size("gx")

    def move(x, step_even, step_odd):
        pairs = [(i, i + (step_odd if i % 2 else step_even)) for i in range(size)]
        return lax.ppermute(x, "gx", [(i, j) for i, j in pairs if 0 <= j < size])

    far = move(far, -1, 1)
    far2 = move(far2, 2, -2)
    near2 = move(near2, -2, 2)
    near = move(near, 1, -1)

    strips = (2, 2, USED, STRIP, 128)
    return pl.pallas_call(
        main_kernel,
        in_specs=[vmem] * 8,
        out_specs=[vmem] * 2,
        out_shape=[
            jax.ShapeDtypeStruct(prev_basis.shape, F32),
            jax.ShapeDtypeStruct((*prev_basis.shape[:3], 27), F32),
        ],
        scratch_shapes=[
            pltpu.VMEM((LANE_TILES, 40, 128), F32),
            pltpu.VMEM((LANE_TILES, 40, 128), F32),
            pltpu.VMEM((LANE_TILES, 6, 40, 128), F32),
            pltpu.VMEM((LANE_TILES, 40, 128), F32),
            pltpu.VMEM(strips, F32),
            pltpu.VMEM(strips, F32),
            pltpu.VMEM(strips, F32),
            pltpu.VMEM((32, 128), jnp.int32),
            pltpu.VMEM((4, 16, 128), F32),
        ],
        compiler_params=pltpu.CompilerParams(vmem_limit_bytes=32 * 1024 * 1024),
        name="smooth",
    )(*arguments, near, far, far2, near2)


def solution(mesh):
    placed = (
        P(("groups", "gx"), None),
        P(("groups", "gx"), None),
        P(("groups", "gx"), None, None, None, None),
        P(("groups", "gx"), None, None, None, None),
    )
    return jax.shard_map(
        shards,
        mesh=mesh,
        in_specs=placed,
        out_specs=(
            P(("groups", "gx"), None, None, None, None),
            P(("groups", "gx"), None, None, None),
        ),
        check_vma=False,
    )
```

```python
import functools

import jax
import jax.numpy as jnp
from jax import lax
from jax.experimental import pallas as pl
from jax.experimental.pallas import tpu as pltpu
from jax.sharding import PartitionSpec as P

ITERS = 2
SUM_FLOOR = 0.5
TINY = 1e-30
F32 = jnp.float32


BLOCKS = 4
LANE_TILES = 8
USED = 6

LEVELS = 16
BULK = 2 * USED * 3
PERM_AT = BULK
STOR_AT = PERM_AT + LANE_TILES
MASK_AT = STOR_AT + LANE_TILES
REST_AT = 8 * (MASK_AT + 2)
HALF = USED // 2
CELLS = 2 * (HALF + USED)
REST = CELLS + 2 * LANE_TILES + 1
THIN = CELLS + 1
EDGE = 3


def whole_tiles(rows):
    return 8 * ((rows + 7) // 8)


MESSAGE = whole_tiles(REST_AT + EDGE * REST + 8 - EDGE)
THIN_MESSAGE = whole_tiles(EDGE * THIN + 8 - EDGE)

OWN, TWO, SIDE, STRIP = 8, 48, 64, 112
PADS = (0, 40, 56, 104)
TILES = tuple((OWN + 8 * k, k) for k in range(4)) + ((TWO, 4),) + tuple((SIDE + 8 * n, (n + 2) % 5) for n in range(5))


def box_tile(by, u):
    return u + 2 * (1 - by)


def lanes_of(tile):
    return pl.ds(128 * tile, 128)


def joined_mask(mask_ref):
    parts = [mask_ref[0, by, bz] for by in range(2) for bz in range(2)]
    return jnp.concatenate(parts, axis=1)


def height_of_lane():
    return lax.rem(lax.broadcasted_iota(jnp.int32, (8, 128), 1), 32)


def share(first, second):
    heights = height_of_lane()
    first_up, second_up = pltpu.roll(first, LEVELS, 1), pltpu.roll(second, LEVELS, 1)
    return jnp.where(heights < LEVELS, first, second_up), first_up, second_up


def unshare(common, first_rest, second_rest):
    heights = height_of_lane()
    first = jnp.where(heights < LEVELS, common, pltpu.roll(first_rest, 128 - LEVELS, 1))
    second = pltpu.roll(jnp.where(heights >= LEVELS, common, second_rest), 128 - LEVELS, 1)
    return first, second


def put_edges(out_ref, at, pieces, rightward):
    for n, tile in enumerate(pieces):
        tile = jnp.where(rightward == 1, pltpu.roll(tile, EDGE, 0), tile)
        out_ref[at + EDGE * n : at + EDGE * (n + 1)] = tile[:EDGE]


def cells(tile):
    low = height_of_lane() < 2
    pieces = []
    for by in range(2):
        common, rests = [], [None] * USED
        for u in range(HALF):
            both, rests[u], rests[u + HALF] = share(tile(by, 0, u), tile(by, 0, u + HALF))
            common.append(both)
        pieces += common + [jnp.where(low, rests[u], tile(by, 1, u)) for u in range(USED)]
    return pieces


def put_message(out_ref, leftward, prev_tile, perm_tile, stor_tile, mask_tile):
    low = height_of_lane() < 2
    def put_tile(n, tile):
        out_ref[8 * n : 8 * n + 8] = tile

    for by in range(2):
        for u in range(USED):
            common, first_up, second_up = share(prev_tile(0, by, 0, u), prev_tile(1, by, 0, u))
            at = 24 * (by * USED + u)
            out_ref[at : at + 8] = common
            out_ref[at + 8 : at + 16] = jnp.where(low, first_up, prev_tile(0, by, 1, u))
            out_ref[at + 16 : at + 24] = jnp.where(low, second_up, prev_tile(1, by, 1, u))
    for n in range(2):
        put_tile(MASK_AT + n, mask_tile(n))
    for t in range(LANE_TILES):
        put_tile(PERM_AT + t, perm_tile(1 - leftward, t))
        put_tile(STOR_AT + t, stor_tile(1 - leftward, t))
    pieces = cells(functools.partial(prev_tile, 2))
    pieces += [perm_tile(leftward, t) for t in range(LANE_TILES)]
    pieces += [stor_tile(leftward, t) for t in range(LANE_TILES)]
    pieces += [mask_tile(2)]
    put_edges(out_ref, REST_AT, pieces, 1 - leftward)
    tail = REST_AT + EDGE * REST
    out_ref[tail:MESSAGE] = jnp.zeros((MESSAGE - tail, 128), F32)


def eight(tile):
    return pl.ds(pl.multiple_of(8 * tile, 8), 8)


def put_thin(out_ref, leftward, prev_tile, mask_tile):
    edge = 3 - 3 * leftward
    pieces = cells(functools.partial(prev_tile, edge)) + [mask_tile(edge)]
    put_edges(out_ref, 0, pieces, 1 - leftward)
    tail = EDGE * THIN
    out_ref[tail:THIN_MESSAGE] = jnp.zeros((THIN_MESSAGE - tail, 128), F32)


def pack_kernel(
    perm_ref, stor_ref, mask_ref, prev_ref, far_ref, far2_ref, near2_ref, near_ref, perm, stor, mask, prev, mask_buf, sems
):
    odd = lax.rem(lax.axis_index("gx"), 2)
    copies = []
    for by in range(2):
        for bz in range(2):
            blk = 2 * by + bz
            lanes = pl.ds(128 * box_tile(by, 0), 128 * USED)
            copies.append((prev_ref.at[0, by, bz, :, lanes], prev.at[blk]))
            copies.append((mask_ref.at[0, by, bz], mask.at[blk]))
    copies += [(perm_ref, perm), (stor_ref, stor)]
    copies = [pltpu.make_async_copy(src, dst, sems.at[n]) for n, (src, dst) in enumerate(copies)]
    for copy in copies:
        copy.start()
    for copy in copies:
        copy.wait()
    mask_buf[...] = jnp.concatenate([mask[blk] for blk in range(BLOCKS)], axis=1).astype(F32)

    def prev_tile(tile, by, bz, u):
        return prev[2 * by + bz, eight(tile), lanes_of(u)]

    def mask_tile(tile):
        return mask_buf[eight(tile), lanes_of(0)]

    def message(out_ref, leftward):
        def tile_at(n):
            return jnp.where(leftward == 1, n, (2, 3, 1)[n])

        put_message(
            out_ref,
            leftward,
            lambda n, by, bz, u: prev_tile(tile_at(n), by, bz, u),
            lambda n, t: perm[eight(n), lanes_of(t)],
            lambda n, t: stor[eight(n), lanes_of(t)],
            lambda n: mask_tile(tile_at(n)),
        )

    message(far_ref, 1 - odd)
    put_thin(far2_ref, odd, prev_tile, mask_tile)
    put_thin(near2_ref, 1 - odd, prev_tile, mask_tile)
    message(near_ref, odd)


def main_kernel(
    perm_ref, stor_ref, mask_ref, prev_ref, near_ref, far_ref, far2_ref, near2_ref,
    basis_ref, coarse_ref,
    kbuf, cbuf, wbuf, gbuf, sup, pbuf, qbuf, own_mask, sums,
):
    here = lax.axis_index("gx")
    last = lax.axis_size("gx") - 1
    odd = lax.rem(here, 2) == 1
    rows = lax.broadcasted_iota(jnp.int32, (8, 128), 0)
    lanes = lax.broadcasted_iota(jnp.int32, (8, 128), 1)
    heights = lax.rem(lanes, 32)
    low_rows = rows < 4
    zero = jnp.zeros((8, 128), F32)

    def left_big(i):
        at = pl.ds(8 * i, 8)
        return jnp.where(odd, near_ref[at], far_ref[at])

    def right_big(i):
        at = pl.ds(8 * i, 8)
        return jnp.where(odd, far_ref[at], near_ref[at])

    def edges(ref, at, left):
        start = at - (8 - EDGE) if left else at
        tile = ref[max(start, 0) : max(start, 0) + 8]
        return pltpu.roll(tile, -start, 0) if start < 0 else tile

    def rest_tile(index):
        at = REST_AT + EDGE * index
        right = jnp.where(odd, edges(far_ref, at, False), edges(near_ref, at, False))
        left = jnp.where(odd, edges(near_ref, at, True), edges(far_ref, at, True))
        return jnp.where(low_rows, right, left)

    def thin_tile(index):
        at = EDGE * index
        right = jnp.where(odd, edges(far2_ref, at, False), edges(near2_ref, at, False))
        left = jnp.where(odd, edges(near2_ref, at, True), edges(far2_ref, at, True))
        return jnp.where(low_rows, right, left)

    for t in range(LANE_TILES):
        for buf, ref, bulk, rest in (
            (kbuf, perm_ref, PERM_AT, CELLS),
            (cbuf, stor_ref, STOR_AT, CELLS + LANE_TILES),
        ):
            buf[t, 0:8] = left_big(bulk + t)
            buf[t, 8:16] = ref[0:8, 128 * t : 128 * t + 128]
            buf[t, 16:24] = ref[8:16, 128 * t : 128 * t + 128]
            buf[t, 24:32] = right_big(bulk + t)
            buf[t, 32:40] = rest_tile(rest + t)

    own_mask[...] = joined_mask(mask_ref)
    block = lanes // 32
    inner = (heights >= 8) & (heights < 24)
    core_bits = jnp.where(inner, jnp.where(lax.rem(block, 2) == 0, 0xFFFF, 0xFFFF00), 0)
    own_bits = [own_mask[8 * k : 8 * k + 8] for k in range(4)]
    own_bits[0] = jnp.where(here == 0, 0, own_bits[0])
    own_bits[1] |= core_bits
    own_bits[2] |= core_bits
    own_bits[3] = jnp.where(here == last, 0, own_bits[3])
    two_bits = thin_tile(THIN - 1).astype(jnp.int32)
    side_bits = [
        right_big(MASK_AT).astype(jnp.int32),
        right_big(MASK_AT + 1).astype(jnp.int32) | core_bits,
        rest_tile(REST - 1).astype(jnp.int32) | core_bits,
        left_big(MASK_AT).astype(jnp.int32) | core_bits,
        left_big(MASK_AT + 1).astype(jnp.int32),
    ]

    lane_bits = []
    for bz in range(2):
        offset = heights - 8 * bz
        valid = (offset >= 0) & (offset < (18, 24)[bz])
        lane_bits.append(jnp.where(valid, jnp.left_shift(1, jnp.clip(offset, 0, 23)), 0))

    def support_of(tile, by, bz, u):
        index = 32 * (2 * by + bz) + 4 * u + 8 * (1 - by) + lanes // 32
        spread = jnp.take_along_axis(tile, index, axis=1, mode="promise_in_bounds")
        return jnp.where((spread & lane_bits[bz]) != 0, 1.0, 0.0)

    side = [{} for _ in range(5)]
    two = {}
    for by in range(2):
        for u in range(USED):
            at = 3 * (by * USED + u)
            for side_tile, first in ((right_big, 0), (left_big, 3)):
                common, first_top, second_top = [side_tile(at + n) for n in range(3)]
                low, high = unshare(common, first_top, second_top)
                side[first][by, 0, u], side[first + 1][by, 0, u] = low, high
                side[first][by, 1, u], side[first + 1][by, 1, u] = first_top, second_top
        base = by * (HALF + USED)
        for fetch, cells_of in ((rest_tile, side[2]), (thin_tile, two)):
            for u in range(HALF):
                tops = [fetch(base + HALF + u), fetch(base + HALF + u + HALF)]
                low, high = unshare(fetch(base + u), *tops)
                cells_of[by, 0, u], cells_of[by, 0, u + HALF] = low, high
                cells_of[by, 1, u], cells_of[by, 1, u + HALF] = tops

    for by in range(2):
        for bz in range(2):
            for u in range(USED):
                for row in PADS:
                    pbuf[by, bz, u, row : row + 8] = zero

                def put(row, tile, bits):
                    s = support_of(bits, by, bz, u)
                    sup[by, bz, u, row : row + 8] = s
                    pbuf[by, bz, u, row : row + 8] = s * tile

                for k in range(4):
                    at = 128 * box_tile(by, u)
                    put(OWN + 8 * k, prev_ref[0, by, bz, 8 * k : 8 * k + 8, at : at + 128], own_bits[k])
                put(TWO, two[by, bz, u], two_bits)
                for n in range(5):
                    put(SIDE + 8 * n, side[n][by, bz, u], side_bits[n])

    def up_y(here_, next_):
        return pltpu.roll(jnp.where(lanes >= 32, here_, next_), 96, 1)

    def down_y(here_, before):
        return pltpu.roll(jnp.where(lanes < 96, here_, before), 32, 1)

    def up_z(v):
        return pltpu.roll(v, 127, 1)

    def down_z(v):
        return pltpu.roll(v, 1, 1)

    def inverse(v):
        first = pl.reciprocal(v, approx=True)
        return first * (2.0 - v * first)

    def harmonic(a, b):
        return 2.0 * (a * b) * inverse(jnp.maximum(a + b, TINY))

    def edge_k(t, i):
        return kbuf[t, 8 * i : 8 * i + 8] if 0 <= t < LANE_TILES else zero

    for t in range(LANE_TILES):
        k = [edge_k(t, i) for i in range(5)]
        ups = [pltpu.roll(v, 7, 0) for v in k]
        downs = [pltpu.roll(v, 1, 0) for v in k]
        for i in range(5):
            faces = [
                harmonic(k[i], jnp.where(rows < 7, ups[i], ups[(i + 1) % 5])),
                harmonic(k[i], jnp.where(rows > 0, downs[i], downs[i - 1])),
                harmonic(k[i], up_y(k[i], edge_k(t + 1, i))),
                harmonic(k[i], down_y(k[i], edge_k(t - 1, i))),
                jnp.where(heights < 31, harmonic(k[i], up_z(k[i])), 0.0),
                jnp.where(heights > 0, harmonic(k[i], down_z(k[i])), 0.0),
            ]
            diag = functools.reduce(lambda a, b: a + b, faces, cbuf[t, 8 * i : 8 * i + 8])
            scale = (2.0 / 3.0) * inverse(jnp.maximum(diag, TINY))
            for d, face in enumerate(faces):
                wbuf[t, d, 8 * i : 8 * i + 8] = face * scale
            gbuf[t, 8 * i : 8 * i + 8] = 1.5 * diag

    def weights_of(t):
        return [[wbuf[t, d, 8 * i : 8 * i + 8] for d in range(6)] for i in range(5)]

    def tile_of(by, bz, u, row):
        if 0 <= u < USED:
            return pbuf[by, bz, u, row : row + 8]
        return zero

    def stencil(by, bz, u, row, v, w):
        near = w[0] * pbuf[by, bz, u, row + 1 : row + 9] + w[1] * pbuf[by, bz, u, row - 1 : row + 7]
        near += w[2] * up_y(v, tile_of(by, bz, u + 1, row)) + w[3] * down_y(v, tile_of(by, bz, u - 1, row))
        return near + (w[4] * up_z(v) + w[5] * down_z(v))

    def relax(by, carry):
        for u in range(USED):
            weights = weights_of(u + 2 * by)
            for bz in range(2):
                for row, i in TILES:
                    v = tile_of(by, bz, u, row)
                    near = stencil(by, bz, u, row, v, weights[i])
                    s = sup[by, bz, u, row : row + 8]
                    qbuf[by, bz, u, row : row + 8] = s * jnp.maximum(v * (1.0 / 3.0) + near, 0.0)
        return carry

    def normalise(final):
        for t in range(LANE_TILES):
            blocks = [(by, bz, t - 2 * by) for by in range(2) for bz in range(2) if 0 <= t - 2 * by < USED]
            for i in range(5):
                at = [(b, row) for b in blocks for row, ring in TILES if ring == i]
                kept = [qbuf[by, bz, u, row : row + 8] for (by, bz, u), row in at]
                total = functools.reduce(lambda a, b: a + b, kept)
                scale = inverse(jnp.maximum(total, SUM_FLOOR))
                for ((by, bz, u), row), v in zip(at, kept):
                    v = v * scale
                    pbuf[by, bz, u, row : row + 8] = v
                    if final and row < TWO:
                        lane = 128 * box_tile(by, u)
                        basis_ref[0, by, bz, row - OWN : row - OWN + 8, lane : lane + 128] = v

    for sweep in range(ITERS):
        lax.fori_loop(0, 2, relax, 0)
        normalise(sweep == ITERS - 1)

    for by in range(2):
        for bz in range(2):
            at = 0 if by == 0 else 768
            basis_ref[0, by, bz, :, at : at + 256] = jnp.zeros((32, 256), F32)

    for by in range(2):
        acc = [[] for _ in range(24)]
        for t in range(by, by + USED + 1):
            u = t - 2 * by
            weights = weights_of(t)
            scale = [gbuf[t, 8 * i : 8 * i + 8] for i in range(5)]
            images = []
            for bz in range(2):
                image = []
                for k in range(4):
                    row = OWN + 8 * k
                    if 0 <= u < USED:
                        v = tile_of(by, bz, u, row)
                        image.append(scale[k] * (v * (2.0 / 3.0) - stencil(by, bz, u, row, v, weights[k])))
                    elif u < 0:
                        image.append(-scale[k] * (weights[k][2] * up_y(zero, tile_of(by, bz, u + 1, row))))
                    else:
                        image.append(-scale[k] * (weights[k][3] * down_y(zero, tile_of(by, bz, u - 1, row))))
                before = beyond = None
                if 0 <= u < USED:
                    edge = pbuf[by, bz, u, OWN + 31 : OWN + 39]
                    beyond = -scale[4] * (weights[4][1] * edge)
                    edge = pbuf[by, bz, u, OWN - 7 : OWN + 1]
                    before = -scale[4] * (weights[4][0] * edge)
                images.append((image, before, beyond))
            for partner in range(BLOCKS):
                by2, bz2 = divmod(partner, 2)
                u2 = t - 2 * by2
                if not 0 <= u2 < USED:
                    continue
                own = [tile_of(by2, bz2, u2, OWN + 8 * k) for k in range(4)]
                side = [tile_of(by2, bz2, u2, SIDE + 8 * k) for k in range(5)]
                for bz in range(2):
                    image, before, beyond = images[bz]
                    at = bz * 12 + partner
                    acc[at] += [image[0] * side[3], image[1] * side[4]]
                    acc[at + 4] += [image[k] * own[k] for k in range(4)]
                    acc[at + 8] += [image[2] * side[0], image[3] * side[1]]
                    if before is not None:
                        acc[at] += [before * side[2]]
                        acc[at + 8] += [beyond * side[2]]
            acc = [[functools.reduce(lambda a, b: a + b, terms)] if terms else [] for terms in acc]
        for bz in range(2):
            for n in range(12):
                sums[2 * by + bz, n] = jnp.sum(acc[bz * 12 + n][0], axis=0)

    entry = lax.broadcasted_iota(jnp.int32, (16, 128), 0)
    column = lax.broadcasted_iota(jnp.int32, (16, 128), 1)
    for by in range(2):
        for bz in range(2):
            values = jnp.sum(sums[2 * by + bz], axis=1, keepdims=True)
            target = 9 * (entry // 4) + 3 * (lax.rem(entry // 2, 2) - by + 1) + (lax.rem(entry, 2) - bz + 1)
            placed = jnp.where((column == target) & (entry < 12), values, 0.0)
            coarse_ref[0, by, bz, :] = jnp.sum(placed, axis=0)[:27]


def shards(permeability, storage, support_mask, prev_basis):
    vmem = pl.BlockSpec(memory_space=pltpu.VMEM)
    arguments = (permeability, storage, support_mask, prev_basis)
    far, far2, near2, near = pl.pallas_call(
        pack_kernel,
        in_specs=[pl.BlockSpec(memory_space=pl.ANY)] * 4,
        out_specs=[vmem] * 4,
        out_shape=[pltpu.VMEM((n, 128), F32) for n in (MESSAGE, THIN_MESSAGE, THIN_MESSAGE, MESSAGE)],
        scratch_shapes=[
            pltpu.VMEM(permeability.shape, F32),
            pltpu.VMEM(storage.shape, F32),
            pltpu.VMEM((BLOCKS, 32, 32), jnp.int32),
            pltpu.VMEM((BLOCKS, 32, 128 * USED), F32),
            pltpu.VMEM((32, 128), F32),
            pltpu.SemaphoreType.DMA((2 * BLOCKS + 2,)),
        ],
        name="pack",
    )(*arguments)
    size = lax.axis_size("gx")

    def move(x, step_even, step_odd):
        pairs = [(i, i + (step_odd if i % 2 else step_even)) for i in range(size)]
        return lax.ppermute(x, "gx", [(i, j) for i, j in pairs if 0 <= j < size])

    far = move(far, -1, 1)
    far2 = move(far2, 2, -2)
    near2 = move(near2, -2, 2)
    near = move(near, 1, -1)

    strips = (2, 2, USED, STRIP, 128)
    return pl.pallas_call(
        main_kernel,
        in_specs=[vmem] * 8,
        out_specs=[vmem] * 2,
        out_shape=[
            jax.ShapeDtypeStruct(prev_basis.shape, F32),
            jax.ShapeDtypeStruct((*prev_basis.shape[:3], 27), F32),
        ],
        scratch_shapes=[
            pltpu.VMEM((LANE_TILES, 40, 128), F32),
            pltpu.VMEM((LANE_TILES, 40, 128), F32),
            pltpu.VMEM((LANE_TILES, 6, 40, 128), F32),
            pltpu.VMEM((LANE_TILES, 40, 128), F32),
            pltpu.VMEM(strips, F32),
            pltpu.VMEM(strips, F32),
            pltpu.VMEM(strips, F32),
            pltpu.VMEM((32, 128), jnp.int32),
            pltpu.VMEM((4, 16, 128), F32),
        ],
        compiler_params=pltpu.CompilerParams(vmem_limit_bytes=32 * 1024 * 1024),
        name="smooth",
    )(*arguments, near, far, far2, near2)


def solution(mesh):
    placed = (
        P(("groups", "gx"), None),
        P(("groups", "gx"), None),
        P(("groups", "gx"), None, None, None, None),
        P(("groups", "gx"), None, None, None, None),
    )
    return jax.shard_map(
        shards,
        mesh=mesh,
        in_specs=placed,
        out_specs=(
            P(("groups", "gx"), None, None, None, None),
            P(("groups", "gx"), None, None, None),
        ),
        check_vma=False,
    )
```

```python
import functools

import jax
import jax.numpy as jnp
from jax import lax
from jax.experimental import pallas as pl
from jax.experimental.pallas import tpu as pltpu
from jax.sharding import PartitionSpec as P

ITERS = 2
SUM_FLOOR = 0.5
TINY = 1e-30
F32 = jnp.float32


BLOCKS = 4
LANE_TILES = 8
USED = 6

LEVELS = 16
BULK = 2 * USED * 3
PERM_AT = BULK
STOR_AT = PERM_AT + LANE_TILES
MASK_AT = STOR_AT + LANE_TILES
REST_AT = 8 * (MASK_AT + 2)
HALF = USED // 2
CELLS = 2 * (HALF + USED)
REST = CELLS + 2 * LANE_TILES + 1
THIN = CELLS + 1
EDGE = 3


def whole_tiles(rows):
    return 8 * ((rows + 7) // 8)


MESSAGE = whole_tiles(REST_AT + EDGE * REST + 8 - EDGE)
THIN_MESSAGE = whole_tiles(EDGE * THIN + 8 - EDGE)

OWN, TWO, SIDE, STRIP = 8, 48, 64, 112
PADS = (0, 40, 56, 104)
TILES = tuple((OWN + 8 * k, k) for k in range(4)) + ((TWO, 4),) + tuple((SIDE + 8 * n, (n + 2) % 5) for n in range(5))


def box_tile(by, u):
    return u + 2 * (1 - by)


def lanes_of(tile):
    return pl.ds(128 * tile, 128)


def joined_mask(mask_ref):
    parts = [mask_ref[0, by, bz] for by in range(2) for bz in range(2)]
    return jnp.concatenate(parts, axis=1)


def height_of_lane():
    return lax.rem(lax.broadcasted_iota(jnp.int32, (8, 128), 1), 32)


def share(first, second):
    heights = height_of_lane()
    first_up, second_up = pltpu.roll(first, LEVELS, 1), pltpu.roll(second, LEVELS, 1)
    return jnp.where(heights < LEVELS, first, second_up), first_up, second_up


def unshare(common, first_rest, second_rest):
    heights = height_of_lane()
    first = jnp.where(heights < LEVELS, common, pltpu.roll(first_rest, 128 - LEVELS, 1))
    second = pltpu.roll(jnp.where(heights >= LEVELS, common, second_rest), 128 - LEVELS, 1)
    return first, second


def put_edges(out_ref, at, pieces, rightward):
    for n, tile in enumerate(pieces):
        tile = jnp.where(rightward == 1, pltpu.roll(tile, EDGE, 0), tile)
        out_ref[at + EDGE * n : at + EDGE * (n + 1)] = tile[:EDGE]


def cells(tile):
    low = height_of_lane() < 2
    pieces = []
    for by in range(2):
        common, rests = [], [None] * USED
        for u in range(HALF):
            both, rests[u], rests[u + HALF] = share(tile(by, 0, u), tile(by, 0, u + HALF))
            common.append(both)
        pieces += common + [jnp.where(low, rests[u], tile(by, 1, u)) for u in range(USED)]
    return pieces


def put_message(out_ref, leftward, prev_tile, perm_tile, stor_tile, mask_tile):
    low = height_of_lane() < 2
    def put_tile(n, tile):
        out_ref[8 * n : 8 * n + 8] = tile

    for by in range(2):
        for u in range(USED):
            common, first_up, second_up = share(prev_tile(0, by, 0, u), prev_tile(1, by, 0, u))
            at = 24 * (by * USED + u)
            out_ref[at : at + 8] = common
            out_ref[at + 8 : at + 16] = jnp.where(low, first_up, prev_tile(0, by, 1, u))
            out_ref[at + 16 : at + 24] = jnp.where(low, second_up, prev_tile(1, by, 1, u))
    for n in range(2):
        put_tile(MASK_AT + n, mask_tile(n))
    for t in range(LANE_TILES):
        put_tile(PERM_AT + t, perm_tile(1 - leftward, t))
        put_tile(STOR_AT + t, stor_tile(1 - leftward, t))
    pieces = cells(functools.partial(prev_tile, 2))
    pieces += [perm_tile(leftward, t) for t in range(LANE_TILES)]
    pieces += [stor_tile(leftward, t) for t in range(LANE_TILES)]
    pieces += [mask_tile(2)]
    put_edges(out_ref, REST_AT, pieces, 1 - leftward)
    tail = REST_AT + EDGE * REST
    out_ref[tail:MESSAGE] = jnp.zeros((MESSAGE - tail, 128), F32)


def eight(tile):
    return pl.ds(pl.multiple_of(8 * tile, 8), 8)


def put_thin(out_ref, leftward, prev_tile, mask_tile):
    edge = 3 - 3 * leftward
    pieces = cells(functools.partial(prev_tile, edge)) + [mask_tile(edge)]
    put_edges(out_ref, 0, pieces, 1 - leftward)
    tail = EDGE * THIN
    out_ref[tail:THIN_MESSAGE] = jnp.zeros((THIN_MESSAGE - tail, 128), F32)


def pack_kernel(
    perm_ref, stor_ref, mask_ref, prev_ref, far_ref, far2_ref, near2_ref, near_ref, perm, stor, mask, prev, mask_buf, sems
):
    odd = lax.rem(lax.axis_index("gx"), 2)
    odd_chip = lax.rem(lax.axis_index("gx") // 2, 2)
    copies = []
    for by in range(2):
        for bz in range(2):
            blk = 2 * by + bz
            lanes = pl.ds(128 * box_tile(by, 0), 128 * USED)
            copies.append((prev_ref.at[0, by, bz, :, lanes], prev.at[blk]))
            copies.append((mask_ref.at[0, by, bz], mask.at[blk]))
    copies += [(perm_ref, perm), (stor_ref, stor)]
    copies = [pltpu.make_async_copy(src, dst, sems.at[n]) for n, (src, dst) in enumerate(copies)]
    for copy in copies:
        copy.start()
    for copy in copies:
        copy.wait()
    mask_buf[...] = jnp.concatenate([mask[blk] for blk in range(BLOCKS)], axis=1).astype(F32)

    def prev_tile(tile, by, bz, u):
        return prev[2 * by + bz, eight(tile), lanes_of(u)]

    def mask_tile(tile):
        return mask_buf[eight(tile), lanes_of(0)]

    def message(out_ref, leftward):
        def tile_at(n):
            return jnp.where(leftward == 1, n, (2, 3, 1)[n])

        put_message(
            out_ref,
            leftward,
            lambda n, by, bz, u: prev_tile(tile_at(n), by, bz, u),
            lambda n, t: perm[eight(n), lanes_of(t)],
            lambda n, t: stor[eight(n), lanes_of(t)],
            lambda n: mask_tile(tile_at(n)),
        )

    message(far_ref, 1 - odd)
    put_thin(far2_ref, odd_chip, prev_tile, mask_tile)
    put_thin(near2_ref, 1 - odd_chip, prev_tile, mask_tile)
    message(near_ref, odd)


def main_kernel(
    perm_ref, stor_ref, mask_ref, prev_ref, far_ref, far2_ref, near2_ref, near_ref,
    basis_ref, coarse_ref,
    kbuf, cbuf, wbuf, gbuf, sup, pbuf, qbuf, own_mask, sums,
):
    here = lax.axis_index("gx")
    last = lax.axis_size("gx") - 1
    odd = lax.rem(here, 2) == 1
    odd_chip = lax.rem(here // 2, 2) == 1
    rows = lax.broadcasted_iota(jnp.int32, (8, 128), 0)
    lanes = lax.broadcasted_iota(jnp.int32, (8, 128), 1)
    heights = lax.rem(lanes, 32)
    low_rows = rows < 4
    zero = jnp.zeros((8, 128), F32)

    def left_big(i):
        at = pl.ds(8 * i, 8)
        return jnp.where(odd, near_ref[at], far_ref[at])

    def right_big(i):
        at = pl.ds(8 * i, 8)
        return jnp.where(odd, far_ref[at], near_ref[at])

    def edges(ref, at, left):
        start = at - (8 - EDGE) if left else at
        tile = ref[max(start, 0) : max(start, 0) + 8]
        return pltpu.roll(tile, -start, 0) if start < 0 else tile

    def rest_tile(index):
        at = REST_AT + EDGE * index
        right = jnp.where(odd, edges(far_ref, at, False), edges(near_ref, at, False))
        left = jnp.where(odd, edges(near_ref, at, True), edges(far_ref, at, True))
        return jnp.where(low_rows, right, left)

    def thin_tile(index):
        at = EDGE * index
        right = jnp.where(odd_chip, edges(near2_ref, at, False), edges(far2_ref, at, False))
        left = jnp.where(odd_chip, edges(far2_ref, at, True), edges(near2_ref, at, True))
        return jnp.where(low_rows, right, left)

    for t in range(LANE_TILES):
        for buf, ref, bulk, rest in (
            (kbuf, perm_ref, PERM_AT, CELLS),
            (cbuf, stor_ref, STOR_AT, CELLS + LANE_TILES),
        ):
            buf[t, 0:8] = left_big(bulk + t)
            buf[t, 8:16] = ref[0:8, 128 * t : 128 * t + 128]
            buf[t, 16:24] = ref[8:16, 128 * t : 128 * t + 128]
            buf[t, 24:32] = right_big(bulk + t)
            buf[t, 32:40] = rest_tile(rest + t)

    own_mask[...] = joined_mask(mask_ref)
    block = lanes // 32
    inner = (heights >= 8) & (heights < 24)
    core_bits = jnp.where(inner, jnp.where(lax.rem(block, 2) == 0, 0xFFFF, 0xFFFF00), 0)
    own_bits = [own_mask[8 * k : 8 * k + 8] for k in range(4)]
    own_bits[0] = jnp.where(here == 0, 0, own_bits[0])
    own_bits[1] |= core_bits
    own_bits[2] |= core_bits
    own_bits[3] = jnp.where(here == last, 0, own_bits[3])
    two_bits = thin_tile(THIN - 1).astype(jnp.int32)
    side_bits = [
        right_big(MASK_AT).astype(jnp.int32),
        right_big(MASK_AT + 1).astype(jnp.int32) | core_bits,
        rest_tile(REST - 1).astype(jnp.int32) | core_bits,
        left_big(MASK_AT).astype(jnp.int32) | core_bits,
        left_big(MASK_AT + 1).astype(jnp.int32),
    ]

    lane_bits = []
    for bz in range(2):
        offset = heights - 8 * bz
        valid = (offset >= 0) & (offset < (18, 24)[bz])
        lane_bits.append(jnp.where(valid, jnp.left_shift(1, jnp.clip(offset, 0, 23)), 0))

    def support_of(tile, by, bz, u):
        index = 32 * (2 * by + bz) + 4 * u + 8 * (1 - by) + lanes // 32
        spread = jnp.take_along_axis(tile, index, axis=1, mode="promise_in_bounds")
        return jnp.where((spread & lane_bits[bz]) != 0, 1.0, 0.0)

    side = [{} for _ in range(5)]
    two = {}
    for by in range(2):
        for u in range(USED):
            at = 3 * (by * USED + u)
            for side_tile, first in ((right_big, 0), (left_big, 3)):
                common, first_top, second_top = [side_tile(at + n) for n in range(3)]
                low, high = unshare(common, first_top, second_top)
                side[first][by, 0, u], side[first + 1][by, 0, u] = low, high
                side[first][by, 1, u], side[first + 1][by, 1, u] = first_top, second_top
        base = by * (HALF + USED)
        for fetch, cells_of in ((rest_tile, side[2]), (thin_tile, two)):
            for u in range(HALF):
                tops = [fetch(base + HALF + u), fetch(base + HALF + u + HALF)]
                low, high = unshare(fetch(base + u), *tops)
                cells_of[by, 0, u], cells_of[by, 0, u + HALF] = low, high
                cells_of[by, 1, u], cells_of[by, 1, u + HALF] = tops

    for by in range(2):
        for bz in range(2):
            for u in range(USED):
                for row in PADS:
                    pbuf[by, bz, u, row : row + 8] = zero

                def put(row, tile, bits):
                    s = support_of(bits, by, bz, u)
                    sup[by, bz, u, row : row + 8] = s
                    pbuf[by, bz, u, row : row + 8] = s * tile

                for k in range(4):
                    at = 128 * box_tile(by, u)
                    put(OWN + 8 * k, prev_ref[0, by, bz, 8 * k : 8 * k + 8, at : at + 128], own_bits[k])
                put(TWO, two[by, bz, u], two_bits)
                for n in range(5):
                    put(SIDE + 8 * n, side[n][by, bz, u], side_bits[n])

    def up_y(here_, next_):
        return pltpu.roll(jnp.where(lanes >= 32, here_, next_), 96, 1)

    def down_y(here_, before):
        return pltpu.roll(jnp.where(lanes < 96, here_, before), 32, 1)

    def up_z(v):
        return pltpu.roll(v, 127, 1)

    def down_z(v):
        return pltpu.roll(v, 1, 1)

    def inverse(v):
        first = pl.reciprocal(v, approx=True)
        return first * (2.0 - v * first)

    def harmonic(a, b):
        return 2.0 * (a * b) * inverse(jnp.maximum(a + b, TINY))

    def edge_k(t, i):
        return kbuf[t, 8 * i : 8 * i + 8] if 0 <= t < LANE_TILES else zero

    for t in range(LANE_TILES):
        k = [edge_k(t, i) for i in range(5)]
        ups = [pltpu.roll(v, 7, 0) for v in k]
        downs = [pltpu.roll(v, 1, 0) for v in k]
        for i in range(5):
            faces = [
                harmonic(k[i], jnp.where(rows < 7, ups[i], ups[(i + 1) % 5])),
                harmonic(k[i], jnp.where(rows > 0, downs[i], downs[i - 1])),
                harmonic(k[i], up_y(k[i], edge_k(t + 1, i))),
                harmonic(k[i], down_y(k[i], edge_k(t - 1, i))),
                jnp.where(heights < 31, harmonic(k[i], up_z(k[i])), 0.0),
                jnp.where(heights > 0, harmonic(k[i], down_z(k[i])), 0.0),
            ]
            diag = functools.reduce(lambda a, b: a + b, faces, cbuf[t, 8 * i : 8 * i + 8])
            scale = (2.0 / 3.0) * inverse(jnp.maximum(diag, TINY))
            for d, face in enumerate(faces):
                wbuf[t, d, 8 * i : 8 * i + 8] = face * scale
            gbuf[t, 8 * i : 8 * i + 8] = 1.5 * diag

    def weights_of(t):
        return [[wbuf[t, d, 8 * i : 8 * i + 8] for d in range(6)] for i in range(5)]

    def tile_of(by, bz, u, row):
        if 0 <= u < USED:
            return pbuf[by, bz, u, row : row + 8]
        return zero

    def stencil(by, bz, u, row, v, w):
        near = w[0] * pbuf[by, bz, u, row + 1 : row + 9] + w[1] * pbuf[by, bz, u, row - 1 : row + 7]
        near += w[2] * up_y(v, tile_of(by, bz, u + 1, row)) + w[3] * down_y(v, tile_of(by, bz, u - 1, row))
        return near + (w[4] * up_z(v) + w[5] * down_z(v))

    def relax(by, carry):
        for u in range(USED):
            weights = weights_of(u + 2 * by)
            for bz in range(2):
                for row, i in TILES:
                    v = tile_of(by, bz, u, row)
                    near = stencil(by, bz, u, row, v, weights[i])
                    s = sup[by, bz, u, row : row + 8]
                    qbuf[by, bz, u, row : row + 8] = s * jnp.maximum(v * (1.0 / 3.0) + near, 0.0)
        return carry

    def normalise(final):
        for t in range(LANE_TILES):
            blocks = [(by, bz, t - 2 * by) for by in range(2) for bz in range(2) if 0 <= t - 2 * by < USED]
            for i in range(5):
                at = [(b, row) for b in blocks for row, ring in TILES if ring == i]
                kept = [qbuf[by, bz, u, row : row + 8] for (by, bz, u), row in at]
                total = functools.reduce(lambda a, b: a + b, kept)
                scale = inverse(jnp.maximum(total, SUM_FLOOR))
                for ((by, bz, u), row), v in zip(at, kept):
                    v = v * scale
                    pbuf[by, bz, u, row : row + 8] = v
                    if final and row < TWO:
                        lane = 128 * box_tile(by, u)
                        basis_ref[0, by, bz, row - OWN : row - OWN + 8, lane : lane + 128] = v

    for sweep in range(ITERS):
        lax.fori_loop(0, 2, relax, 0)
        normalise(sweep == ITERS - 1)

    for by in range(2):
        for bz in range(2):
            at = 0 if by == 0 else 768
            basis_ref[0, by, bz, :, at : at + 256] = jnp.zeros((32, 256), F32)

    for by in range(2):
        acc = [[] for _ in range(24)]
        for t in range(by, by + USED + 1):
            u = t - 2 * by
            weights = weights_of(t)
            scale = [gbuf[t, 8 * i : 8 * i + 8] for i in range(5)]
            images = []
            for bz in range(2):
                image = []
                for k in range(4):
                    row = OWN + 8 * k
                    if 0 <= u < USED:
                        v = tile_of(by, bz, u, row)
                        image.append(scale[k] * (v * (2.0 / 3.0) - stencil(by, bz, u, row, v, weights[k])))
                    elif u < 0:
                        image.append(-scale[k] * (weights[k][2] * up_y(zero, tile_of(by, bz, u + 1, row))))
                    else:
                        image.append(-scale[k] * (weights[k][3] * down_y(zero, tile_of(by, bz, u - 1, row))))
                before = beyond = None
                if 0 <= u < USED:
                    edge = pbuf[by, bz, u, OWN + 31 : OWN + 39]
                    beyond = -scale[4] * (weights[4][1] * edge)
                    edge = pbuf[by, bz, u, OWN - 7 : OWN + 1]
                    before = -scale[4] * (weights[4][0] * edge)
                images.append((image, before, beyond))
            for partner in range(BLOCKS):
                by2, bz2 = divmod(partner, 2)
                u2 = t - 2 * by2
                if not 0 <= u2 < USED:
                    continue
                own = [tile_of(by2, bz2, u2, OWN + 8 * k) for k in range(4)]
                side = [tile_of(by2, bz2, u2, SIDE + 8 * k) for k in range(5)]
                for bz in range(2):
                    image, before, beyond = images[bz]
                    at = bz * 12 + partner
                    acc[at] += [image[0] * side[3], image[1] * side[4]]
                    acc[at + 4] += [image[k] * own[k] for k in range(4)]
                    acc[at + 8] += [image[2] * side[0], image[3] * side[1]]
                    if before is not None:
                        acc[at] += [before * side[2]]
                        acc[at + 8] += [beyond * side[2]]
            acc = [[functools.reduce(lambda a, b: a + b, terms)] if terms else [] for terms in acc]
        for bz in range(2):
            for n in range(12):
                sums[2 * by + bz, n] = jnp.sum(acc[bz * 12 + n][0], axis=0)

    entry = lax.broadcasted_iota(jnp.int32, (16, 128), 0)
    column = lax.broadcasted_iota(jnp.int32, (16, 128), 1)
    for by in range(2):
        for bz in range(2):
            values = jnp.sum(sums[2 * by + bz], axis=1, keepdims=True)
            target = 9 * (entry // 4) + 3 * (lax.rem(entry // 2, 2) - by + 1) + (lax.rem(entry, 2) - bz + 1)
            placed = jnp.where((column == target) & (entry < 12), values, 0.0)
            coarse_ref[0, by, bz, :] = jnp.sum(placed, axis=0)[:27]


def shards(permeability, storage, support_mask, prev_basis):
    vmem = pl.BlockSpec(memory_space=pltpu.VMEM)
    arguments = (permeability, storage, support_mask, prev_basis)
    far, far2, near2, near = pl.pallas_call(
        pack_kernel,
        in_specs=[pl.BlockSpec(memory_space=pl.ANY)] * 4,
        out_specs=[vmem] * 4,
        out_shape=[pltpu.VMEM((n, 128), F32) for n in (MESSAGE, THIN_MESSAGE, THIN_MESSAGE, MESSAGE)],
        scratch_shapes=[
            pltpu.VMEM(permeability.shape, F32),
            pltpu.VMEM(storage.shape, F32),
            pltpu.VMEM((BLOCKS, 32, 32), jnp.int32),
            pltpu.VMEM((BLOCKS, 32, 128 * USED), F32),
            pltpu.VMEM((32, 128), F32),
            pltpu.SemaphoreType.DMA((2 * BLOCKS + 2,)),
        ],
        name="pack",
    )(*arguments)
    size = lax.axis_size("gx")

    def move(x, step, width):
        pairs = [(i, i + (-step if i // width % 2 else step)) for i in range(size)]
        return lax.ppermute(x, "gx", [(i, j) for i, j in pairs if 0 <= j < size])

    far = move(far, -1, 1)
    far2 = move(far2, 2, 2)
    near2 = move(near2, -2, 2)
    near = move(near, 1, 1)

    strips = (2, 2, USED, STRIP, 128)
    return pl.pallas_call(
        main_kernel,
        in_specs=[vmem] * 8,
        out_specs=[vmem] * 2,
        out_shape=[
            jax.ShapeDtypeStruct(prev_basis.shape, F32),
            jax.ShapeDtypeStruct((*prev_basis.shape[:3], 27), F32),
        ],
        scratch_shapes=[
            pltpu.VMEM((LANE_TILES, 40, 128), F32),
            pltpu.VMEM((LANE_TILES, 40, 128), F32),
            pltpu.VMEM((LANE_TILES, 6, 40, 128), F32),
            pltpu.VMEM((LANE_TILES, 40, 128), F32),
            pltpu.VMEM(strips, F32),
            pltpu.VMEM(strips, F32),
            pltpu.VMEM(strips, F32),
            pltpu.VMEM((32, 128), jnp.int32),
            pltpu.VMEM((4, 16, 128), F32),
        ],
        compiler_params=pltpu.CompilerParams(vmem_limit_bytes=32 * 1024 * 1024),
        name="smooth",
    )(*arguments, far, far2, near2, near)


def solution(mesh):
    placed = (
        P(("groups", "gx"), None),
        P(("groups", "gx"), None),
        P(("groups", "gx"), None, None, None, None),
        P(("groups", "gx"), None, None, None, None),
    )
    return jax.shard_map(
        shards,
        mesh=mesh,
        in_specs=placed,
        out_specs=(
            P(("groups", "gx"), None, None, None, None),
            P(("groups", "gx"), None, None, None),
        ),
        check_vma=False,
    )
```

```python
import functools

import jax
import jax.numpy as jnp
from jax import lax
from jax.experimental import pallas as pl
from jax.experimental.pallas import tpu as pltpu
from jax.sharding import PartitionSpec as P

ITERS = 2
SUM_FLOOR = 0.5
TINY = 1e-30
F32 = jnp.float32


BLOCKS = 4
LANE_TILES = 8
USED = 6

LEVELS = 16
BULK = 2 * USED * 3
PERM_AT = BULK
STOR_AT = PERM_AT + LANE_TILES
MASK_AT = STOR_AT + LANE_TILES
REST_AT = 8 * (MASK_AT + 2)
HALF = USED // 2
CELLS = 2 * (HALF + USED)
REST = CELLS + 2 * LANE_TILES + 1
THIN = CELLS + 1
EDGE = 3


def whole_tiles(rows):
    return 8 * ((rows + 7) // 8)


MESSAGE = whole_tiles(REST_AT + EDGE * REST + 8 - EDGE)
THIN_MESSAGE = whole_tiles(EDGE * THIN + 8 - EDGE)

OWN, TWO, SIDE, STRIP = 8, 48, 64, 112
SPAN = 96
PADS = (0, 40, 56, 104)
TILES = tuple((OWN + 8 * k, k) for k in range(4)) + ((TWO, 4),) + tuple((SIDE + 8 * n, (n + 2) % 5) for n in range(5))


def box_tile(by, u):
    return u + 2 * (1 - by)


def lanes_of(tile):
    return pl.ds(128 * tile, 128)


def joined_mask(mask_ref):
    parts = [mask_ref[0, by, bz] for by in range(2) for bz in range(2)]
    return jnp.concatenate(parts, axis=1)


def height_of_lane():
    return lax.rem(lax.broadcasted_iota(jnp.int32, (8, 128), 1), 32)


def share(first, second):
    heights = height_of_lane()
    first_up, second_up = pltpu.roll(first, LEVELS, 1), pltpu.roll(second, LEVELS, 1)
    return jnp.where(heights < LEVELS, first, second_up), first_up, second_up


def unshare(common, first_rest, second_rest):
    heights = height_of_lane()
    first = jnp.where(heights < LEVELS, common, pltpu.roll(first_rest, 128 - LEVELS, 1))
    second = pltpu.roll(jnp.where(heights >= LEVELS, common, second_rest), 128 - LEVELS, 1)
    return first, second


def put_edges(out_ref, at, pieces, rightward):
    for n, tile in enumerate(pieces):
        tile = jnp.where(rightward == 1, pltpu.roll(tile, EDGE, 0), tile)
        out_ref[at + EDGE * n : at + EDGE * (n + 1)] = tile[:EDGE]


def cells(tile):
    low = height_of_lane() < 2
    pieces = []
    for by in range(2):
        common, rests = [], [None] * USED
        for u in range(HALF):
            both, rests[u], rests[u + HALF] = share(tile(by, 0, u), tile(by, 0, u + HALF))
            common.append(both)
        pieces += common + [jnp.where(low, rests[u], tile(by, 1, u)) for u in range(USED)]
    return pieces


def put_message(out_ref, leftward, prev_tile, perm_tile, stor_tile, mask_tile):
    low = height_of_lane() < 2
    def put_tile(n, tile):
        out_ref[8 * n : 8 * n + 8] = tile

    for by in range(2):
        for u in range(USED):
            common, first_up, second_up = share(prev_tile(0, by, 0, u), prev_tile(1, by, 0, u))
            at = 24 * (by * USED + u)
            out_ref[at : at + 8] = common
            out_ref[at + 8 : at + 16] = jnp.where(low, first_up, prev_tile(0, by, 1, u))
            out_ref[at + 16 : at + 24] = jnp.where(low, second_up, prev_tile(1, by, 1, u))
    for n in range(2):
        put_tile(MASK_AT + n, mask_tile(n))
    for t in range(LANE_TILES):
        put_tile(PERM_AT + t, perm_tile(1 - leftward, t))
        put_tile(STOR_AT + t, stor_tile(1 - leftward, t))
    pieces = cells(functools.partial(prev_tile, 2))
    pieces += [perm_tile(leftward, t) for t in range(LANE_TILES)]
    pieces += [stor_tile(leftward, t) for t in range(LANE_TILES)]
    pieces += [mask_tile(2)]
    put_edges(out_ref, REST_AT, pieces, 1 - leftward)
    tail = REST_AT + EDGE * REST
    out_ref[tail:MESSAGE] = jnp.zeros((MESSAGE - tail, 128), F32)


def eight(tile):
    return pl.ds(pl.multiple_of(8 * tile, 8), 8)


def put_thin(out_ref, leftward, prev_tile, mask_tile):
    edge = 3 - 3 * leftward
    pieces = cells(functools.partial(prev_tile, edge)) + [mask_tile(edge)]
    put_edges(out_ref, 0, pieces, 1 - leftward)
    tail = EDGE * THIN
    out_ref[tail:THIN_MESSAGE] = jnp.zeros((THIN_MESSAGE - tail, 128), F32)


def pack_kernel(
    perm_ref, stor_ref, mask_ref, prev_ref, far_ref, far2_ref, near2_ref, near_ref, perm, stor, mask, prev, mask_buf, sems
):
    odd = lax.rem(lax.axis_index("gx"), 2)
    odd_chip = lax.rem(lax.axis_index("gx") // 2, 2)
    copies = []
    for by in range(2):
        for bz in range(2):
            blk = 2 * by + bz
            lanes = pl.ds(128 * box_tile(by, 0), 128 * USED)
            copies.append((prev_ref.at[0, by, bz, :, lanes], prev.at[blk]))
            copies.append((mask_ref.at[0, by, bz], mask.at[blk]))
    copies += [(perm_ref, perm), (stor_ref, stor)]
    copies = [pltpu.make_async_copy(src, dst, sems.at[n]) for n, (src, dst) in enumerate(copies)]
    for copy in copies:
        copy.start()
    for copy in copies:
        copy.wait()
    mask_buf[...] = jnp.concatenate([mask[blk] for blk in range(BLOCKS)], axis=1).astype(F32)

    def prev_tile(tile, by, bz, u):
        return prev[2 * by + bz, eight(tile), lanes_of(u)]

    def mask_tile(tile):
        return mask_buf[eight(tile), lanes_of(0)]

    def message(out_ref, leftward):
        def tile_at(n):
            return jnp.where(leftward == 1, n, (2, 3, 1)[n])

        put_message(
            out_ref,
            leftward,
            lambda n, by, bz, u: prev_tile(tile_at(n), by, bz, u),
            lambda n, t: perm[eight(n), lanes_of(t)],
            lambda n, t: stor[eight(n), lanes_of(t)],
            lambda n: mask_tile(tile_at(n)),
        )

    message(far_ref, 1 - odd)
    put_thin(far2_ref, odd_chip, prev_tile, mask_tile)
    put_thin(near2_ref, 1 - odd_chip, prev_tile, mask_tile)
    message(near_ref, odd)


def main_kernel(
    perm_ref, stor_ref, mask_ref, prev_ref, far_ref, far2_ref, near2_ref, near_ref,
    basis_ref, coarse_ref,
    kbuf, cbuf, wbuf, gbuf, sup, pbuf, qbuf, own_mask, sums, zbuf, shift,
):
    here = lax.axis_index("gx")
    last = lax.axis_size("gx") - 1
    odd = lax.rem(here, 2) == 1
    odd_chip = lax.rem(here // 2, 2) == 1
    rows = lax.broadcasted_iota(jnp.int32, (8, 128), 0)
    lanes = lax.broadcasted_iota(jnp.int32, (8, 128), 1)
    heights = lax.rem(lanes, 32)
    low_rows = rows < 4
    zero = jnp.zeros((8, 128), F32)

    def left_big(i):
        at = pl.ds(8 * i, 8)
        return jnp.where(odd, near_ref[at], far_ref[at])

    def right_big(i):
        at = pl.ds(8 * i, 8)
        return jnp.where(odd, far_ref[at], near_ref[at])

    def edges(ref, at, left):
        start = at - (8 - EDGE) if left else at
        tile = ref[max(start, 0) : max(start, 0) + 8]
        return pltpu.roll(tile, -start, 0) if start < 0 else tile

    def rest_tile(index):
        at = REST_AT + EDGE * index
        right = jnp.where(odd, edges(far_ref, at, False), edges(near_ref, at, False))
        left = jnp.where(odd, edges(near_ref, at, True), edges(far_ref, at, True))
        return jnp.where(low_rows, right, left)

    def thin_tile(index):
        at = EDGE * index
        right = jnp.where(odd_chip, edges(near2_ref, at, False), edges(far2_ref, at, False))
        left = jnp.where(odd_chip, edges(far2_ref, at, True), edges(near2_ref, at, True))
        return jnp.where(low_rows, right, left)

    for t in range(LANE_TILES):
        for buf, ref, bulk, rest in (
            (kbuf, perm_ref, PERM_AT, CELLS),
            (cbuf, stor_ref, STOR_AT, CELLS + LANE_TILES),
        ):
            buf[t, 0:8] = left_big(bulk + t)
            buf[t, 8:16] = ref[0:8, 128 * t : 128 * t + 128]
            buf[t, 16:24] = ref[8:16, 128 * t : 128 * t + 128]
            buf[t, 24:32] = right_big(bulk + t)
            buf[t, 32:40] = rest_tile(rest + t)

    own_mask[...] = joined_mask(mask_ref)
    block = lanes // 32
    inner = (heights >= 8) & (heights < 24)
    core_bits = jnp.where(inner, jnp.where(lax.rem(block, 2) == 0, 0xFFFF, 0xFFFF00), 0)
    own_bits = [own_mask[8 * k : 8 * k + 8] for k in range(4)]
    own_bits[0] = jnp.where(here == 0, 0, own_bits[0])
    own_bits[1] |= core_bits
    own_bits[2] |= core_bits
    own_bits[3] = jnp.where(here == last, 0, own_bits[3])
    two_bits = thin_tile(THIN - 1).astype(jnp.int32)
    side_bits = [
        right_big(MASK_AT).astype(jnp.int32),
        right_big(MASK_AT + 1).astype(jnp.int32) | core_bits,
        rest_tile(REST - 1).astype(jnp.int32) | core_bits,
        left_big(MASK_AT).astype(jnp.int32) | core_bits,
        left_big(MASK_AT + 1).astype(jnp.int32),
    ]

    lane_bits = []
    for bz in range(2):
        offset = heights - 8 * bz
        valid = (offset >= 0) & (offset < (18, 24)[bz])
        lane_bits.append(jnp.where(valid, jnp.left_shift(1, jnp.clip(offset, 0, 23)), 0))

    def support_of(tile, by, bz, u):
        index = 32 * (2 * by + bz) + 4 * u + 8 * (1 - by) + lanes // 32
        spread = jnp.take_along_axis(tile, index, axis=1, mode="promise_in_bounds")
        return jnp.where((spread & lane_bits[bz]) != 0, 1.0, 0.0)

    side = [{} for _ in range(5)]
    two = {}
    for by in range(2):
        for u in range(USED):
            at = 3 * (by * USED + u)
            for side_tile, first in ((right_big, 0), (left_big, 3)):
                common, first_top, second_top = [side_tile(at + n) for n in range(3)]
                low, high = unshare(common, first_top, second_top)
                side[first][by, 0, u], side[first + 1][by, 0, u] = low, high
                side[first][by, 1, u], side[first + 1][by, 1, u] = first_top, second_top
        base = by * (HALF + USED)
        for fetch, cells_of in ((rest_tile, side[2]), (thin_tile, two)):
            for u in range(HALF):
                tops = [fetch(base + HALF + u), fetch(base + HALF + u + HALF)]
                low, high = unshare(fetch(base + u), *tops)
                cells_of[by, 0, u], cells_of[by, 0, u + HALF] = low, high
                cells_of[by, 1, u], cells_of[by, 1, u + HALF] = tops

    for by in range(2):
        for bz in range(2):
            for u in range(USED):
                for row in PADS:
                    pbuf[by, bz, u, row : row + 8] = zero

                def put(row, tile, bits):
                    s = support_of(bits, by, bz, u)
                    sup[by, bz, u, row : row + 8] = s
                    pbuf[by, bz, u, row : row + 8] = s * tile

                for k in range(4):
                    at = 128 * box_tile(by, u)
                    put(OWN + 8 * k, prev_ref[0, by, bz, 8 * k : 8 * k + 8, at : at + 128], own_bits[k])
                put(TWO, two[by, bz, u], two_bits)
                for n in range(5):
                    put(SIDE + 8 * n, side[n][by, bz, u], side_bits[n])

    def up_y(here_, next_):
        return pltpu.roll(jnp.where(lanes >= 32, here_, next_), 96, 1)

    def down_y(here_, before):
        return pltpu.roll(jnp.where(lanes < 96, here_, before), 32, 1)

    def up_z(v):
        return pltpu.roll(v, 127, 1)

    def down_z(v):
        return pltpu.roll(v, 1, 1)

    def inverse(v):
        first = pl.reciprocal(v, approx=True)
        return first * (2.0 - v * first)

    def harmonic(a, b):
        return 2.0 * (a * b) * inverse(jnp.maximum(a + b, TINY))

    def edge_k(t, i):
        return kbuf[t, 8 * i : 8 * i + 8] if 0 <= t < LANE_TILES else zero

    for t in range(LANE_TILES):
        k = [edge_k(t, i) for i in range(5)]
        ups = [pltpu.roll(v, 7, 0) for v in k]
        downs = [pltpu.roll(v, 1, 0) for v in k]
        for i in range(5):
            faces = [
                harmonic(k[i], jnp.where(rows < 7, ups[i], ups[(i + 1) % 5])),
                harmonic(k[i], jnp.where(rows > 0, downs[i], downs[i - 1])),
                harmonic(k[i], up_y(k[i], edge_k(t + 1, i))),
                harmonic(k[i], down_y(k[i], edge_k(t - 1, i))),
                jnp.where(heights < 31, harmonic(k[i], up_z(k[i])), 0.0),
                jnp.where(heights > 0, harmonic(k[i], down_z(k[i])), 0.0),
            ]
            diag = functools.reduce(lambda a, b: a + b, faces, cbuf[t, 8 * i : 8 * i + 8])
            scale = (2.0 / 3.0) * inverse(jnp.maximum(diag, TINY))
            for d, face in enumerate(faces):
                wbuf[t, d, 8 * i : 8 * i + 8] = face * scale
            gbuf[t, 8 * i : 8 * i + 8] = 1.5 * diag

    def weights_of(t):
        return [[wbuf[t, d, 8 * i : 8 * i + 8] for d in range(6)] for i in range(5)]

    def tile_of(by, bz, u, row):
        if 0 <= u < USED:
            return pbuf[by, bz, u, row : row + 8]
        return zero

    def stencil(by, bz, u, row, v, w, beside_z=None):
        upper, lower = beside_z or (up_z(v), down_z(v))
        near = w[0] * pbuf[by, bz, u, row + 1 : row + 9] + w[1] * pbuf[by, bz, u, row - 1 : row + 7]
        near += w[2] * up_y(v, tile_of(by, bz, u + 1, row)) + w[3] * down_y(v, tile_of(by, bz, u - 1, row))
        return near + (w[4] * upper + w[5] * lower)

    deep = lax.broadcasted_iota(jnp.int32, (256, 256), 0) % 128
    wide = lax.broadcasted_iota(jnp.int32, (256, 256), 1)
    source = jnp.where(wide < 128, wide + 1, wide - 129)
    shift[...] = jnp.where(deep == source, 1.0, 0.0).astype(jnp.bfloat16)

    def relax(by, carry):
        v = pbuf[by, :, :, OWN : OWN + SPAN].reshape(2 * USED * SPAN, 128)
        high = v.astype(jnp.bfloat16)
        low = (v - high.astype(F32)).astype(jnp.bfloat16)
        parts = jnp.concatenate([high, low], axis=1)
        zbuf[...] = jnp.dot(parts, shift[...], preferred_element_type=F32).reshape(2, USED, SPAN, 256)
        for u in range(USED):
            weights = weights_of(u + 2 * by)
            for bz in range(2):
                for row, i in TILES:
                    v = tile_of(by, bz, u, row)
                    at = slice(row - OWN, row - OWN + 8)
                    beside_z = zbuf[bz, u, at, 0:128], zbuf[bz, u, at, 128:256]
                    near = stencil(by, bz, u, row, v, weights[i], beside_z)
                    s = sup[by, bz, u, row : row + 8]
                    qbuf[by, bz, u, row : row + 8] = s * jnp.maximum(v * (1.0 / 3.0) + near, 0.0)
        return carry

    def normalise(final):
        for t in range(LANE_TILES):
            blocks = [(by, bz, t - 2 * by) for by in range(2) for bz in range(2) if 0 <= t - 2 * by < USED]
            for i in range(5):
                at = [(b, row) for b in blocks for row, ring in TILES if ring == i]
                kept = [qbuf[by, bz, u, row : row + 8] for (by, bz, u), row in at]
                total = functools.reduce(lambda a, b: a + b, kept)
                scale = inverse(jnp.maximum(total, SUM_FLOOR))
                for ((by, bz, u), row), v in zip(at, kept):
                    v = v * scale
                    pbuf[by, bz, u, row : row + 8] = v
                    if final and row < TWO:
                        lane = 128 * box_tile(by, u)
                        basis_ref[0, by, bz, row - OWN : row - OWN + 8, lane : lane + 128] = v

    for sweep in range(ITERS):
        for by in range(2):
            relax(by, 0)
        normalise(sweep == ITERS - 1)

    for by in range(2):
        for bz in range(2):
            at = 0 if by == 0 else 768
            basis_ref[0, by, bz, :, at : at + 256] = jnp.zeros((32, 256), F32)

    for by in range(2):
        acc = [[] for _ in range(24)]
        for t in range(by, by + USED + 1):
            u = t - 2 * by
            weights = weights_of(t)
            scale = [gbuf[t, 8 * i : 8 * i + 8] for i in range(5)]
            images = []
            for bz in range(2):
                image = []
                for k in range(4):
                    row = OWN + 8 * k
                    if 0 <= u < USED:
                        v = tile_of(by, bz, u, row)
                        image.append(scale[k] * (v * (2.0 / 3.0) - stencil(by, bz, u, row, v, weights[k])))
                    elif u < 0:
                        image.append(-scale[k] * (weights[k][2] * up_y(zero, tile_of(by, bz, u + 1, row))))
                    else:
                        image.append(-scale[k] * (weights[k][3] * down_y(zero, tile_of(by, bz, u - 1, row))))
                before = beyond = None
                if 0 <= u < USED:
                    edge = pbuf[by, bz, u, OWN + 31 : OWN + 39]
                    beyond = -scale[4] * (weights[4][1] * edge)
                    edge = pbuf[by, bz, u, OWN - 7 : OWN + 1]
                    before = -scale[4] * (weights[4][0] * edge)
                images.append((image, before, beyond))
            for partner in range(BLOCKS):
                by2, bz2 = divmod(partner, 2)
                u2 = t - 2 * by2
                if not 0 <= u2 < USED:
                    continue
                own = [tile_of(by2, bz2, u2, OWN + 8 * k) for k in range(4)]
                side = [tile_of(by2, bz2, u2, SIDE + 8 * k) for k in range(5)]
                for bz in range(2):
                    image, before, beyond = images[bz]
                    at = bz * 12 + partner
                    acc[at] += [image[0] * side[3], image[1] * side[4]]
                    acc[at + 4] += [image[k] * own[k] for k in range(4)]
                    acc[at + 8] += [image[2] * side[0], image[3] * side[1]]
                    if before is not None:
                        acc[at] += [before * side[2]]
                        acc[at + 8] += [beyond * side[2]]
            acc = [[functools.reduce(lambda a, b: a + b, terms)] if terms else [] for terms in acc]
        for bz in range(2):
            for n in range(12):
                sums[2 * by + bz, n] = jnp.sum(acc[bz * 12 + n][0], axis=0)

    entry = lax.broadcasted_iota(jnp.int32, (16, 128), 0)
    column = lax.broadcasted_iota(jnp.int32, (16, 128), 1)
    for by in range(2):
        for bz in range(2):
            values = jnp.sum(sums[2 * by + bz], axis=1, keepdims=True)
            target = 9 * (entry // 4) + 3 * (lax.rem(entry // 2, 2) - by + 1) + (lax.rem(entry, 2) - bz + 1)
            placed = jnp.where((column == target) & (entry < 12), values, 0.0)
            coarse_ref[0, by, bz, :] = jnp.sum(placed, axis=0)[:27]


def shards(permeability, storage, support_mask, prev_basis):
    vmem = pl.BlockSpec(memory_space=pltpu.VMEM)
    arguments = (permeability, storage, support_mask, prev_basis)
    far, far2, near2, near = pl.pallas_call(
        pack_kernel,
        in_specs=[pl.BlockSpec(memory_space=pl.ANY)] * 4,
        out_specs=[vmem] * 4,
        out_shape=[pltpu.VMEM((n, 128), F32) for n in (MESSAGE, THIN_MESSAGE, THIN_MESSAGE, MESSAGE)],
        scratch_shapes=[
            pltpu.VMEM(permeability.shape, F32),
            pltpu.VMEM(storage.shape, F32),
            pltpu.VMEM((BLOCKS, 32, 32), jnp.int32),
            pltpu.VMEM((BLOCKS, 32, 128 * USED), F32),
            pltpu.VMEM((32, 128), F32),
            pltpu.SemaphoreType.DMA((2 * BLOCKS + 2,)),
        ],
        name="pack",
    )(*arguments)
    size = lax.axis_size("gx")

    def move(x, step, width):
        pairs = [(i, i + (-step if i // width % 2 else step)) for i in range(size)]
        return lax.ppermute(x, "gx", [(i, j) for i, j in pairs if 0 <= j < size])

    far = move(far, -1, 1)
    far2 = move(far2, 2, 2)
    near2 = move(near2, -2, 2)
    near = move(near, 1, 1)

    strips = (2, 2, USED, STRIP, 128)
    return pl.pallas_call(
        main_kernel,
        in_specs=[vmem] * 8,
        out_specs=[vmem] * 2,
        out_shape=[
            jax.ShapeDtypeStruct(prev_basis.shape, F32),
            jax.ShapeDtypeStruct((*prev_basis.shape[:3], 27), F32),
        ],
        scratch_shapes=[
            pltpu.VMEM((LANE_TILES, 40, 128), F32),
            pltpu.VMEM((LANE_TILES, 40, 128), F32),
            pltpu.VMEM((LANE_TILES, 6, 40, 128), F32),
            pltpu.VMEM((LANE_TILES, 40, 128), F32),
            pltpu.VMEM(strips, F32),
            pltpu.VMEM(strips, F32),
            pltpu.VMEM(strips, F32),
            pltpu.VMEM((32, 128), jnp.int32),
            pltpu.VMEM((4, 16, 128), F32),
            pltpu.VMEM((2, USED, SPAN, 256), F32),
            pltpu.VMEM((256, 256), jnp.bfloat16),
        ],
        compiler_params=pltpu.CompilerParams(vmem_limit_bytes=32 * 1024 * 1024),
        name="smooth",
    )(*arguments, far, far2, near2, near)


def solution(mesh):
    placed = (
        P(("groups", "gx"), None),
        P(("groups", "gx"), None),
        P(("groups", "gx"), None, None, None, None),
        P(("groups", "gx"), None, None, None, None),
    )
    return jax.shard_map(
        shards,
        mesh=mesh,
        in_specs=placed,
        out_specs=(
            P(("groups", "gx"), None, None, None, None),
            P(("groups", "gx"), None, None, None),
        ),
        check_vma=False,
    )
```

```python
import functools

import jax
import jax.numpy as jnp
from jax import lax
from jax.experimental import pallas as pl
from jax.experimental.pallas import tpu as pltpu
from jax.sharding import PartitionSpec as P

ITERS = 2
SUM_FLOOR = 0.5
TINY = 1e-30
F32 = jnp.float32


BLOCKS = 4
LANE_TILES = 8
USED = 6

LEVELS = 16
BULK = 2 * USED * 3
PERM_AT = BULK
STOR_AT = PERM_AT + LANE_TILES
MASK_AT = STOR_AT + LANE_TILES
REST_AT = 8 * (MASK_AT + 2)
HALF = USED // 2
CELLS = 2 * (HALF + USED)
REST = CELLS + 2 * LANE_TILES + 1
THIN = CELLS + 1
EDGE = 3


def whole_tiles(rows):
    return 8 * ((rows + 7) // 8)


MESSAGE = whole_tiles(REST_AT + EDGE * REST + 8 - EDGE)
THIN_MESSAGE = whole_tiles(EDGE * THIN + 8 - EDGE)

OWN, TWO, SIDE, STRIP = 8, 48, 64, 112
SPAN = 96
PADS = (0, 40, 56, 104)
TILES = tuple((OWN + 8 * k, k) for k in range(4)) + ((TWO, 4),) + tuple((SIDE + 8 * n, (n + 2) % 5) for n in range(5))


def box_tile(by, u):
    return u + 2 * (1 - by)


def lanes_of(tile):
    return pl.ds(128 * tile, 128)


def height_of_lane():
    return lax.rem(lax.broadcasted_iota(jnp.int32, (8, 128), 1), 32)


def share(first, second):
    heights = height_of_lane()
    first_up, second_up = pltpu.roll(first, LEVELS, 1), pltpu.roll(second, LEVELS, 1)
    return jnp.where(heights < LEVELS, first, second_up), first_up, second_up


def unshare(common, first_rest, second_rest):
    heights = height_of_lane()
    first = jnp.where(heights < LEVELS, common, pltpu.roll(first_rest, 128 - LEVELS, 1))
    second = pltpu.roll(jnp.where(heights >= LEVELS, common, second_rest), 128 - LEVELS, 1)
    return first, second


def put_edges(out_ref, at, pieces, rightward):
    for n, tile in enumerate(pieces):
        tile = jnp.where(rightward == 1, pltpu.roll(tile, EDGE, 0), tile)
        out_ref[at + EDGE * n : at + EDGE * (n + 1)] = tile[:EDGE]


def cells(tile):
    low = height_of_lane() < 2
    pieces = []
    for by in range(2):
        common, rests = [], [None] * USED
        for u in range(HALF):
            both, rests[u], rests[u + HALF] = share(tile(by, 0, u), tile(by, 0, u + HALF))
            common.append(both)
        pieces += common + [jnp.where(low, rests[u], tile(by, 1, u)) for u in range(USED)]
    return pieces


def put_message(out_ref, rest_ref, rest_at, leftward, prev_tile, perm_tile, stor_tile, mask_tile):
    low = height_of_lane() < 2
    def put_tile(n, tile):
        out_ref[8 * n : 8 * n + 8] = tile

    for by in range(2):
        for u in range(USED):
            common, first_up, second_up = share(prev_tile(0, by, 0, u), prev_tile(1, by, 0, u))
            at = 24 * (by * USED + u)
            out_ref[at : at + 8] = common
            out_ref[at + 8 : at + 16] = jnp.where(low, first_up, prev_tile(0, by, 1, u))
            out_ref[at + 16 : at + 24] = jnp.where(low, second_up, prev_tile(1, by, 1, u))
    for n in range(2):
        put_tile(MASK_AT + n, mask_tile(n))
    for t in range(LANE_TILES):
        put_tile(PERM_AT + t, perm_tile(1 - leftward, t))
        put_tile(STOR_AT + t, stor_tile(1 - leftward, t))
    pieces = cells(functools.partial(prev_tile, 2))
    pieces += [perm_tile(leftward, t) for t in range(LANE_TILES)]
    pieces += [stor_tile(leftward, t) for t in range(LANE_TILES)]
    pieces += [mask_tile(2)]
    put_edges(rest_ref, rest_at, pieces, 1 - leftward)
    tail, end = rest_at + EDGE * REST, rest_at + MESSAGE - REST_AT
    rest_ref[tail:end] = jnp.zeros((end - tail, 128), F32)


def eight(tile):
    return pl.ds(pl.multiple_of(8 * tile, 8), 8)


def put_thin(out_ref, leftward, prev_tile, mask_tile):
    edge = 3 - 3 * leftward
    pieces = cells(functools.partial(prev_tile, edge)) + [mask_tile(edge)]
    put_edges(out_ref, 0, pieces, 1 - leftward)
    tail = EDGE * THIN
    out_ref[tail:THIN_MESSAGE] = jnp.zeros((THIN_MESSAGE - tail, 128), F32)


def pack_kernel(
    perm_ref, stor_ref, mask_ref, prev_ref,
    far_ref, far2_ref, near2_ref, near_ref, rest_ref, perm, stor, mask_buf, prev, mask, sems,
):
    odd = lax.rem(lax.axis_index("gx"), 2)
    odd_chip = lax.rem(lax.axis_index("gx") // 2, 2)
    copies = []
    for by in range(2):
        for bz in range(2):
            blk = 2 * by + bz
            lanes = pl.ds(128 * box_tile(by, 0), 128 * USED)
            copies.append((prev_ref.at[0, by, bz, :, lanes], prev.at[blk]))
            copies.append((mask_ref.at[0, by, bz], mask.at[blk]))
    copies += [(perm_ref, perm), (stor_ref, stor)]
    copies = [pltpu.make_async_copy(src, dst, sems.at[n]) for n, (src, dst) in enumerate(copies)]
    for copy in copies:
        copy.start()
    for copy in copies:
        copy.wait()
    mask_buf[...] = jnp.concatenate([mask[blk] for blk in range(BLOCKS)], axis=1).astype(F32)

    def prev_tile(tile, by, bz, u):
        return prev[2 * by + bz, eight(tile), lanes_of(u)]

    def mask_tile(tile):
        return mask_buf[eight(tile), lanes_of(0)]

    def message(out_ref, rest_ref, rest_at, leftward):
        def tile_at(n):
            return jnp.where(leftward == 1, n, (2, 3, 1)[n])

        put_message(
            out_ref,
            rest_ref,
            rest_at,
            leftward,
            lambda n, by, bz, u: prev_tile(tile_at(n), by, bz, u),
            lambda n, t: perm[eight(n), lanes_of(t)],
            lambda n, t: stor[eight(n), lanes_of(t)],
            lambda n: mask_tile(tile_at(n)),
        )

    message(far_ref, far_ref, REST_AT, 1 - odd)
    put_thin(far2_ref, odd_chip, prev_tile, mask_tile)
    put_thin(near2_ref, 1 - odd_chip, prev_tile, mask_tile)
    message(near_ref, rest_ref, 0, odd)


def tile_rows(n):
    return slice(8 * n, 8 * n + 8)


def lane_index():
    return lax.broadcasted_iota(jnp.int32, (8, 128), 1)


def zeros():
    return jnp.zeros((8, 128), F32)


def up_y(here, after):
    return pltpu.roll(jnp.where(lane_index() >= 32, here, after), 96, 1)


def down_y(here, before):
    return pltpu.roll(jnp.where(lane_index() < 96, here, before), 32, 1)


def up_z(v):
    return pltpu.roll(v, 127, 1)


def down_z(v):
    return pltpu.roll(v, 1, 1)


def inverse(v):
    first = pl.reciprocal(v, approx=True)
    return first * (2.0 - v * first)


def harmonic(a, b):
    return 2.0 * (a * b) * inverse(jnp.maximum(a + b, TINY))


def edges(ref, at, index, left):
    start = at + EDGE * index - (8 - EDGE) * left
    tile = ref[max(start, 0) : max(start, 0) + 8]
    return pltpu.roll(tile, -start, 0) if start < 0 else tile


def fill_coefficients(rings, buf, own_ref, bulk, rest, sides):
    low = lax.broadcasted_iota(jnp.int32, (8, 128), 0) < 4
    for t in range(LANE_TILES):
        for i in rings:
            if i in (1, 2):
                tile = own_ref[tile_rows(i - 1), lanes_of(t)]
            elif i < 4:
                tile = sides[i // 3][0][tile_rows(bulk + t)]
            else:
                ends = [edges(*ref[1:], rest + t, n == 0) if ref is not None else None for n, ref in enumerate(sides)]
                tile = ends[0] if ends[1] is None else ends[1] if ends[0] is None else jnp.where(low, ends[1], ends[0])
            buf[t, tile_rows(i)] = tile


def fill_weights(rings, kbuf, cbuf, wbuf, gbuf):
    rows = lax.broadcasted_iota(jnp.int32, (8, 128), 0)
    heights = height_of_lane()

    def k_of(t, i):
        return kbuf[t, tile_rows(i % 5)] if 0 <= t < LANE_TILES else zeros()

    for t in range(LANE_TILES):
        for i in rings:
            k = k_of(t, i)
            east = jnp.where(rows < 7, pltpu.roll(k, 7, 0), pltpu.roll(k_of(t, i + 1), 7, 0))
            west = jnp.where(rows > 0, pltpu.roll(k, 1, 0), pltpu.roll(k_of(t, i + 4), 1, 0))
            faces = [
                harmonic(k, east),
                harmonic(k, west),
                harmonic(k, up_y(k, k_of(t + 1, i))),
                harmonic(k, down_y(k, k_of(t - 1, i))),
                jnp.where(heights < 31, harmonic(k, up_z(k)), 0.0),
                jnp.where(heights > 0, harmonic(k, down_z(k)), 0.0),
            ]
            diag = functools.reduce(lambda a, b: a + b, faces, cbuf[t, tile_rows(i)])
            scale = (2.0 / 3.0) * inverse(jnp.maximum(diag, TINY))
            for d, face in enumerate(faces):
                wbuf[t, d, tile_rows(i)] = face * scale
            gbuf[t, tile_rows(i)] = 1.5 * diag


def core_bits():
    lanes = lane_index()
    j = lax.rem(lanes, 32)
    return jnp.where((j >= 8) & (j < 24), jnp.where(lax.rem(lanes // 32, 2) == 0, 0xFFFF, 0xFFFF00), 0)


def support_of(bits, by, bz, u):
    offset = height_of_lane() - 8 * bz
    valid = (offset >= 0) & (offset < (18, 24)[bz])
    lane_bit = jnp.where(valid, jnp.left_shift(1, jnp.clip(offset, 0, 23)), 0)
    index = 32 * (2 * by + bz) + 4 * u + 8 * (1 - by) + lane_index() // 32
    spread = jnp.take_along_axis(bits, index, axis=1, mode="promise_in_bounds")
    return jnp.where((spread & lane_bit) != 0, 1.0, 0.0)


def message_cells(ref):
    found = [{}, {}]
    for by in range(2):
        for u in range(USED):
            at = 3 * (by * USED + u)
            common, first_top, second_top = [ref[tile_rows(at + n)] for n in range(3)]
            found[0][by, 0, u], found[1][by, 0, u] = unshare(common, first_top, second_top)
            found[0][by, 1, u], found[1][by, 1, u] = first_top, second_top
    return found


def edge_cells(fetch):
    found = {}
    for by in range(2):
        base = by * (HALF + USED)
        for u in range(HALF):
            tops = [fetch(base + HALF + u), fetch(base + HALF + u + HALF)]
            found[by, 0, u], found[by, 0, u + HALF] = unshare(fetch(base + u), *tops)
            found[by, 1, u], found[by, 1, u + HALF] = tops
    return found


def put_cells(pbuf, sup, row, found, bits):
    for (by, bz, u), tile in found.items():
        s = support_of(bits, by, bz, u)
        sup[by, bz, u, row : row + 8] = s
        pbuf[by, bz, u, row : row + 8] = s * tile


def side_row(ring):
    return SIDE + 8 * ((ring - 2) % 5)


def tile_of(pbuf, by, bz, u, row):
    return pbuf[by, bz, u, row : row + 8] if 0 <= u < USED else zeros()


def stencil(pbuf, by, bz, u, row, v, w, beside_z=None):
    upper, lower = beside_z or (up_z(v), down_z(v))
    near = w[0] * pbuf[by, bz, u, row + 1 : row + 9] + w[1] * pbuf[by, bz, u, row - 1 : row + 7]
    near += w[2] * up_y(v, tile_of(pbuf, by, bz, u + 1, row)) + w[3] * down_y(v, tile_of(pbuf, by, bz, u - 1, row))
    return near + (w[4] * upper + w[5] * lower)


def relax(pbuf, qbuf, sup, wbuf, by, tiles, zbuf=None, shift=None, spans=()):
    if spans:
        count = sum(b - a for a, b in spans)
        v = jnp.concatenate([pbuf[by, :, :, a:b] for a, b in spans], axis=2).reshape(2 * USED * count, 128)
        high = v.astype(jnp.bfloat16)
        low = (v - high.astype(F32)).astype(jnp.bfloat16)
        parts = jnp.concatenate([high, low], axis=1)
        beside = jnp.dot(parts, shift[...], preferred_element_type=F32)
        zbuf[:, :, :count] = beside.reshape(2, USED, count, 256)
    places = {}
    for a, b in spans:
        for row in range(a, b, 8):
            places[row] = 8 * len(places)
    for u in range(USED):
        for bz in range(2):
            for row, i in tiles:
                v = tile_of(pbuf, by, bz, u, row)
                w = [wbuf[u + 2 * by, d, tile_rows(i)] for d in range(6)]
                beside_z = None
                if spans:
                    at = slice(places[row], places[row] + 8)
                    beside_z = zbuf[bz, u, at, 0:128], zbuf[bz, u, at, 128:256]
                near = stencil(pbuf, by, bz, u, row, v, w, beside_z)
                s = sup[by, bz, u, row : row + 8]
                qbuf[by, bz, u, row : row + 8] = s * jnp.maximum(v * (1.0 / 3.0) + near, 0.0)


def normalise(qbuf, pbuf, tiles, basis_ref=None):
    for t in range(LANE_TILES):
        blocks = [(by, bz, t - 2 * by) for by in range(2) for bz in range(2) if 0 <= t - 2 * by < USED]
        for i in sorted({ring for _, ring in tiles}):
            at = [(b, row) for b in blocks for row, ring in tiles if ring == i]
            kept = [qbuf[by, bz, u, row : row + 8] for (by, bz, u), row in at]
            total = functools.reduce(lambda a, b: a + b, kept)
            scale = inverse(jnp.maximum(total, SUM_FLOOR))
            for ((by, bz, u), row), v in zip(at, kept):
                v = v * scale
                pbuf[by, bz, u, row : row + 8] = v
                if basis_ref is not None and row < TWO:
                    basis_ref[0, by, bz, row - OWN : row - OWN + 8, lanes_of(box_tile(by, u))] = v


def halves(odd):
    return ((1, 0), (2, 3)) if odd else ((2, 3), (1, 0))


def by_parity(body):
    parity = lax.rem(lax.axis_index("gx"), 2)
    for odd in range(2):
        pl.when(parity == odd)(functools.partial(body, odd))


def begin_kernel(perm_ref, stor_ref, mask_ref, prev_ref, near_ref, rest_ref, first, second, sup, wbuf, gbuf, shift, kbuf, cbuf, qbuf):
    here = lax.axis_index("gx")
    last = lax.axis_size("gx") - 1
    deep = lax.broadcasted_iota(jnp.int32, (256, 256), 0) % 128
    wide = lax.broadcasted_iota(jnp.int32, (256, 256), 1)
    source = jnp.where(wide < 128, wide + 1, wide - 129)
    shift[...] = jnp.where(deep == source, 1.0, 0.0).astype(jnp.bfloat16)

    own_bits = [mask_ref[tile_rows(k)].astype(jnp.int32) for k in range(4)]
    own_bits[0] = jnp.where(here == 0, 0, own_bits[0])
    own_bits[1] |= core_bits()
    own_bits[2] |= core_bits()
    own_bits[3] = jnp.where(here == last, 0, own_bits[3])
    for by in range(2):
        for bz in range(2):
            for u in range(USED):
                for row in PADS:
                    first[by, bz, u, row : row + 8] = zeros()
                    second[by, bz, u, row : row + 8] = zeros()
    for k in range(4):
        found = {
            (by, bz, u): prev_ref[2 * by + bz, tile_rows(k), lanes_of(u)]
            for by in range(2)
            for bz in range(2)
            for u in range(USED)
        }
        put_cells(first, sup, OWN + 8 * k, found, own_bits[k])

    def body(odd):
        (inner, outer), _ = halves(odd)
        near = (near_ref, rest_ref, 0)
        sides = (near, None) if odd else (None, near)
        fill_coefficients((1, 2, outer, 4), kbuf, perm_ref, PERM_AT, CELLS, sides)
        fill_coefficients((inner, outer), cbuf, stor_ref, STOR_AT, CELLS + LANE_TILES, sides)
        fill_weights((inner, outer), kbuf, cbuf, wbuf, gbuf)
        found = message_cells(near_ref)
        for n in range(2):
            ring = n if odd else n + 2
            bits = near_ref[tile_rows(MASK_AT + n)].astype(jnp.int32)
            put_cells(first, sup, side_row(ring), found[n], bits | core_bits() if ring in (0, 3) else bits)

        def rest(index):
            return edges(rest_ref, 0, index, odd == 1)

        put_cells(first, sup, side_row(4), edge_cells(rest), rest(REST - 1).astype(jnp.int32) | core_bits())
        tiles = [(row, i) for row, i in TILES if i in (inner, outer)]
        for by in range(2):
            relax(first, qbuf, sup, wbuf, by, tiles)
        normalise(qbuf, second, tiles)

    by_parity(body)


def finish_kernel(
    far_ref, far2_ref, near2_ref, near_ref, rest_ref, perm_ref, stor_ref, shift, _first, _second, _sup, _wbuf, _gbuf,
    basis_ref, coarse_ref, first, second, sup, wbuf, gbuf,
    kbuf, cbuf, qbuf, sums, zbuf,
):
    here = lax.axis_index("gx")
    odd_chip = lax.rem(here // 2, 2) == 1
    rows = lax.broadcasted_iota(jnp.int32, (8, 128), 0)
    low_rows = rows < 4

    def thin(index):
        right = jnp.where(odd_chip, edges(near2_ref, 0, index, False), edges(far2_ref, 0, index, False))
        left = jnp.where(odd_chip, edges(far2_ref, 0, index, True), edges(near2_ref, 0, index, True))
        return jnp.where(low_rows, right, left)

    def body(odd):
        (_, near_outer), (inner, outer) = halves(odd)
        near, far = (near_ref, rest_ref, 0), (far_ref, far_ref, REST_AT)
        sides = (near, far) if odd else (far, near)
        fill_coefficients((1, 2, near_outer, outer, 4), kbuf, perm_ref, PERM_AT, CELLS, sides)
        fill_coefficients((inner, outer, 4), cbuf, stor_ref, STOR_AT, CELLS + LANE_TILES, sides)
        fill_weights((inner, outer, 4), kbuf, cbuf, wbuf, gbuf)
        found = message_cells(far_ref)
        for n in range(2):
            ring = n + 2 if odd else n
            bits = far_ref[tile_rows(MASK_AT + n)].astype(jnp.int32)
            put_cells(first, sup, side_row(ring), found[n], bits | core_bits() if ring in (0, 3) else bits)

        def rest(index):
            return jnp.where(low_rows, edges(*sides[1][1:], index, False), edges(*sides[0][1:], index, True))

        put_cells(first, sup, side_row(4), edge_cells(rest), rest(REST - 1).astype(jnp.int32) | core_bits())
        put_cells(first, sup, TWO, edge_cells(thin), thin(THIN - 1).astype(jnp.int32))
        tiles = [(row, i) for row, i in TILES if i in (inner, outer, 4)]
        own = OWN + 16 * odd
        side = SIDE + 16 * (1 - odd)
        spans = ((own, own + 16), (TWO, TWO + 8), (side, side + 24))
        for by in range(2):
            relax(first, qbuf, sup, wbuf, by, tiles, zbuf, shift, spans)
        normalise(qbuf, second, tiles)

    by_parity(body)

    pbuf, other = second, first
    for sweep in range(1, ITERS):
        for by in range(2):
            relax(pbuf, qbuf, sup, wbuf, by, TILES, zbuf, shift, ((OWN, OWN + SPAN),))
        normalise(qbuf, other, TILES, basis_ref if sweep == ITERS - 1 else None)
        pbuf, other = other, pbuf

    for by in range(2):
        for bz in range(2):
            at = 0 if by == 0 else 768
            basis_ref[0, by, bz, :, at : at + 256] = jnp.zeros((32, 256), F32)

    for by in range(2):
        acc = [[] for _ in range(24)]
        for t in range(by, by + USED + 1):
            u = t - 2 * by
            weights = [[wbuf[t, d, tile_rows(i)] for d in range(6)] for i in range(5)]
            scale = [gbuf[t, 8 * i : 8 * i + 8] for i in range(5)]
            images = []
            for bz in range(2):
                image = []
                for k in range(4):
                    row = OWN + 8 * k
                    if 0 <= u < USED:
                        v = tile_of(pbuf, by, bz, u, row)
                        image.append(scale[k] * (v * (2.0 / 3.0) - stencil(pbuf, by, bz, u, row, v, weights[k])))
                    elif u < 0:
                        image.append(-scale[k] * (weights[k][2] * up_y(zeros(), tile_of(pbuf, by, bz, u + 1, row))))
                    else:
                        image.append(-scale[k] * (weights[k][3] * down_y(zeros(), tile_of(pbuf, by, bz, u - 1, row))))
                before = beyond = None
                if 0 <= u < USED:
                    edge = pbuf[by, bz, u, OWN + 31 : OWN + 39]
                    beyond = -scale[4] * (weights[4][1] * edge)
                    edge = pbuf[by, bz, u, OWN - 7 : OWN + 1]
                    before = -scale[4] * (weights[4][0] * edge)
                images.append((image, before, beyond))
            for partner in range(BLOCKS):
                by2, bz2 = divmod(partner, 2)
                u2 = t - 2 * by2
                if not 0 <= u2 < USED:
                    continue
                own = [tile_of(pbuf, by2, bz2, u2, OWN + 8 * k) for k in range(4)]
                side = [tile_of(pbuf, by2, bz2, u2, SIDE + 8 * k) for k in range(5)]
                for bz in range(2):
                    image, before, beyond = images[bz]
                    at = bz * 12 + partner
                    acc[at] += [image[0] * side[3], image[1] * side[4]]
                    acc[at + 4] += [image[k] * own[k] for k in range(4)]
                    acc[at + 8] += [image[2] * side[0], image[3] * side[1]]
                    if before is not None:
                        acc[at] += [before * side[2]]
                        acc[at + 8] += [beyond * side[2]]
            acc = [[functools.reduce(lambda a, b: a + b, terms)] if terms else [] for terms in acc]
        for bz in range(2):
            for n in range(12):
                sums[2 * by + bz, n] = jnp.sum(acc[bz * 12 + n][0], axis=0)

    entry = lax.broadcasted_iota(jnp.int32, (16, 128), 0)
    column = lax.broadcasted_iota(jnp.int32, (16, 128), 1)
    for by in range(2):
        for bz in range(2):
            values = jnp.sum(sums[2 * by + bz], axis=1, keepdims=True)
            target = 9 * (entry // 4) + 3 * (lax.rem(entry // 2, 2) - by + 1) + (lax.rem(entry, 2) - bz + 1)
            placed = jnp.where((column == target) & (entry < 12), values, 0.0)
            coarse_ref[0, by, bz, :] = jnp.sum(placed, axis=0)[:27]


def shards(permeability, storage, support_mask, prev_basis):
    vmem = pl.BlockSpec(memory_space=pltpu.VMEM)
    far, far2, near2, near, rest, *own = pl.pallas_call(
        pack_kernel,
        in_specs=[pl.BlockSpec(memory_space=pl.ANY)] * 4,
        out_specs=[vmem] * 9,
        out_shape=[
            *[pltpu.VMEM((n, 128), F32) for n in (MESSAGE, THIN_MESSAGE, THIN_MESSAGE, REST_AT, MESSAGE - REST_AT)],
            pltpu.VMEM(permeability.shape, F32),
            pltpu.VMEM(storage.shape, F32),
            pltpu.VMEM((32, 128), F32),
            pltpu.VMEM((BLOCKS, 32, 128 * USED), F32),
        ],
        scratch_shapes=[
            pltpu.VMEM((BLOCKS, 32, 32), jnp.int32),
            pltpu.SemaphoreType.DMA((2 * BLOCKS + 2,)),
        ],
        name="pack",
    )(permeability, storage, support_mask, prev_basis)
    size = lax.axis_size("gx")

    def move(x, step, width):
        pairs = [(i, i + (-step if i // width % 2 else step)) for i in range(size)]
        return lax.ppermute(x, "gx", [(i, j) for i, j in pairs if 0 <= j < size])

    far = move(far, -1, 1)
    far2 = move(far2, 2, 2)
    near2 = move(near2, -2, 2)
    near = move(near, 1, 1)
    rest = move(rest, 1, 1)

    strips = (2, 2, USED, STRIP, 128)
    state = [
        pltpu.VMEM(strips, F32),
        pltpu.VMEM(strips, F32),
        pltpu.VMEM(strips, F32),
        pltpu.VMEM((LANE_TILES, 6, 40, 128), F32),
        pltpu.VMEM((LANE_TILES, 40, 128), F32),
    ]
    scratch = [
        pltpu.VMEM((LANE_TILES, 40, 128), F32),
        pltpu.VMEM((LANE_TILES, 40, 128), F32),
        pltpu.VMEM(strips, F32),
    ]
    limit = pltpu.CompilerParams(vmem_limit_bytes=32 * 1024 * 1024)
    *filled, shift = pl.pallas_call(
        begin_kernel,
        in_specs=[vmem] * 6,
        out_specs=[vmem] * 6,
        out_shape=[*state, pltpu.VMEM((256, 256), jnp.bfloat16)],
        scratch_shapes=scratch,
        compiler_params=limit,
        cost_estimate=pl.CostEstimate(flops=0, bytes_accessed=0, transcendentals=0),
        name="begin",
    )(*own, near, rest)
    return pl.pallas_call(
        finish_kernel,
        in_specs=[vmem] * 13,
        out_specs=[vmem] * 7,
        out_shape=[
            jax.ShapeDtypeStruct(prev_basis.shape, F32),
            jax.ShapeDtypeStruct((*prev_basis.shape[:3], 27), F32),
            *state,
        ],
        input_output_aliases={8 + n: 2 + n for n in range(5)},
        scratch_shapes=[
            *scratch,
            pltpu.VMEM((4, 16, 128), F32),
            pltpu.VMEM((2, USED, SPAN, 256), F32),
        ],
        compiler_params=limit,
        name="finish",
    )(far, far2, near2, near, rest, *own[:2], shift, *filled)[:2]


def solution(mesh):
    placed = (
        P(("groups", "gx"), None),
        P(("groups", "gx"), None),
        P(("groups", "gx"), None, None, None, None),
        P(("groups", "gx"), None, None, None, None),
    )
    return jax.shard_map(
        shards,
        mesh=mesh,
        in_specs=placed,
        out_specs=(
            P(("groups", "gx"), None, None, None, None),
            P(("groups", "gx"), None, None, None),
        ),
        check_vma=False,
    )
```

```python
import functools

import jax
import jax.numpy as jnp
from jax import lax
from jax.experimental import pallas as pl
from jax.experimental.pallas import tpu as pltpu
from jax.sharding import PartitionSpec as P

SUM_FLOOR = 0.5
TINY = 1e-30
F32 = jnp.float32


BLOCKS = 4
LANE_TILES = 8
USED = 6

LEVELS = 16
BULK = 2 * USED * 3
PERM_AT = BULK
STOR_AT = PERM_AT + LANE_TILES
MASK_AT = STOR_AT + LANE_TILES
REST_AT = 8 * (MASK_AT + 2)
HALF = USED // 2
CELLS = 2 * (HALF + USED)
REST = CELLS + 2 * LANE_TILES + 1
THIN = CELLS + 1
EDGE = 3


def whole_tiles(rows):
    return 8 * ((rows + 7) // 8)


MESSAGE = whole_tiles(REST_AT + EDGE * REST + 8 - EDGE)
THIN_MESSAGE = whole_tiles(EDGE * THIN + 8 - EDGE)

OWN, TWO, SIDE, STRIP = 8, 48, 64, 112
SPAN = 48
PADS = (0, 40, 56, 104)
TILES = tuple((OWN + 8 * k, k) for k in range(4)) + ((TWO, 4),) + tuple((SIDE + 8 * n, (n + 2) % 5) for n in range(5))


def box_tile(by, u):
    return u + 2 * (1 - by)


def lanes_of(tile):
    return pl.ds(128 * tile, 128)


def height_of_lane():
    return lax.rem(lax.broadcasted_iota(jnp.int32, (8, 128), 1), 32)


def share(first, second):
    heights = height_of_lane()
    first_up, second_up = pltpu.roll(first, LEVELS, 1), pltpu.roll(second, LEVELS, 1)
    return jnp.where(heights < LEVELS, first, second_up), first_up, second_up


def unshare(common, first_rest, second_rest):
    heights = height_of_lane()
    first = jnp.where(heights < LEVELS, common, pltpu.roll(first_rest, 128 - LEVELS, 1))
    second = pltpu.roll(jnp.where(heights >= LEVELS, common, second_rest), 128 - LEVELS, 1)
    return first, second


def put_edges(out_ref, at, pieces, rightward):
    for n, tile in enumerate(pieces):
        tile = jnp.where(rightward == 1, pltpu.roll(tile, EDGE, 0), tile)
        out_ref[at + EDGE * n : at + EDGE * (n + 1)] = tile[:EDGE]


def cells(tile):
    low = height_of_lane() < 2
    pieces = []
    for by in range(2):
        common, rests = [], [None] * USED
        for u in range(HALF):
            both, rests[u], rests[u + HALF] = share(tile(by, 0, u), tile(by, 0, u + HALF))
            common.append(both)
        pieces += common + [jnp.where(low, rests[u], tile(by, 1, u)) for u in range(USED)]
    return pieces


def put_message(out_ref, rest_ref, rest_at, leftward, prev_tile, perm_tile, stor_tile, mask_tile):
    low = height_of_lane() < 2
    def put_tile(n, tile):
        out_ref[8 * n : 8 * n + 8] = tile

    for by in range(2):
        for u in range(USED):
            common, first_up, second_up = share(prev_tile(0, by, 0, u), prev_tile(1, by, 0, u))
            at = 24 * (by * USED + u)
            out_ref[at : at + 8] = common
            out_ref[at + 8 : at + 16] = jnp.where(low, first_up, prev_tile(0, by, 1, u))
            out_ref[at + 16 : at + 24] = jnp.where(low, second_up, prev_tile(1, by, 1, u))
    for n in range(2):
        put_tile(MASK_AT + n, mask_tile(n))
    for t in range(LANE_TILES):
        put_tile(PERM_AT + t, perm_tile(1 - leftward, t))
        put_tile(STOR_AT + t, stor_tile(1 - leftward, t))
    pieces = cells(functools.partial(prev_tile, 2))
    pieces += [perm_tile(leftward, t) for t in range(LANE_TILES)]
    pieces += [stor_tile(leftward, t) for t in range(LANE_TILES)]
    pieces += [mask_tile(2)]
    put_edges(rest_ref, rest_at, pieces, 1 - leftward)
    tail, end = rest_at + EDGE * REST, rest_at + MESSAGE - REST_AT
    rest_ref[tail:end] = jnp.zeros((end - tail, 128), F32)


def eight(tile):
    return pl.ds(pl.multiple_of(8 * tile, 8), 8)


def put_thin(out_ref, leftward, prev_tile, mask_tile):
    edge = 3 - 3 * leftward
    pieces = cells(functools.partial(prev_tile, edge)) + [mask_tile(edge)]
    put_edges(out_ref, 0, pieces, 1 - leftward)
    tail = EDGE * THIN
    out_ref[tail:THIN_MESSAGE] = jnp.zeros((THIN_MESSAGE - tail, 128), F32)


def pack_kernel(
    perm_ref, stor_ref, mask_ref, prev_ref,
    far_ref, far2_ref, near2_ref, near_ref, rest_ref, perm, stor, mask_buf, prev, mask, sems,
):
    odd = lax.rem(lax.axis_index("gx"), 2)
    odd_chip = lax.rem(lax.axis_index("gx") // 2, 2)
    copies = []
    for by in range(2):
        for bz in range(2):
            blk = 2 * by + bz
            lanes = pl.ds(128 * box_tile(by, 0), 128 * USED)
            copies.append((prev_ref.at[0, by, bz, :, lanes], prev.at[blk]))
            copies.append((mask_ref.at[0, by, bz], mask.at[blk]))
    copies += [(perm_ref, perm), (stor_ref, stor)]
    copies = [pltpu.make_async_copy(src, dst, sems.at[n]) for n, (src, dst) in enumerate(copies)]
    for copy in copies:
        copy.start()
    for copy in copies:
        copy.wait()
    mask_buf[...] = jnp.concatenate([mask[blk] for blk in range(BLOCKS)], axis=1).astype(F32)

    def prev_tile(tile, by, bz, u):
        return prev[2 * by + bz, eight(tile), lanes_of(u)]

    def mask_tile(tile):
        return mask_buf[eight(tile), lanes_of(0)]

    def message(out_ref, rest_ref, rest_at, leftward):
        def tile_at(n):
            return jnp.where(leftward == 1, n, (2, 3, 1)[n])

        put_message(
            out_ref,
            rest_ref,
            rest_at,
            leftward,
            lambda n, by, bz, u: prev_tile(tile_at(n), by, bz, u),
            lambda n, t: perm[eight(n), lanes_of(t)],
            lambda n, t: stor[eight(n), lanes_of(t)],
            lambda n: mask_tile(tile_at(n)),
        )

    message(far_ref, far_ref, REST_AT, 1 - odd)
    put_thin(far2_ref, odd_chip, prev_tile, mask_tile)
    put_thin(near2_ref, 1 - odd_chip, prev_tile, mask_tile)
    message(near_ref, rest_ref, 0, odd)


def tile_rows(n):
    return slice(8 * n, 8 * n + 8)


def lane_index():
    return lax.broadcasted_iota(jnp.int32, (8, 128), 1)


def zeros():
    return jnp.zeros((8, 128), F32)


def up_y(here, after):
    return pltpu.roll(jnp.where(lane_index() >= 32, here, after), 96, 1)


def down_y(here, before):
    return pltpu.roll(jnp.where(lane_index() < 96, here, before), 32, 1)


def up_z(v):
    return pltpu.roll(v, 127, 1)


def down_z(v):
    return pltpu.roll(v, 1, 1)


def inverse(v):
    first = pl.reciprocal(v, approx=True)
    return first * (2.0 - v * first)


def harmonic(a, b):
    return 2.0 * (a * b) * inverse(jnp.maximum(a + b, TINY))


def edges(ref, at, index, left):
    start = at + EDGE * index - (8 - EDGE) * left
    tile = ref[max(start, 0) : max(start, 0) + 8]
    return pltpu.roll(tile, -start, 0) if start < 0 else tile


def fill_coefficients(rings, buf, own_ref, bulk, rest, sides):
    low = lax.broadcasted_iota(jnp.int32, (8, 128), 0) < 4
    for t in range(LANE_TILES):
        for i in rings:
            if i in (1, 2):
                tile = own_ref[tile_rows(i - 1), lanes_of(t)]
            elif i < 4:
                tile = sides[i // 3][0][tile_rows(bulk + t)]
            else:
                ends = [edges(*ref[1:], rest + t, n == 0) if ref is not None else None for n, ref in enumerate(sides)]
                tile = ends[0] if ends[1] is None else ends[1] if ends[0] is None else jnp.where(low, ends[1], ends[0])
            buf[t, tile_rows(i)] = tile


def fill_weights(rings, kbuf, cbuf, wbuf, gbuf):
    rows = lax.broadcasted_iota(jnp.int32, (8, 128), 0)
    heights = height_of_lane()

    def k_of(t, i):
        return kbuf[t, tile_rows(i % 5)] if 0 <= t < LANE_TILES else zeros()

    for t in range(LANE_TILES):
        for i in rings:
            k = k_of(t, i)
            east = jnp.where(rows < 7, pltpu.roll(k, 7, 0), pltpu.roll(k_of(t, i + 1), 7, 0))
            west = jnp.where(rows > 0, pltpu.roll(k, 1, 0), pltpu.roll(k_of(t, i + 4), 1, 0))
            faces = [
                harmonic(k, east),
                harmonic(k, west),
                harmonic(k, up_y(k, k_of(t + 1, i))),
                harmonic(k, down_y(k, k_of(t - 1, i))),
                jnp.where(heights < 31, harmonic(k, up_z(k)), 0.0),
                jnp.where(heights > 0, harmonic(k, down_z(k)), 0.0),
            ]
            diag = functools.reduce(lambda a, b: a + b, faces, cbuf[t, tile_rows(i)])
            scale = (2.0 / 3.0) * inverse(jnp.maximum(diag, TINY))
            for d, face in enumerate(faces):
                wbuf[t, d, tile_rows(i)] = face * scale
            gbuf[t, tile_rows(i)] = 1.5 * diag


def core_bits():
    lanes = lane_index()
    j = lax.rem(lanes, 32)
    return jnp.where((j >= 8) & (j < 24), jnp.where(lax.rem(lanes // 32, 2) == 0, 0xFFFF, 0xFFFF00), 0)


def support_of(bits, by, bz, u):
    offset = height_of_lane() - 8 * bz
    valid = (offset >= 0) & (offset < (18, 24)[bz])
    lane_bit = jnp.where(valid, jnp.left_shift(1, jnp.clip(offset, 0, 23)), 0)
    index = 32 * (2 * by + bz) + 4 * u + 8 * (1 - by) + lane_index() // 32
    spread = jnp.take_along_axis(bits, index, axis=1, mode="promise_in_bounds")
    return jnp.where((spread & lane_bit) != 0, 1.0, 0.0)


def message_cells(ref):
    found = [{}, {}]
    for by in range(2):
        for u in range(USED):
            at = 3 * (by * USED + u)
            common, first_top, second_top = [ref[tile_rows(at + n)] for n in range(3)]
            found[0][by, 0, u], found[1][by, 0, u] = unshare(common, first_top, second_top)
            found[0][by, 1, u], found[1][by, 1, u] = first_top, second_top
    return found


def edge_cells(fetch):
    found = {}
    for by in range(2):
        base = by * (HALF + USED)
        for u in range(HALF):
            tops = [fetch(base + HALF + u), fetch(base + HALF + u + HALF)]
            found[by, 0, u], found[by, 0, u + HALF] = unshare(fetch(base + u), *tops)
            found[by, 1, u], found[by, 1, u + HALF] = tops
    return found


def put_cells(pbuf, sup, row, found, bits):
    for (by, bz, u), tile in found.items():
        s = support_of(bits, by, bz, u)
        sup[by, bz, u, row : row + 8] = s
        pbuf[by, bz, u, row : row + 8] = s * tile


def side_row(ring):
    return SIDE + 8 * ((ring - 2) % 5)


def tile_of(pbuf, by, bz, u, row):
    return pbuf[by, bz, u, row : row + 8] if 0 <= u < USED else zeros()


def stencil(pbuf, by, bz, u, row, v, beside_y, w, beside_z=None):
    before, after = beside_y
    upper, lower = beside_z or (up_z(v), down_z(v))
    near = w[0] * pbuf[by, bz, u, row + 1 : row + 9] + w[1] * pbuf[by, bz, u, row - 1 : row + 7]
    near += w[2] * up_y(v, after) + w[3] * down_y(v, before)
    return near + (w[4] * upper + w[5] * lower)


def relax(pbuf, qbuf, sup, wbuf, by, tiles, zbuf=None, shift=None, spans=(), unfinished=()):
    if spans:
        count = sum(b - a for a, b in spans)
        v = jnp.concatenate([pbuf[by, :, :, a:b] for a, b in spans], axis=2).reshape(2 * USED * count, 128)
        high = v.astype(jnp.bfloat16)
        low = (v - high.astype(F32)).astype(jnp.bfloat16)
        parts = jnp.concatenate([high, low], axis=1)
        beside = jnp.dot(parts, shift[...], preferred_element_type=F32)
        zbuf[:, :, :count] = beside.reshape(2, USED, count, 256)
    places = {}
    for a, b in spans:
        for row in range(a, b, 8):
            places[row] = 8 * len(places)
    for i in sorted({ring for _, ring in tiles}):
        lines = [(bz, row) for bz in range(2) for row, ring in tiles if ring == i]
        before = [zeros()] * len(lines)
        here = [pbuf[by, bz, 0, row : row + 8] for bz, row in lines]
        for u in range(USED):
            w = [wbuf[u + 2 * by, d, tile_rows(i)] for d in range(6)]
            after = [tile_of(pbuf, by, bz, u + 1, row) for bz, row in lines]
            for n, (bz, row) in enumerate(lines):
                v = here[n]
                beside_z = None
                if spans:
                    at = slice(places[row], places[row] + 8)
                    beside_z = zbuf[bz, u, at, 0:128], zbuf[bz, u, at, 128:256]
                near = stencil(pbuf, by, bz, u, row, v, (before[n], after[n]), w, beside_z)
                kept = v * (1.0 / 3.0) + near
                if row not in unfinished:
                    kept = sup[by, bz, u, row : row + 8] * jnp.maximum(kept, 0.0)
                qbuf[by, bz, u, row : row + 8] = kept
            before, here = here, after


def complete(pbuf, qbuf, sup, wbuf, row, ring, eastward):
    edge = lax.broadcasted_iota(jnp.int32, (8, 128), 0) == (7 if eastward else 0)
    at = row + 1 if eastward else row - 1
    for by in range(2):
        for u in range(USED):
            w = jnp.where(edge, wbuf[u + 2 * by, 0 if eastward else 1, tile_rows(ring)], 0.0)
            for bz in range(2):
                kept = qbuf[by, bz, u, row : row + 8] + w * jnp.where(edge, pbuf[by, bz, u, at : at + 8], 0.0)
                qbuf[by, bz, u, row : row + 8] = sup[by, bz, u, row : row + 8] * jnp.maximum(kept, 0.0)


def normalise(qbuf, pbuf, tiles, basis_ref=None):
    for t in range(LANE_TILES):
        blocks = [(by, bz, t - 2 * by) for by in range(2) for bz in range(2) if 0 <= t - 2 * by < USED]
        for i in sorted({ring for _, ring in tiles}):
            at = [(b, row) for b in blocks for row, ring in tiles if ring == i]
            kept = [qbuf[by, bz, u, row : row + 8] for (by, bz, u), row in at]
            total = functools.reduce(lambda a, b: a + b, kept)
            scale = inverse(jnp.maximum(total, SUM_FLOOR))
            for ((by, bz, u), row), v in zip(at, kept):
                v = v * scale
                pbuf[by, bz, u, row : row + 8] = v
                if basis_ref is not None and row < TWO:
                    basis_ref[0, by, bz, row - OWN : row - OWN + 8, lanes_of(box_tile(by, u))] = v


def halves(odd):
    return ((1, 0), (2, 3)) if odd else ((2, 3), (1, 0))


def by_parity(body):
    parity = lax.rem(lax.axis_index("gx"), 2)
    for odd in range(2):
        pl.when(parity == odd)(functools.partial(body, odd))


def begin_kernel(perm_ref, stor_ref, mask_ref, prev_ref, near_ref, rest_ref, first, second, sup, wbuf, gbuf, qbuf, shift, kbuf, cbuf):
    here = lax.axis_index("gx")
    last = lax.axis_size("gx") - 1
    deep = lax.broadcasted_iota(jnp.int32, (256, 256), 0) % 128
    wide = lax.broadcasted_iota(jnp.int32, (256, 256), 1)
    source = jnp.where(wide < 128, wide + 1, wide - 129)
    shift[...] = jnp.where(deep == source, 1.0, 0.0).astype(jnp.bfloat16)

    own_bits = [mask_ref[tile_rows(k)].astype(jnp.int32) for k in range(4)]
    own_bits[0] = jnp.where(here == 0, 0, own_bits[0])
    own_bits[1] |= core_bits()
    own_bits[2] |= core_bits()
    own_bits[3] = jnp.where(here == last, 0, own_bits[3])
    for by in range(2):
        for bz in range(2):
            for u in range(USED):
                for row in PADS:
                    first[by, bz, u, row : row + 8] = zeros()
                    second[by, bz, u, row : row + 8] = zeros()
    for k in range(4):
        found = {
            (by, bz, u): prev_ref[2 * by + bz, tile_rows(k), lanes_of(u)]
            for by in range(2)
            for bz in range(2)
            for u in range(USED)
        }
        put_cells(first, sup, OWN + 8 * k, found, own_bits[k])

    def body(odd):
        (inner, outer), (far_inner, _) = halves(odd)
        near = (near_ref, rest_ref, 0)
        sides = (near, None) if odd else (None, near)
        fill_coefficients((1, 2, outer, 4), kbuf, perm_ref, PERM_AT, CELLS, sides)
        fill_coefficients((inner, outer), cbuf, stor_ref, STOR_AT, CELLS + LANE_TILES, sides)
        fill_weights((inner, outer), kbuf, cbuf, wbuf, gbuf)
        found = message_cells(near_ref)
        for n in range(2):
            ring = n if odd else n + 2
            bits = near_ref[tile_rows(MASK_AT + n)].astype(jnp.int32)
            put_cells(first, sup, side_row(ring), found[n], bits | core_bits() if ring in (0, 3) else bits)

        def rest(index):
            return edges(rest_ref, 0, index, odd == 1)

        put_cells(first, sup, side_row(4), edge_cells(rest), rest(REST - 1).astype(jnp.int32) | core_bits())
        tiles = [(row, i) for row, i in TILES if i in (inner, outer)]
        for by in range(2):
            relax(first, qbuf, sup, wbuf, by, tiles)
        normalise(qbuf, second, tiles)
        for by in range(2):
            for bz in range(2):
                for u in range(USED):
                    for row in (OWN + 8 * far_inner, side_row(4)):
                        second[by, bz, u, row : row + 8] = zeros()
        for by in range(2):
            relax(second, qbuf, sup, wbuf, by, tiles, unfinished=(OWN + 8 * inner, side_row(outer)))

    by_parity(body)


def finish_kernel(
    far_ref, far2_ref, near2_ref, near_ref, rest_ref, perm_ref, stor_ref, shift, _first, _second, _sup, _wbuf, _gbuf, _qbuf,
    basis_ref, coarse_ref, first, second, sup, wbuf, gbuf, qbuf,
    kbuf, cbuf, sums, zbuf,
):
    here = lax.axis_index("gx")
    odd_chip = lax.rem(here // 2, 2) == 1
    rows = lax.broadcasted_iota(jnp.int32, (8, 128), 0)
    low_rows = rows < 4

    def thin(index):
        right = jnp.where(odd_chip, edges(near2_ref, 0, index, False), edges(far2_ref, 0, index, False))
        left = jnp.where(odd_chip, edges(far2_ref, 0, index, True), edges(near2_ref, 0, index, True))
        return jnp.where(low_rows, right, left)

    def body(odd):
        (near_inner, near_outer), (inner, outer) = halves(odd)
        near, far = (near_ref, rest_ref, 0), (far_ref, far_ref, REST_AT)
        sides = (near, far) if odd else (far, near)
        fill_coefficients((1, 2, near_outer, outer, 4), kbuf, perm_ref, PERM_AT, CELLS, sides)
        fill_coefficients((inner, outer, 4), cbuf, stor_ref, STOR_AT, CELLS + LANE_TILES, sides)
        fill_weights((inner, outer, 4), kbuf, cbuf, wbuf, gbuf)
        found = message_cells(far_ref)
        for n in range(2):
            ring = n + 2 if odd else n
            bits = far_ref[tile_rows(MASK_AT + n)].astype(jnp.int32)
            put_cells(first, sup, side_row(ring), found[n], bits | core_bits() if ring in (0, 3) else bits)

        def rest(index):
            return jnp.where(low_rows, edges(*sides[1][1:], index, False), edges(*sides[0][1:], index, True))

        put_cells(first, sup, side_row(4), edge_cells(rest), rest(REST - 1).astype(jnp.int32) | core_bits())
        put_cells(first, sup, TWO, edge_cells(thin), thin(THIN - 1).astype(jnp.int32))
        tiles = [(row, i) for row, i in TILES if i in (inner, outer, 4)]
        own = OWN + 16 * odd
        side = SIDE + 16 * (1 - odd)
        spans = ((own, own + 16), (TWO, TWO + 8), (side, side + 24))
        for by in range(2):
            relax(first, qbuf, sup, wbuf, by, tiles, zbuf, shift, spans)
        normalise(qbuf, second, tiles)
        for by in range(2):
            relax(second, qbuf, sup, wbuf, by, tiles, zbuf, shift, spans)
        complete(second, qbuf, sup, wbuf, OWN + 8 * near_inner, near_inner, odd == 1)
        complete(second, qbuf, sup, wbuf, side_row(near_outer), near_outer, odd == 0)

    by_parity(body)

    pbuf = first
    normalise(qbuf, pbuf, TILES, basis_ref)
    for by in range(2):
        for bz in range(2):
            at = 0 if by == 0 else 768
            basis_ref[0, by, bz, :, at : at + 256] = jnp.zeros((32, 256), F32)

    for by in range(2):
        acc = [[] for _ in range(24)]
        for t in range(by, by + USED + 1):
            u = t - 2 * by
            weights = [[wbuf[t, d, tile_rows(i)] for d in range(6)] for i in range(5)]
            scale = [gbuf[t, 8 * i : 8 * i + 8] for i in range(5)]
            images = [[], []]
            for k in range(4):
                row = OWN + 8 * k
                for bz in range(2):
                    beside_y = tile_of(pbuf, by, bz, u - 1, row), tile_of(pbuf, by, bz, u + 1, row)
                    if 0 <= u < USED:
                        v = tile_of(pbuf, by, bz, u, row)
                        near = stencil(pbuf, by, bz, u, row, v, beside_y, weights[k])
                        images[bz].append(scale[k] * (v * (2.0 / 3.0) - near))
                    elif u < 0:
                        images[bz].append(-scale[k] * (weights[k][2] * up_y(zeros(), beside_y[1])))
                    else:
                        images[bz].append(-scale[k] * (weights[k][3] * down_y(zeros(), beside_y[0])))
            ends = [None, None]
            if 0 <= u < USED:
                for bz in range(2):
                    beyond = -scale[4] * (weights[4][1] * pbuf[by, bz, u, OWN + 31 : OWN + 39])
                    before = -scale[4] * (weights[4][0] * pbuf[by, bz, u, OWN - 7 : OWN + 1])
                    ends[bz] = before, beyond
            for partner in range(BLOCKS):
                by2, bz2 = divmod(partner, 2)
                u2 = t - 2 * by2
                if not 0 <= u2 < USED:
                    continue
                own = [tile_of(pbuf, by2, bz2, u2, OWN + 8 * k) for k in range(4)]
                side = [tile_of(pbuf, by2, bz2, u2, SIDE + 8 * k) for k in range(5)]
                for bz in range(2):
                    image = images[bz]
                    at = bz * 12 + partner
                    acc[at] += [image[0] * side[3], image[1] * side[4]]
                    acc[at + 4] += [image[k] * own[k] for k in range(4)]
                    acc[at + 8] += [image[2] * side[0], image[3] * side[1]]
                    if ends[bz] is not None:
                        acc[at] += [ends[bz][0] * side[2]]
                        acc[at + 8] += [ends[bz][1] * side[2]]
            acc = [[functools.reduce(lambda a, b: a + b, terms)] if terms else [] for terms in acc]
        for bz in range(2):
            for n in range(12):
                sums[2 * by + bz, n] = jnp.sum(acc[bz * 12 + n][0], axis=0)

    entry = lax.broadcasted_iota(jnp.int32, (16, 128), 0)
    column = lax.broadcasted_iota(jnp.int32, (16, 128), 1)
    for by in range(2):
        for bz in range(2):
            values = jnp.sum(sums[2 * by + bz], axis=1, keepdims=True)
            target = 9 * (entry // 4) + 3 * (lax.rem(entry // 2, 2) - by + 1) + (lax.rem(entry, 2) - bz + 1)
            placed = jnp.where((column == target) & (entry < 12), values, 0.0)
            coarse_ref[0, by, bz, :] = jnp.sum(placed, axis=0)[:27]


def shards(permeability, storage, support_mask, prev_basis):
    vmem = pl.BlockSpec(memory_space=pltpu.VMEM)
    far, far2, near2, near, rest, *own = pl.pallas_call(
        pack_kernel,
        in_specs=[pl.BlockSpec(memory_space=pl.ANY)] * 4,
        out_specs=[vmem] * 9,
        out_shape=[
            *[pltpu.VMEM((n, 128), F32) for n in (MESSAGE, THIN_MESSAGE, THIN_MESSAGE, REST_AT, MESSAGE - REST_AT)],
            pltpu.VMEM(permeability.shape, F32),
            pltpu.VMEM(storage.shape, F32),
            pltpu.VMEM((32, 128), F32),
            pltpu.VMEM((BLOCKS, 32, 128 * USED), F32),
        ],
        scratch_shapes=[
            pltpu.VMEM((BLOCKS, 32, 32), jnp.int32),
            pltpu.SemaphoreType.DMA((2 * BLOCKS + 2,)),
        ],
        name="pack",
    )(permeability, storage, support_mask, prev_basis)
    size = lax.axis_size("gx")

    def move(x, step, width):
        pairs = [(i, i + (-step if i // width % 2 else step)) for i in range(size)]
        return lax.ppermute(x, "gx", [(i, j) for i, j in pairs if 0 <= j < size])

    far = move(far, -1, 1)
    far2 = move(far2, 2, 2)
    near2 = move(near2, -2, 2)
    near = move(near, 1, 1)
    rest = move(rest, 1, 1)

    strips = (2, 2, USED, STRIP, 128)
    state = [
        pltpu.VMEM(strips, F32),
        pltpu.VMEM(strips, F32),
        pltpu.VMEM(strips, F32),
        pltpu.VMEM((LANE_TILES, 6, 40, 128), F32),
        pltpu.VMEM((LANE_TILES, 40, 128), F32),
        pltpu.VMEM(strips, F32),
    ]
    scratch = [pltpu.VMEM((LANE_TILES, 40, 128), F32)] * 2
    limit = pltpu.CompilerParams(vmem_limit_bytes=32 * 1024 * 1024)
    *filled, shift = pl.pallas_call(
        begin_kernel,
        in_specs=[vmem] * 6,
        out_specs=[vmem] * 7,
        out_shape=[*state, pltpu.VMEM((256, 256), jnp.bfloat16)],
        scratch_shapes=scratch,
        compiler_params=limit,
        cost_estimate=pl.CostEstimate(flops=0, bytes_accessed=0, transcendentals=0),
        name="begin",
    )(*own, near, rest)
    return pl.pallas_call(
        finish_kernel,
        in_specs=[vmem] * 14,
        out_specs=[vmem] * 8,
        out_shape=[
            jax.ShapeDtypeStruct(prev_basis.shape, F32),
            jax.ShapeDtypeStruct((*prev_basis.shape[:3], 27), F32),
            *state,
        ],
        input_output_aliases={8 + n: 2 + n for n in range(6)},
        scratch_shapes=[
            *scratch,
            pltpu.VMEM((4, 16, 128), F32),
            pltpu.VMEM((2, USED, SPAN, 256), F32),
        ],
        compiler_params=limit,
        name="finish",
    )(far, far2, near2, near, rest, *own[:2], shift, *filled)[:2]


def solution(mesh):
    placed = (
        P(("groups", "gx"), None),
        P(("groups", "gx"), None),
        P(("groups", "gx"), None, None, None, None),
        P(("groups", "gx"), None, None, None, None),
    )
    return jax.shard_map(
        shards,
        mesh=mesh,
        in_specs=placed,
        out_specs=(
            P(("groups", "gx"), None, None, None, None),
            P(("groups", "gx"), None, None, None),
        ),
        check_vma=False,
    )
```

```python
import functools

import jax
import jax.numpy as jnp
from jax import lax
from jax.experimental import pallas as pl
from jax.experimental.pallas import tpu as pltpu
from jax.sharding import PartitionSpec as P

SUM_FLOOR = 0.5
TINY = 1e-30
F32 = jnp.float32


BLOCKS = 4
LANE_TILES = 8
USED = 6

LEVELS = 16
BULK = 2 * USED * 3
PERM_AT = BULK
STOR_AT = PERM_AT + LANE_TILES
MASK_AT = STOR_AT + LANE_TILES
REST_AT = 8 * (MASK_AT + 2)
HALF = USED // 2
CELLS = 2 * (HALF + USED)
REST = CELLS + 2 * LANE_TILES + 1
THIN = CELLS + 1
EDGE = 3


def whole_tiles(rows):
    return 8 * ((rows + 7) // 8)


MESSAGE = whole_tiles(REST_AT + EDGE * REST + 8 - EDGE)
THIN_MESSAGE = whole_tiles(EDGE * THIN + 8 - EDGE)

OWN, TWO, SIDE, STRIP = 8, 48, 64, 112
SPAN = 48
PADS = (0, 40, 56, 104)
TILES = tuple((OWN + 8 * k, k) for k in range(4)) + ((TWO, 4),) + tuple((SIDE + 8 * n, (n + 2) % 5) for n in range(5))


def box_tile(by, u):
    return u + 2 * (1 - by)


def lanes_of(tile):
    return pl.ds(128 * tile, 128)


def height_of_lane():
    return lax.rem(lax.broadcasted_iota(jnp.int32, (8, 128), 1), 32)


def share(first, second):
    heights = height_of_lane()
    first_up, second_up = pltpu.roll(first, LEVELS, 1), pltpu.roll(second, LEVELS, 1)
    return jnp.where(heights < LEVELS, first, second_up), first_up, second_up


def unshare(common, first_rest, second_rest):
    heights = height_of_lane()
    first = jnp.where(heights < LEVELS, common, pltpu.roll(first_rest, 128 - LEVELS, 1))
    second = pltpu.roll(jnp.where(heights >= LEVELS, common, second_rest), 128 - LEVELS, 1)
    return first, second


def put_edges(out_ref, at, pieces, rightward):
    for n, tile in enumerate(pieces):
        tile = jnp.where(rightward == 1, pltpu.roll(tile, EDGE, 0), tile)
        out_ref[at + EDGE * n : at + EDGE * (n + 1)] = tile[:EDGE]


def cells(tile):
    low = height_of_lane() < 2
    pieces = []
    for by in range(2):
        common, rests = [], [None] * USED
        for u in range(HALF):
            both, rests[u], rests[u + HALF] = share(tile(by, 0, u), tile(by, 0, u + HALF))
            common.append(both)
        pieces += common + [jnp.where(low, rests[u], tile(by, 1, u)) for u in range(USED)]
    return pieces


def put_message(out_ref, rest_ref, rest_at, leftward, prev_tile, perm_tile, stor_tile, mask_tile):
    low = height_of_lane() < 2
    def put_tile(n, tile):
        out_ref[8 * n : 8 * n + 8] = tile

    for by in range(2):
        for u in range(USED):
            common, first_up, second_up = share(prev_tile(0, by, 0, u), prev_tile(1, by, 0, u))
            at = 24 * (by * USED + u)
            out_ref[at : at + 8] = common
            out_ref[at + 8 : at + 16] = jnp.where(low, first_up, prev_tile(0, by, 1, u))
            out_ref[at + 16 : at + 24] = jnp.where(low, second_up, prev_tile(1, by, 1, u))
    for n in range(2):
        put_tile(MASK_AT + n, mask_tile(n))
    for t in range(LANE_TILES):
        put_tile(PERM_AT + t, perm_tile(1 - leftward, t))
        put_tile(STOR_AT + t, stor_tile(1 - leftward, t))
    pieces = cells(functools.partial(prev_tile, 2))
    pieces += [perm_tile(leftward, t) for t in range(LANE_TILES)]
    pieces += [stor_tile(leftward, t) for t in range(LANE_TILES)]
    pieces += [mask_tile(2)]
    end = rest_at + MESSAGE - REST_AT
    rest_ref[end - 8 : end] = zeros()
    put_edges(rest_ref, rest_at, pieces, 1 - leftward)


def eight(tile):
    return pl.ds(pl.multiple_of(8 * tile, 8), 8)


def put_thin(out_ref, leftward, prev_tile, mask_tile):
    edge = 3 - 3 * leftward
    pieces = cells(functools.partial(prev_tile, edge)) + [mask_tile(edge)]
    out_ref[THIN_MESSAGE - 8 : THIN_MESSAGE] = zeros()
    put_edges(out_ref, 0, pieces, 1 - leftward)


def pack_kernel(
    perm_ref, stor_ref, mask_ref, prev_ref,
    far_ref, far2_ref, near2_ref, near_ref, rest_ref, perm, stor, mask_buf, prev, mask, sems,
):
    odd = lax.rem(lax.axis_index("gx"), 2)
    odd_chip = lax.rem(lax.axis_index("gx") // 2, 2)
    copies = []
    for by in range(2):
        for bz in range(2):
            blk = 2 * by + bz
            lanes = pl.ds(128 * box_tile(by, 0), 128 * USED)
            copies.append((prev_ref.at[0, by, bz, :, lanes], prev.at[blk]))
            copies.append((mask_ref.at[0, by, bz], mask.at[blk]))
    copies += [(perm_ref, perm), (stor_ref, stor)]
    copies = [pltpu.make_async_copy(src, dst, sems.at[n]) for n, (src, dst) in enumerate(copies)]
    for copy in copies:
        copy.start()
    for copy in copies:
        copy.wait()
    mask_buf[...] = jnp.concatenate([mask[blk] for blk in range(BLOCKS)], axis=1).astype(F32)

    def prev_tile(tile, by, bz, u):
        return prev[2 * by + bz, eight(tile), lanes_of(u)]

    def mask_tile(tile):
        return mask_buf[eight(tile), lanes_of(0)]

    def message(out_ref, rest_ref, rest_at, leftward):
        def tile_at(n):
            return jnp.where(leftward == 1, n, (2, 3, 1)[n])

        put_message(
            out_ref,
            rest_ref,
            rest_at,
            leftward,
            lambda n, by, bz, u: prev_tile(tile_at(n), by, bz, u),
            lambda n, t: perm[eight(n), lanes_of(t)],
            lambda n, t: stor[eight(n), lanes_of(t)],
            lambda n: mask_tile(tile_at(n)),
        )

    message(far_ref, far_ref, REST_AT, 1 - odd)
    put_thin(far2_ref, odd_chip, prev_tile, mask_tile)
    put_thin(near2_ref, 1 - odd_chip, prev_tile, mask_tile)
    message(near_ref, rest_ref, 0, odd)


def tile_rows(n):
    return slice(8 * n, 8 * n + 8)


def lane_index():
    return lax.broadcasted_iota(jnp.int32, (8, 128), 1)


def zeros():
    return jnp.zeros((8, 128), F32)


def up_y(here, after):
    return pltpu.roll(jnp.where(lane_index() >= 32, here, after), 96, 1)


def down_y(here, before):
    return pltpu.roll(jnp.where(lane_index() < 96, here, before), 32, 1)


def up_z(v):
    return pltpu.roll(v, 127, 1)


def down_z(v):
    return pltpu.roll(v, 1, 1)


def inverse(v):
    first = pl.reciprocal(v, approx=True)
    return first * (2.0 - v * first)


def harmonic(a, b):
    return 2.0 * (a * b) * inverse(jnp.maximum(a + b, TINY))


def edges(ref, at, index, left):
    start = at + EDGE * index - (8 - EDGE) * left
    tile = ref[max(start, 0) : max(start, 0) + 8]
    return pltpu.roll(tile, -start, 0) if start < 0 else tile


def fill_coefficients(rings, buf, own_ref, bulk, rest, sides):
    low = lax.broadcasted_iota(jnp.int32, (8, 128), 0) < 4
    for t in range(LANE_TILES):
        for i in rings:
            if i in (1, 2):
                tile = own_ref[tile_rows(i - 1), lanes_of(t)]
            elif i < 4:
                tile = sides[i // 3][0][tile_rows(bulk + t)]
            else:
                ends = [edges(*ref[1:], rest + t, n == 0) if ref is not None else None for n, ref in enumerate(sides)]
                tile = ends[0] if ends[1] is None else ends[1] if ends[0] is None else jnp.where(low, ends[1], ends[0])
            buf[t, tile_rows(i)] = tile


def fill_weights(rings, kbuf, cbuf, wbuf, gbuf):
    rows = lax.broadcasted_iota(jnp.int32, (8, 128), 0)
    heights = height_of_lane()

    def k_of(t, i):
        return kbuf[t, tile_rows(i % 5)] if 0 <= t < LANE_TILES else zeros()

    for t in range(LANE_TILES):
        for i in rings:
            k = k_of(t, i)
            east = jnp.where(rows < 7, pltpu.roll(k, 7, 0), pltpu.roll(k_of(t, i + 1), 7, 0))
            west = jnp.where(rows > 0, pltpu.roll(k, 1, 0), pltpu.roll(k_of(t, i + 4), 1, 0))
            faces = [
                harmonic(k, east),
                harmonic(k, west),
                harmonic(k, up_y(k, k_of(t + 1, i))),
                harmonic(k, down_y(k, k_of(t - 1, i))),
                jnp.where(heights < 31, harmonic(k, up_z(k)), 0.0),
                jnp.where(heights > 0, harmonic(k, down_z(k)), 0.0),
            ]
            diag = functools.reduce(lambda a, b: a + b, faces, cbuf[t, tile_rows(i)])
            scale = (2.0 / 3.0) * inverse(jnp.maximum(diag, TINY))
            for d, face in enumerate(faces):
                wbuf[t, d, tile_rows(i)] = face * scale
            gbuf[t, tile_rows(i)] = 1.5 * diag


def core_bits():
    lanes = lane_index()
    j = lax.rem(lanes, 32)
    return jnp.where((j >= 8) & (j < 24), jnp.where(lax.rem(lanes // 32, 2) == 0, 0xFFFF, 0xFFFF00), 0)


def support_of(bits, by, bz, u):
    offset = height_of_lane() - 8 * bz
    valid = (offset >= 0) & (offset < (18, 24)[bz])
    lane_bit = jnp.where(valid, jnp.left_shift(1, jnp.clip(offset, 0, 23)), 0)
    index = 32 * (2 * by + bz) + 4 * u + 8 * (1 - by) + lane_index() // 32
    spread = jnp.take_along_axis(bits, index, axis=1, mode="promise_in_bounds")
    return jnp.where((spread & lane_bit) != 0, 1.0, 0.0)


def message_cells(ref):
    found = [{}, {}]
    for by in range(2):
        for u in range(USED):
            at = 3 * (by * USED + u)
            common, first_top, second_top = [ref[tile_rows(at + n)] for n in range(3)]
            found[0][by, 0, u], found[1][by, 0, u] = unshare(common, first_top, second_top)
            found[0][by, 1, u], found[1][by, 1, u] = first_top, second_top
    return found


def edge_cells(fetch):
    found = {}
    for by in range(2):
        base = by * (HALF + USED)
        for u in range(HALF):
            tops = [fetch(base + HALF + u), fetch(base + HALF + u + HALF)]
            found[by, 0, u], found[by, 0, u + HALF] = unshare(fetch(base + u), *tops)
            found[by, 1, u], found[by, 1, u + HALF] = tops
    return found


def put_cells(pbuf, sup, row, found, bits):
    for (by, bz, u), tile in found.items():
        s = support_of(bits, by, bz, u)
        sup[by, bz, u, row : row + 8] = s
        pbuf[by, bz, u, row : row + 8] = s * tile


def side_row(ring):
    return SIDE + 8 * ((ring - 2) % 5)


def tile_of(pbuf, by, bz, u, row):
    return pbuf[by, bz, u, row : row + 8] if 0 <= u < USED else zeros()


def stencil(pbuf, by, bz, u, row, v, beside_y, w, beside_z=None):
    before, after = beside_y
    upper, lower = beside_z or (up_z(v), down_z(v))
    near = w[0] * pbuf[by, bz, u, row + 1 : row + 9] + w[1] * pbuf[by, bz, u, row - 1 : row + 7]
    near += w[2] * up_y(v, after) + w[3] * down_y(v, before)
    return near + (w[4] * upper + w[5] * lower)


def relax(pbuf, qbuf, sup, wbuf, by, tiles, zbuf=None, shift=None, spans=(), unfinished=()):
    if spans:
        count = sum(b - a for a, b in spans)
        v = jnp.concatenate([pbuf[by, :, :, a:b] for a, b in spans], axis=2).reshape(2 * USED * count, 128)
        high = v.astype(jnp.bfloat16)
        low = (v - high.astype(F32)).astype(jnp.bfloat16)
        parts = jnp.concatenate([high, low], axis=1)
        beside = jnp.dot(parts, shift[...], preferred_element_type=F32)
        zbuf[:, :, :count] = beside.reshape(2, USED, count, 256)
    places = {}
    for a, b in spans:
        for row in range(a, b, 8):
            places[row] = 8 * len(places)
    for i in sorted({ring for _, ring in tiles}):
        lines = [(bz, row) for bz in range(2) for row, ring in tiles if ring == i]
        before = [zeros()] * len(lines)
        here = [pbuf[by, bz, 0, row : row + 8] for bz, row in lines]
        for u in range(USED):
            w = [wbuf[u + 2 * by, d, tile_rows(i)] for d in range(6)]
            after = [tile_of(pbuf, by, bz, u + 1, row) for bz, row in lines]
            for n, (bz, row) in enumerate(lines):
                v = here[n]
                beside_z = None
                if spans:
                    at = slice(places[row], places[row] + 8)
                    beside_z = zbuf[bz, u, at, 0:128], zbuf[bz, u, at, 128:256]
                near = stencil(pbuf, by, bz, u, row, v, (before[n], after[n]), w, beside_z)
                kept = v * (1.0 / 3.0) + near
                if row not in unfinished:
                    kept = sup[by, bz, u, row : row + 8] * jnp.maximum(kept, 0.0)
                qbuf[by, bz, u, row : row + 8] = kept
            before, here = here, after


def complete(pbuf, qbuf, sup, wbuf, row, ring, eastward):
    edge = lax.broadcasted_iota(jnp.int32, (8, 128), 0) == (7 if eastward else 0)
    at = row + 1 if eastward else row - 1
    for by in range(2):
        for u in range(USED):
            w = jnp.where(edge, wbuf[u + 2 * by, 0 if eastward else 1, tile_rows(ring)], 0.0)
            for bz in range(2):
                kept = qbuf[by, bz, u, row : row + 8] + w * jnp.where(edge, pbuf[by, bz, u, at : at + 8], 0.0)
                qbuf[by, bz, u, row : row + 8] = sup[by, bz, u, row : row + 8] * jnp.maximum(kept, 0.0)


def normalise(qbuf, pbuf, tiles, basis_ref=None):
    for t in range(LANE_TILES):
        blocks = [(by, bz, t - 2 * by) for by in range(2) for bz in range(2) if 0 <= t - 2 * by < USED]
        for i in sorted({ring for _, ring in tiles}):
            at = [(b, row) for b in blocks for row, ring in tiles if ring == i]
            kept = [qbuf[by, bz, u, row : row + 8] for (by, bz, u), row in at]
            total = functools.reduce(lambda a, b: a + b, kept)
            scale = inverse(jnp.maximum(total, SUM_FLOOR))
            for ((by, bz, u), row), v in zip(at, kept):
                v = v * scale
                pbuf[by, bz, u, row : row + 8] = v
                if basis_ref is not None and row < TWO:
                    basis_ref[0, by, bz, row - OWN : row - OWN + 8, lanes_of(box_tile(by, u))] = v


def halves(odd):
    return ((1, 0), (2, 3)) if odd else ((2, 3), (1, 0))


def by_parity(body):
    parity = lax.rem(lax.axis_index("gx"), 2)
    for odd in range(2):
        pl.when(parity == odd)(functools.partial(body, odd))


def begin_kernel(perm_ref, stor_ref, mask_ref, prev_ref, near_ref, rest_ref, first, second, sup, wbuf, gbuf, qbuf, shift, kbuf, cbuf):
    here = lax.axis_index("gx")
    last = lax.axis_size("gx") - 1
    deep = lax.broadcasted_iota(jnp.int32, (256, 256), 0) % 128
    wide = lax.broadcasted_iota(jnp.int32, (256, 256), 1)
    source = jnp.where(wide < 128, wide + 1, wide - 129)
    shift[...] = jnp.where(deep == source, 1.0, 0.0).astype(jnp.bfloat16)

    own_bits = [mask_ref[tile_rows(k)].astype(jnp.int32) for k in range(4)]
    own_bits[0] = jnp.where(here == 0, 0, own_bits[0])
    own_bits[1] |= core_bits()
    own_bits[2] |= core_bits()
    own_bits[3] = jnp.where(here == last, 0, own_bits[3])
    for by in range(2):
        for bz in range(2):
            for u in range(USED):
                for row in PADS:
                    first[by, bz, u, row : row + 8] = zeros()
                    second[by, bz, u, row : row + 8] = zeros()
    for k in range(4):
        found = {
            (by, bz, u): prev_ref[2 * by + bz, tile_rows(k), lanes_of(u)]
            for by in range(2)
            for bz in range(2)
            for u in range(USED)
        }
        put_cells(first, sup, OWN + 8 * k, found, own_bits[k])

    def body(odd):
        (inner, outer), (far_inner, _) = halves(odd)
        near = (near_ref, rest_ref, 0)
        sides = (near, None) if odd else (None, near)
        fill_coefficients((1, 2, outer, 4), kbuf, perm_ref, PERM_AT, CELLS, sides)
        fill_coefficients((inner, outer), cbuf, stor_ref, STOR_AT, CELLS + LANE_TILES, sides)
        fill_weights((inner, outer), kbuf, cbuf, wbuf, gbuf)
        found = message_cells(near_ref)
        for n in range(2):
            ring = n if odd else n + 2
            bits = near_ref[tile_rows(MASK_AT + n)].astype(jnp.int32)
            put_cells(first, sup, side_row(ring), found[n], bits | core_bits() if ring in (0, 3) else bits)

        def rest(index):
            return edges(rest_ref, 0, index, odd == 1)

        put_cells(first, sup, side_row(4), edge_cells(rest), rest(REST - 1).astype(jnp.int32) | core_bits())
        tiles = [(row, i) for row, i in TILES if i in (inner, outer)]
        for by in range(2):
            relax(first, qbuf, sup, wbuf, by, tiles)
        normalise(qbuf, second, tiles)
        for by in range(2):
            for bz in range(2):
                for u in range(USED):
                    for row in (OWN + 8 * far_inner, side_row(4)):
                        second[by, bz, u, row : row + 8] = zeros()
        for by in range(2):
            relax(second, qbuf, sup, wbuf, by, tiles, unfinished=(OWN + 8 * inner, side_row(outer)))

    by_parity(body)


def finish_kernel(
    far_ref, far2_ref, near2_ref, near_ref, rest_ref, perm_ref, stor_ref, shift, _first, _second, _sup, _wbuf, _gbuf, _qbuf,
    basis_ref, coarse_ref, first, second, sup, wbuf, gbuf, qbuf,
    kbuf, cbuf, sums, zbuf,
):
    here = lax.axis_index("gx")
    odd_chip = lax.rem(here // 2, 2) == 1
    rows = lax.broadcasted_iota(jnp.int32, (8, 128), 0)
    low_rows = rows < 4

    def thin(index):
        right = jnp.where(odd_chip, edges(near2_ref, 0, index, False), edges(far2_ref, 0, index, False))
        left = jnp.where(odd_chip, edges(far2_ref, 0, index, True), edges(near2_ref, 0, index, True))
        return jnp.where(low_rows, right, left)

    def body(odd):
        (near_inner, near_outer), (inner, outer) = halves(odd)
        near, far = (near_ref, rest_ref, 0), (far_ref, far_ref, REST_AT)
        sides = (near, far) if odd else (far, near)
        fill_coefficients((1, 2, near_outer, outer, 4), kbuf, perm_ref, PERM_AT, CELLS, sides)
        fill_coefficients((inner, outer, 4), cbuf, stor_ref, STOR_AT, CELLS + LANE_TILES, sides)
        fill_weights((inner, outer, 4), kbuf, cbuf, wbuf, gbuf)
        found = message_cells(far_ref)
        for n in range(2):
            ring = n + 2 if odd else n
            bits = far_ref[tile_rows(MASK_AT + n)].astype(jnp.int32)
            put_cells(first, sup, side_row(ring), found[n], bits | core_bits() if ring in (0, 3) else bits)

        def rest(index):
            return jnp.where(low_rows, edges(*sides[1][1:], index, False), edges(*sides[0][1:], index, True))

        put_cells(first, sup, side_row(4), edge_cells(rest), rest(REST - 1).astype(jnp.int32) | core_bits())
        put_cells(first, sup, TWO, edge_cells(thin), thin(THIN - 1).astype(jnp.int32))
        tiles = [(row, i) for row, i in TILES if i in (inner, outer, 4)]
        own = OWN + 16 * odd
        side = SIDE + 16 * (1 - odd)
        spans = ((own, own + 16), (TWO, TWO + 8), (side, side + 24))
        for by in range(2):
            relax(first, qbuf, sup, wbuf, by, tiles, zbuf, shift, spans)
        normalise(qbuf, second, tiles)
        for by in range(2):
            relax(second, qbuf, sup, wbuf, by, tiles, zbuf, shift, spans)
        complete(second, qbuf, sup, wbuf, OWN + 8 * near_inner, near_inner, odd == 1)
        complete(second, qbuf, sup, wbuf, side_row(near_outer), near_outer, odd == 0)

    by_parity(body)

    pbuf = first
    normalise(qbuf, pbuf, TILES, basis_ref)
    for by in range(2):
        for bz in range(2):
            at = 0 if by == 0 else 768
            basis_ref[0, by, bz, :, at : at + 256] = jnp.zeros((32, 256), F32)

    for by in range(2):
        acc = [[] for _ in range(24)]
        for t in range(by, by + USED + 1):
            u = t - 2 * by
            weights = [[wbuf[t, d, tile_rows(i)] for d in range(6)] for i in range(5)]
            scale = [gbuf[t, 8 * i : 8 * i + 8] for i in range(5)]
            images = [[], []]
            for k in range(4):
                row = OWN + 8 * k
                for bz in range(2):
                    beside_y = tile_of(pbuf, by, bz, u - 1, row), tile_of(pbuf, by, bz, u + 1, row)
                    if 0 <= u < USED:
                        v = tile_of(pbuf, by, bz, u, row)
                        near = stencil(pbuf, by, bz, u, row, v, beside_y, weights[k])
                        images[bz].append(scale[k] * (v * (2.0 / 3.0) - near))
                    elif u < 0:
                        images[bz].append(-scale[k] * (weights[k][2] * up_y(zeros(), beside_y[1])))
                    else:
                        images[bz].append(-scale[k] * (weights[k][3] * down_y(zeros(), beside_y[0])))
            ends = [None, None]
            if 0 <= u < USED:
                for bz in range(2):
                    beyond = -scale[4] * (weights[4][1] * pbuf[by, bz, u, OWN + 31 : OWN + 39])
                    before = -scale[4] * (weights[4][0] * pbuf[by, bz, u, OWN - 7 : OWN + 1])
                    ends[bz] = before, beyond
            for partner in range(BLOCKS):
                by2, bz2 = divmod(partner, 2)
                u2 = t - 2 * by2
                if not 0 <= u2 < USED:
                    continue
                own = [tile_of(pbuf, by2, bz2, u2, OWN + 8 * k) for k in range(4)]
                side = [tile_of(pbuf, by2, bz2, u2, SIDE + 8 * k) for k in range(5)]
                for bz in range(2):
                    image = images[bz]
                    at = bz * 12 + partner
                    acc[at] += [image[0] * side[3], image[1] * side[4]]
                    acc[at + 4] += [image[k] * own[k] for k in range(4)]
                    acc[at + 8] += [image[2] * side[0], image[3] * side[1]]
                    if ends[bz] is not None:
                        acc[at] += [ends[bz][0] * side[2]]
                        acc[at + 8] += [ends[bz][1] * side[2]]
            acc = [[functools.reduce(lambda a, b: a + b, terms)] if terms else [] for terms in acc]
        for bz in range(2):
            for n in range(12):
                sums[2 * by + bz, n] = jnp.sum(acc[bz * 12 + n][0], axis=0)

    entry = lax.broadcasted_iota(jnp.int32, (16, 128), 0)
    column = lax.broadcasted_iota(jnp.int32, (16, 128), 1)
    for by in range(2):
        for bz in range(2):
            values = jnp.sum(sums[2 * by + bz], axis=1, keepdims=True)
            target = 9 * (entry // 4) + 3 * (lax.rem(entry // 2, 2) - by + 1) + (lax.rem(entry, 2) - bz + 1)
            placed = jnp.where((column == target) & (entry < 12), values, 0.0)
            coarse_ref[0, by, bz, :] = jnp.sum(placed, axis=0)[:27]


def shards(permeability, storage, support_mask, prev_basis):
    vmem = pl.BlockSpec(memory_space=pltpu.VMEM)
    far, far2, near2, near, rest, *own = pl.pallas_call(
        pack_kernel,
        in_specs=[pl.BlockSpec(memory_space=pl.ANY)] * 4,
        out_specs=[vmem] * 9,
        out_shape=[
            *[pltpu.VMEM((n, 128), F32) for n in (MESSAGE, THIN_MESSAGE, THIN_MESSAGE, REST_AT, MESSAGE - REST_AT)],
            pltpu.VMEM(permeability.shape, F32),
            pltpu.VMEM(storage.shape, F32),
            pltpu.VMEM((32, 128), F32),
            pltpu.VMEM((BLOCKS, 32, 128 * USED), F32),
        ],
        scratch_shapes=[
            pltpu.VMEM((BLOCKS, 32, 32), jnp.int32),
            pltpu.SemaphoreType.DMA((2 * BLOCKS + 2,)),
        ],
        name="pack",
    )(permeability, storage, support_mask, prev_basis)
    size = lax.axis_size("gx")

    def move(x, step, width):
        pairs = [(i, i + (-step if i // width % 2 else step)) for i in range(size)]
        return lax.ppermute(x, "gx", [(i, j) for i, j in pairs if 0 <= j < size])

    far = move(far, -1, 1)
    far2 = move(far2, 2, 2)
    near2 = move(near2, -2, 2)
    near = move(near, 1, 1)
    rest = move(rest, 1, 1)

    strips = (2, 2, USED, STRIP, 128)
    state = [
        pltpu.VMEM(strips, F32),
        pltpu.VMEM(strips, F32),
        pltpu.VMEM(strips, F32),
        pltpu.VMEM((LANE_TILES, 6, 40, 128), F32),
        pltpu.VMEM((LANE_TILES, 40, 128), F32),
        pltpu.VMEM(strips, F32),
    ]
    scratch = [pltpu.VMEM((LANE_TILES, 40, 128), F32)] * 2
    limit = pltpu.CompilerParams(vmem_limit_bytes=32 * 1024 * 1024)
    *filled, shift = pl.pallas_call(
        begin_kernel,
        in_specs=[vmem] * 6,
        out_specs=[vmem] * 7,
        out_shape=[*state, pltpu.VMEM((256, 256), jnp.bfloat16)],
        scratch_shapes=scratch,
        compiler_params=limit,
        cost_estimate=pl.CostEstimate(flops=0, bytes_accessed=0, transcendentals=0),
        name="begin",
    )(*own, near, rest)
    return pl.pallas_call(
        finish_kernel,
        in_specs=[vmem] * 14,
        out_specs=[vmem] * 8,
        out_shape=[
            jax.ShapeDtypeStruct(prev_basis.shape, F32),
            jax.ShapeDtypeStruct((*prev_basis.shape[:3], 27), F32),
            *state,
        ],
        input_output_aliases={8 + n: 2 + n for n in range(6)},
        scratch_shapes=[
            *scratch,
            pltpu.VMEM((4, 16, 128), F32),
            pltpu.VMEM((2, USED, SPAN, 256), F32),
        ],
        compiler_params=limit,
        name="finish",
    )(far, far2, near2, near, rest, *own[:2], shift, *filled)[:2]


def solution(mesh):
    placed = (
        P(("groups", "gx"), None),
        P(("groups", "gx"), None),
        P(("groups", "gx"), None, None, None, None),
        P(("groups", "gx"), None, None, None, None),
    )
    return jax.shard_map(
        shards,
        mesh=mesh,
        in_specs=placed,
        out_specs=(
            P(("groups", "gx"), None, None, None, None),
            P(("groups", "gx"), None, None, None),
        ),
        check_vma=False,
    )
```

```python
import functools

import jax
import jax.numpy as jnp
from jax import lax
from jax.experimental import pallas as pl
from jax.experimental.pallas import tpu as pltpu
from jax.sharding import PartitionSpec as P

SUM_FLOOR = 0.5
TINY = 1e-30
F32 = jnp.float32


BLOCKS = 4
LANE_TILES = 8
USED = 6

LEVELS = 16
BULK = 2 * USED * 3
PERM_AT = BULK
STOR_AT = PERM_AT + LANE_TILES
MASK_AT = STOR_AT + LANE_TILES
REST_AT = 8 * (MASK_AT + 2)
HALF = USED // 2
CELLS = 2 * (HALF + USED)
REST = CELLS + 2 * LANE_TILES + 1
THIN = CELLS + 1
EDGE = 3


def whole_tiles(rows):
    return 8 * ((rows + 7) // 8)


MESSAGE = whole_tiles(REST_AT + EDGE * REST + 8 - EDGE)
THIN_MESSAGE = whole_tiles(EDGE * THIN + 8 - EDGE)

OWN, TWO, SIDE, STRIP = 8, 48, 64, 112
SPAN = 48
PADS = (0, 40, 56, 104)
TILES = tuple((OWN + 8 * k, k) for k in range(4)) + ((TWO, 4),) + tuple((SIDE + 8 * n, (n + 2) % 5) for n in range(5))


def box_tile(by, u):
    return u + 2 * (1 - by)


def lanes_of(tile):
    return pl.ds(128 * tile, 128)


def height_of_lane():
    return lax.rem(lax.broadcasted_iota(jnp.int32, (8, 128), 1), 32)


def share(first, second):
    heights = height_of_lane()
    first_up, second_up = pltpu.roll(first, LEVELS, 1), pltpu.roll(second, LEVELS, 1)
    return jnp.where(heights < LEVELS, first, second_up), first_up, second_up


def unshare(common, first_rest, second_rest):
    heights = height_of_lane()
    first = jnp.where(heights < LEVELS, common, pltpu.roll(first_rest, 128 - LEVELS, 1))
    second = pltpu.roll(jnp.where(heights >= LEVELS, common, second_rest), 128 - LEVELS, 1)
    return first, second


def put_edges(out_ref, at, pieces, rightward):
    for n, tile in enumerate(pieces):
        tile = jnp.where(rightward == 1, pltpu.roll(tile, EDGE, 0), tile)
        out_ref[at + EDGE * n : at + EDGE * (n + 1)] = tile[:EDGE]


def cells(tile):
    low = height_of_lane() < 2
    pieces = []
    for by in range(2):
        common, rests = [], [None] * USED
        for u in range(HALF):
            both, rests[u], rests[u + HALF] = share(tile(by, 0, u), tile(by, 0, u + HALF))
            common.append(both)
        pieces += common + [jnp.where(low, rests[u], tile(by, 1, u)) for u in range(USED)]
    return pieces


def put_message(out_ref, rest_ref, rest_at, leftward, prev_tile, perm_tile, stor_tile, mask_tile):
    low = height_of_lane() < 2
    def put_tile(n, tile):
        out_ref[8 * n : 8 * n + 8] = tile

    for by in range(2):
        for u in range(USED):
            common, first_up, second_up = share(prev_tile(0, by, 0, u), prev_tile(1, by, 0, u))
            at = 24 * (by * USED + u)
            out_ref[at : at + 8] = common
            out_ref[at + 8 : at + 16] = jnp.where(low, first_up, prev_tile(0, by, 1, u))
            out_ref[at + 16 : at + 24] = jnp.where(low, second_up, prev_tile(1, by, 1, u))
    for n in range(2):
        put_tile(MASK_AT + n, mask_tile(n))
    for t in range(LANE_TILES):
        put_tile(PERM_AT + t, perm_tile(1 - leftward, t))
        put_tile(STOR_AT + t, stor_tile(1 - leftward, t))
    pieces = cells(functools.partial(prev_tile, 2))
    pieces += [perm_tile(leftward, t) for t in range(LANE_TILES)]
    pieces += [stor_tile(leftward, t) for t in range(LANE_TILES)]
    pieces += [mask_tile(2)]
    end = rest_at + MESSAGE - REST_AT
    rest_ref[end - 8 : end] = zeros()
    put_edges(rest_ref, rest_at, pieces, 1 - leftward)


def eight(tile):
    return pl.ds(pl.multiple_of(8 * tile, 8), 8)


def put_thin(out_ref, leftward, prev_tile, mask_tile):
    edge = 3 - 3 * leftward
    pieces = cells(functools.partial(prev_tile, edge)) + [mask_tile(edge)]
    out_ref[THIN_MESSAGE - 8 : THIN_MESSAGE] = zeros()
    put_edges(out_ref, 0, pieces, 1 - leftward)


def pack_kernel(
    perm_ref, stor_ref, mask_ref, prev_ref,
    far_ref, far2_ref, near2_ref, near_ref, rest_ref, perm, stor, mask_buf, prev, mask, sems,
):
    odd = lax.rem(lax.axis_index("gx"), 2)
    odd_chip = lax.rem(lax.axis_index("gx") // 2, 2)
    copies = []
    for by in range(2):
        lanes = pl.ds(128 * box_tile(by, 0), 128 * USED)
        copies.append((prev_ref.at[0, by, :, :, lanes], prev.at[pl.ds(2 * by, 2)]))
    copies += [(mask_ref.at[0], mask), (perm_ref, perm), (stor_ref, stor)]
    copies = [pltpu.make_async_copy(src, dst, sems.at[n]) for n, (src, dst) in enumerate(copies)]
    for copy in copies:
        copy.start()
    for copy in copies:
        copy.wait()
    mask_buf[...] = jnp.concatenate([mask[blk // 2, blk % 2] for blk in range(BLOCKS)], axis=1).astype(F32)

    def prev_tile(tile, by, bz, u):
        return prev[2 * by + bz, eight(tile), lanes_of(u)]

    def mask_tile(tile):
        return mask_buf[eight(tile), lanes_of(0)]

    def message(out_ref, rest_ref, rest_at, leftward):
        def tile_at(n):
            return jnp.where(leftward == 1, n, (2, 3, 1)[n])

        put_message(
            out_ref,
            rest_ref,
            rest_at,
            leftward,
            lambda n, by, bz, u: prev_tile(tile_at(n), by, bz, u),
            lambda n, t: perm[eight(n), lanes_of(t)],
            lambda n, t: stor[eight(n), lanes_of(t)],
            lambda n: mask_tile(tile_at(n)),
        )

    message(far_ref, far_ref, REST_AT, 1 - odd)
    put_thin(far2_ref, odd_chip, prev_tile, mask_tile)
    put_thin(near2_ref, 1 - odd_chip, prev_tile, mask_tile)
    message(near_ref, rest_ref, 0, odd)


def tile_rows(n):
    return slice(8 * n, 8 * n + 8)


def lane_index():
    return lax.broadcasted_iota(jnp.int32, (8, 128), 1)


def zeros():
    return jnp.zeros((8, 128), F32)


def up_y(here, after):
    return pltpu.roll(jnp.where(lane_index() >= 32, here, after), 96, 1)


def down_y(here, before):
    return pltpu.roll(jnp.where(lane_index() < 96, here, before), 32, 1)


def up_z(v):
    return pltpu.roll(v, 127, 1)


def down_z(v):
    return pltpu.roll(v, 1, 1)


def inverse(v):
    first = pl.reciprocal(v, approx=True)
    return first * (2.0 - v * first)


def harmonic(a, b):
    return 2.0 * (a * b) * inverse(jnp.maximum(a + b, TINY))


def edges(ref, at, index, left):
    start = at + EDGE * index - (8 - EDGE) * left
    tile = ref[max(start, 0) : max(start, 0) + 8]
    return pltpu.roll(tile, -start, 0) if start < 0 else tile


def fill_coefficients(rings, buf, own_ref, bulk, rest, sides):
    low = lax.broadcasted_iota(jnp.int32, (8, 128), 0) < 4
    for t in range(LANE_TILES):
        for i in rings:
            if i in (1, 2):
                tile = own_ref[tile_rows(i - 1), lanes_of(t)]
            elif i < 4:
                tile = sides[i // 3][0][tile_rows(bulk + t)]
            else:
                ends = [edges(*ref[1:], rest + t, n == 0) if ref is not None else None for n, ref in enumerate(sides)]
                tile = ends[0] if ends[1] is None else ends[1] if ends[0] is None else jnp.where(low, ends[1], ends[0])
            buf[t, tile_rows(i)] = tile


def fill_weights(rings, kbuf, cbuf, wbuf, gbuf):
    rows = lax.broadcasted_iota(jnp.int32, (8, 128), 0)
    heights = height_of_lane()

    def k_of(t, i):
        return kbuf[t, tile_rows(i % 5)] if 0 <= t < LANE_TILES else zeros()

    for t in range(LANE_TILES):
        for i in rings:
            k = k_of(t, i)
            east = jnp.where(rows < 7, pltpu.roll(k, 7, 0), pltpu.roll(k_of(t, i + 1), 7, 0))
            west = jnp.where(rows > 0, pltpu.roll(k, 1, 0), pltpu.roll(k_of(t, i + 4), 1, 0))
            faces = [
                harmonic(k, east),
                harmonic(k, west),
                harmonic(k, up_y(k, k_of(t + 1, i))),
                harmonic(k, down_y(k, k_of(t - 1, i))),
                jnp.where(heights < 31, harmonic(k, up_z(k)), 0.0),
                jnp.where(heights > 0, harmonic(k, down_z(k)), 0.0),
            ]
            diag = functools.reduce(lambda a, b: a + b, faces, cbuf[t, tile_rows(i)])
            scale = (2.0 / 3.0) * inverse(jnp.maximum(diag, TINY))
            for d, face in enumerate(faces):
                wbuf[t, d, tile_rows(i)] = face * scale
            gbuf[t, tile_rows(i)] = 1.5 * diag


def core_bits():
    lanes = lane_index()
    j = lax.rem(lanes, 32)
    return jnp.where((j >= 8) & (j < 24), jnp.where(lax.rem(lanes // 32, 2) == 0, 0xFFFF, 0xFFFF00), 0)


def support_of(bits, by, bz, u):
    offset = height_of_lane() - 8 * bz
    valid = (offset >= 0) & (offset < (18, 24)[bz])
    lane_bit = jnp.where(valid, jnp.left_shift(1, jnp.clip(offset, 0, 23)), 0)
    index = 32 * (2 * by + bz) + 4 * u + 8 * (1 - by) + lane_index() // 32
    spread = jnp.take_along_axis(bits, index, axis=1, mode="promise_in_bounds")
    return jnp.where((spread & lane_bit) != 0, 1.0, 0.0)


def message_cells(ref):
    found = [{}, {}]
    for by in range(2):
        for u in range(USED):
            at = 3 * (by * USED + u)
            common, first_top, second_top = [ref[tile_rows(at + n)] for n in range(3)]
            found[0][by, 0, u], found[1][by, 0, u] = unshare(common, first_top, second_top)
            found[0][by, 1, u], found[1][by, 1, u] = first_top, second_top
    return found


def edge_cells(fetch):
    found = {}
    for by in range(2):
        base = by * (HALF + USED)
        for u in range(HALF):
            tops = [fetch(base + HALF + u), fetch(base + HALF + u + HALF)]
            found[by, 0, u], found[by, 0, u + HALF] = unshare(fetch(base + u), *tops)
            found[by, 1, u], found[by, 1, u + HALF] = tops
    return found


def put_cells(pbuf, sup, row, found, bits):
    for (by, bz, u), tile in found.items():
        s = support_of(bits, by, bz, u)
        sup[by, bz, u, row : row + 8] = s
        pbuf[by, bz, u, row : row + 8] = s * tile


def side_row(ring):
    return SIDE + 8 * ((ring - 2) % 5)


def tile_of(pbuf, by, bz, u, row):
    return pbuf[by, bz, u, row : row + 8] if 0 <= u < USED else zeros()


def stencil(pbuf, by, bz, u, row, v, beside_y, w, beside_z=None):
    before, after = beside_y
    upper, lower = beside_z or (up_z(v), down_z(v))
    near = w[0] * pbuf[by, bz, u, row + 1 : row + 9] + w[1] * pbuf[by, bz, u, row - 1 : row + 7]
    near += w[2] * up_y(v, after) + w[3] * down_y(v, before)
    return near + (w[4] * upper + w[5] * lower)


def relax(pbuf, qbuf, sup, wbuf, by, tiles, zbuf=None, shift=None, spans=(), unfinished=()):
    if spans:
        count = sum(b - a for a, b in spans)
        v = jnp.concatenate([pbuf[by, :, :, a:b] for a, b in spans], axis=2).reshape(2 * USED * count, 128)
        high = v.astype(jnp.bfloat16)
        low = (v - high.astype(F32)).astype(jnp.bfloat16)
        parts = jnp.concatenate([high, low], axis=1)
        beside = jnp.dot(parts, shift[...], preferred_element_type=F32)
        zbuf[:, :, :count] = beside.reshape(2, USED, count, 256)
    places = {}
    for a, b in spans:
        for row in range(a, b, 8):
            places[row] = 8 * len(places)
    for i in sorted({ring for _, ring in tiles}):
        lines = [(bz, row) for bz in range(2) for row, ring in tiles if ring == i]
        before = [zeros()] * len(lines)
        here = [pbuf[by, bz, 0, row : row + 8] for bz, row in lines]
        for u in range(USED):
            w = [wbuf[u + 2 * by, d, tile_rows(i)] for d in range(6)]
            after = [tile_of(pbuf, by, bz, u + 1, row) for bz, row in lines]
            for n, (bz, row) in enumerate(lines):
                v = here[n]
                beside_z = None
                if spans:
                    at = slice(places[row], places[row] + 8)
                    beside_z = zbuf[bz, u, at, 0:128], zbuf[bz, u, at, 128:256]
                near = stencil(pbuf, by, bz, u, row, v, (before[n], after[n]), w, beside_z)
                kept = v * (1.0 / 3.0) + near
                if row not in unfinished:
                    kept = sup[by, bz, u, row : row + 8] * jnp.maximum(kept, 0.0)
                qbuf[by, bz, u, row : row + 8] = kept
            before, here = here, after


def complete(pbuf, qbuf, sup, wbuf, row, ring, eastward):
    edge = lax.broadcasted_iota(jnp.int32, (8, 128), 0) == (7 if eastward else 0)
    at = row + 1 if eastward else row - 1
    for by in range(2):
        for u in range(USED):
            w = jnp.where(edge, wbuf[u + 2 * by, 0 if eastward else 1, tile_rows(ring)], 0.0)
            for bz in range(2):
                kept = qbuf[by, bz, u, row : row + 8] + w * jnp.where(edge, pbuf[by, bz, u, at : at + 8], 0.0)
                qbuf[by, bz, u, row : row + 8] = sup[by, bz, u, row : row + 8] * jnp.maximum(kept, 0.0)


def normalise(qbuf, pbuf, tiles, basis_ref=None):
    for t in range(LANE_TILES):
        blocks = [(by, bz, t - 2 * by) for by in range(2) for bz in range(2) if 0 <= t - 2 * by < USED]
        for i in sorted({ring for _, ring in tiles}):
            at = [(b, row) for b in blocks for row, ring in tiles if ring == i]
            kept = [qbuf[by, bz, u, row : row + 8] for (by, bz, u), row in at]
            total = functools.reduce(lambda a, b: a + b, kept)
            scale = inverse(jnp.maximum(total, SUM_FLOOR))
            for ((by, bz, u), row), v in zip(at, kept):
                v = v * scale
                pbuf[by, bz, u, row : row + 8] = v
                if basis_ref is not None and row < TWO:
                    basis_ref[0, by, bz, row - OWN : row - OWN + 8, lanes_of(box_tile(by, u))] = v


def halves(odd):
    return ((1, 0), (2, 3)) if odd else ((2, 3), (1, 0))


def by_parity(body):
    parity = lax.rem(lax.axis_index("gx"), 2)
    for odd in range(2):
        pl.when(parity == odd)(functools.partial(body, odd))


def begin_kernel(perm_ref, stor_ref, mask_ref, prev_ref, near_ref, rest_ref, first, second, sup, wbuf, gbuf, qbuf, shift, kbuf, cbuf):
    here = lax.axis_index("gx")
    last = lax.axis_size("gx") - 1
    deep = lax.broadcasted_iota(jnp.int32, (256, 256), 0) % 128
    wide = lax.broadcasted_iota(jnp.int32, (256, 256), 1)
    source = jnp.where(wide < 128, wide + 1, wide - 129)
    shift[...] = jnp.where(deep == source, 1.0, 0.0).astype(jnp.bfloat16)

    own_bits = [mask_ref[tile_rows(k)].astype(jnp.int32) for k in range(4)]
    own_bits[0] = jnp.where(here == 0, 0, own_bits[0])
    own_bits[1] |= core_bits()
    own_bits[2] |= core_bits()
    own_bits[3] = jnp.where(here == last, 0, own_bits[3])
    for by in range(2):
        for bz in range(2):
            for u in range(USED):
                for row in PADS:
                    first[by, bz, u, row : row + 8] = zeros()
                    second[by, bz, u, row : row + 8] = zeros()
    for k in range(4):
        found = {
            (by, bz, u): prev_ref[2 * by + bz, tile_rows(k), lanes_of(u)]
            for by in range(2)
            for bz in range(2)
            for u in range(USED)
        }
        put_cells(first, sup, OWN + 8 * k, found, own_bits[k])

    def body(odd):
        (inner, outer), (far_inner, _) = halves(odd)
        near = (near_ref, rest_ref, 0)
        sides = (near, None) if odd else (None, near)
        fill_coefficients((1, 2, outer, 4), kbuf, perm_ref, PERM_AT, CELLS, sides)
        fill_coefficients((inner, outer), cbuf, stor_ref, STOR_AT, CELLS + LANE_TILES, sides)
        fill_weights((inner, outer), kbuf, cbuf, wbuf, gbuf)
        found = message_cells(near_ref)
        for n in range(2):
            ring = n if odd else n + 2
            bits = near_ref[tile_rows(MASK_AT + n)].astype(jnp.int32)
            put_cells(first, sup, side_row(ring), found[n], bits | core_bits() if ring in (0, 3) else bits)

        def rest(index):
            return edges(rest_ref, 0, index, odd == 1)

        put_cells(first, sup, side_row(4), edge_cells(rest), rest(REST - 1).astype(jnp.int32) | core_bits())
        tiles = [(row, i) for row, i in TILES if i in (inner, outer)]
        for by in range(2):
            relax(first, qbuf, sup, wbuf, by, tiles)
        normalise(qbuf, second, tiles)
        for by in range(2):
            for bz in range(2):
                for u in range(USED):
                    for row in (OWN + 8 * far_inner, side_row(4)):
                        second[by, bz, u, row : row + 8] = zeros()
        for by in range(2):
            relax(second, qbuf, sup, wbuf, by, tiles, unfinished=(OWN + 8 * inner, side_row(outer)))

    by_parity(body)


def finish_kernel(
    far_ref, far2_ref, near2_ref, near_ref, rest_ref, perm_ref, stor_ref, shift, _first, _second, _sup, _wbuf, _gbuf, _qbuf,
    basis_ref, coarse_ref, first, second, sup, wbuf, gbuf, qbuf,
    kbuf, cbuf, sums, zbuf,
):
    here = lax.axis_index("gx")
    odd_chip = lax.rem(here // 2, 2) == 1
    rows = lax.broadcasted_iota(jnp.int32, (8, 128), 0)
    low_rows = rows < 4

    def thin(index):
        right = jnp.where(odd_chip, edges(near2_ref, 0, index, False), edges(far2_ref, 0, index, False))
        left = jnp.where(odd_chip, edges(far2_ref, 0, index, True), edges(near2_ref, 0, index, True))
        return jnp.where(low_rows, right, left)

    def body(odd):
        (near_inner, near_outer), (inner, outer) = halves(odd)
        near, far = (near_ref, rest_ref, 0), (far_ref, far_ref, REST_AT)
        sides = (near, far) if odd else (far, near)
        fill_coefficients((1, 2, near_outer, outer, 4), kbuf, perm_ref, PERM_AT, CELLS, sides)
        fill_coefficients((inner, outer, 4), cbuf, stor_ref, STOR_AT, CELLS + LANE_TILES, sides)
        fill_weights((inner, outer, 4), kbuf, cbuf, wbuf, gbuf)
        found = message_cells(far_ref)
        for n in range(2):
            ring = n + 2 if odd else n
            bits = far_ref[tile_rows(MASK_AT + n)].astype(jnp.int32)
            put_cells(first, sup, side_row(ring), found[n], bits | core_bits() if ring in (0, 3) else bits)

        def rest(index):
            return jnp.where(low_rows, edges(*sides[1][1:], index, False), edges(*sides[0][1:], index, True))

        put_cells(first, sup, side_row(4), edge_cells(rest), rest(REST - 1).astype(jnp.int32) | core_bits())
        put_cells(first, sup, TWO, edge_cells(thin), thin(THIN - 1).astype(jnp.int32))
        tiles = [(row, i) for row, i in TILES if i in (inner, outer, 4)]
        own = OWN + 16 * odd
        side = SIDE + 16 * (1 - odd)
        spans = ((own, own + 16), (TWO, TWO + 8), (side, side + 24))
        for by in range(2):
            relax(first, qbuf, sup, wbuf, by, tiles, zbuf, shift, spans)
        normalise(qbuf, second, tiles)
        for by in range(2):
            relax(second, qbuf, sup, wbuf, by, tiles, zbuf, shift, spans)
        complete(second, qbuf, sup, wbuf, OWN + 8 * near_inner, near_inner, odd == 1)
        complete(second, qbuf, sup, wbuf, side_row(near_outer), near_outer, odd == 0)

    by_parity(body)

    pbuf = first
    normalise(qbuf, pbuf, TILES, basis_ref)
    for by in range(2):
        for bz in range(2):
            at = 0 if by == 0 else 768
            basis_ref[0, by, bz, :, at : at + 256] = jnp.zeros((32, 256), F32)

    for by in range(2):
        acc = [[] for _ in range(24)]
        for t in range(by, by + USED + 1):
            u = t - 2 * by
            weights = [[wbuf[t, d, tile_rows(i)] for d in range(6)] for i in range(5)]
            scale = [gbuf[t, 8 * i : 8 * i + 8] for i in range(5)]
            images = [[], []]
            for k in range(4):
                row = OWN + 8 * k
                for bz in range(2):
                    beside_y = tile_of(pbuf, by, bz, u - 1, row), tile_of(pbuf, by, bz, u + 1, row)
                    if 0 <= u < USED:
                        v = tile_of(pbuf, by, bz, u, row)
                        near = stencil(pbuf, by, bz, u, row, v, beside_y, weights[k])
                        images[bz].append(scale[k] * (v * (2.0 / 3.0) - near))
                    elif u < 0:
                        images[bz].append(-scale[k] * (weights[k][2] * up_y(zeros(), beside_y[1])))
                    else:
                        images[bz].append(-scale[k] * (weights[k][3] * down_y(zeros(), beside_y[0])))
            ends = [None, None]
            if 0 <= u < USED:
                for bz in range(2):
                    beyond = -scale[4] * (weights[4][1] * pbuf[by, bz, u, OWN + 31 : OWN + 39])
                    before = -scale[4] * (weights[4][0] * pbuf[by, bz, u, OWN - 7 : OWN + 1])
                    ends[bz] = before, beyond
            for partner in range(BLOCKS):
                by2, bz2 = divmod(partner, 2)
                u2 = t - 2 * by2
                if not 0 <= u2 < USED:
                    continue
                own = [tile_of(pbuf, by2, bz2, u2, OWN + 8 * k) for k in range(4)]
                side = [tile_of(pbuf, by2, bz2, u2, SIDE + 8 * k) for k in range(5)]
                for bz in range(2):
                    image = images[bz]
                    at = bz * 12 + partner
                    acc[at] += [image[0] * side[3], image[1] * side[4]]
                    acc[at + 4] += [image[k] * own[k] for k in range(4)]
                    acc[at + 8] += [image[2] * side[0], image[3] * side[1]]
                    if ends[bz] is not None:
                        acc[at] += [ends[bz][0] * side[2]]
                        acc[at + 8] += [ends[bz][1] * side[2]]
            acc = [[functools.reduce(lambda a, b: a + b, terms)] if terms else [] for terms in acc]
        for bz in range(2):
            for n in range(12):
                sums[2 * by + bz, n] = jnp.sum(acc[bz * 12 + n][0], axis=0)

    entry = lax.broadcasted_iota(jnp.int32, (16, 128), 0)
    column = lax.broadcasted_iota(jnp.int32, (16, 128), 1)
    for by in range(2):
        for bz in range(2):
            values = jnp.sum(sums[2 * by + bz], axis=1, keepdims=True)
            target = 9 * (entry // 4) + 3 * (lax.rem(entry // 2, 2) - by + 1) + (lax.rem(entry, 2) - bz + 1)
            placed = jnp.where((column == target) & (entry < 12), values, 0.0)
            coarse_ref[0, by, bz, :] = jnp.sum(placed, axis=0)[:27]


def shards(permeability, storage, support_mask, prev_basis):
    vmem = pl.BlockSpec(memory_space=pltpu.VMEM)
    far, far2, near2, near, rest, *own = pl.pallas_call(
        pack_kernel,
        in_specs=[pl.BlockSpec(memory_space=pl.ANY)] * 4,
        out_specs=[vmem] * 9,
        out_shape=[
            *[pltpu.VMEM((n, 128), F32) for n in (MESSAGE, THIN_MESSAGE, THIN_MESSAGE, REST_AT, MESSAGE - REST_AT)],
            pltpu.VMEM(permeability.shape, F32),
            pltpu.VMEM(storage.shape, F32),
            pltpu.VMEM((32, 128), F32),
            pltpu.VMEM((BLOCKS, 32, 128 * USED), F32),
        ],
        scratch_shapes=[
            pltpu.VMEM((2, 2, 32, 32), jnp.int32),
            pltpu.SemaphoreType.DMA((5,)),
        ],
        name="pack",
    )(permeability, storage, support_mask, prev_basis)
    size = lax.axis_size("gx")

    def move(x, step, width):
        pairs = [(i, i + (-step if i // width % 2 else step)) for i in range(size)]
        return lax.ppermute(x, "gx", [(i, j) for i, j in pairs if 0 <= j < size])

    far = move(far, -1, 1)
    far2 = move(far2, 2, 2)
    near2 = move(near2, -2, 2)
    near = move(near, 1, 1)
    rest = move(rest, 1, 1)

    strips = (2, 2, USED, STRIP, 128)
    state = [
        pltpu.VMEM(strips, F32),
        pltpu.VMEM(strips, F32),
        pltpu.VMEM(strips, F32),
        pltpu.VMEM((LANE_TILES, 6, 40, 128), F32),
        pltpu.VMEM((LANE_TILES, 40, 128), F32),
        pltpu.VMEM(strips, F32),
    ]
    scratch = [pltpu.VMEM((LANE_TILES, 40, 128), F32)] * 2
    limit = pltpu.CompilerParams(vmem_limit_bytes=32 * 1024 * 1024)
    *filled, shift = pl.pallas_call(
        begin_kernel,
        in_specs=[vmem] * 6,
        out_specs=[vmem] * 7,
        out_shape=[*state, pltpu.VMEM((256, 256), jnp.bfloat16)],
        scratch_shapes=scratch,
        compiler_params=limit,
        cost_estimate=pl.CostEstimate(flops=0, bytes_accessed=0, transcendentals=0),
        name="begin",
    )(*own, near, rest)
    return pl.pallas_call(
        finish_kernel,
        in_specs=[vmem] * 14,
        out_specs=[vmem] * 8,
        out_shape=[
            jax.ShapeDtypeStruct(prev_basis.shape, F32),
            jax.ShapeDtypeStruct((*prev_basis.shape[:3], 27), F32),
            *state,
        ],
        input_output_aliases={8 + n: 2 + n for n in range(6)},
        scratch_shapes=[
            *scratch,
            pltpu.VMEM((4, 16, 128), F32),
            pltpu.VMEM((2, USED, SPAN, 256), F32),
        ],
        compiler_params=limit,
        name="finish",
    )(far, far2, near2, near, rest, *own[:2], shift, *filled)[:2]


def solution(mesh):
    placed = (
        P(("groups", "gx"), None),
        P(("groups", "gx"), None),
        P(("groups", "gx"), None, None, None, None),
        P(("groups", "gx"), None, None, None, None),
    )
    return jax.shard_map(
        shards,
        mesh=mesh,
        in_specs=placed,
        out_specs=(
            P(("groups", "gx"), None, None, None, None),
            P(("groups", "gx"), None, None, None),
        ),
        check_vma=False,
    )
```
